256 devices in a mesh: depth: 2 (over core), row: 8 (over z), col: 16 (over y, x).
Axes of the slice: x: 4, y: 4, z: 8, core: 2. Of those that a mesh axis runs over, the one named last changes fastest.
Arguments:
- rhs: float32 [2, 4096, 256], P('depth', ('row', 'col')), may hold values from -8 to 8
- factor_blocks: float32 [2, 8, 16, 512, 4096], P('depth', 'row', 'col'), may hold values from -0.1875 to 0.1875
- block_rows: int32 [2, 8, 16, 512], P('depth', 'row', 'col'), may hold values from 0 to 511
- block_cols: int32 [2, 8, 16, 512], P('depth', 'row', 'col'), may hold values from 0 to 255
- diag_inverse: float32 [2, 4096, 4096], P('depth', ('row', 'col')), may hold values from -0.225 to 1.225
- coupling: float32 [2, 128, 4096], P('depth', ('row', 'col')), may hold values from -2 to 2
Outputs:
- solution: float32 [2, 4096, 256], P('depth', ('row', 'col'))
The draws below stay inside these ranges and needn't reach their ends.
All inputs are finite; a program needn't handle non-finite values.
Results may differ from the reference program's by a relative error of at most 0.00015.
Values sent between devices are 32-bit elements; how exact they have to be, the bound alone decides.
A program may use at most 128 MiB of HBM per device.

```python
import math
import jax
import jax.numpy as jnp
from jax import lax

BLOCK = 64
RHS = 4
NBF = 32
NZ = 512
PANELS = 2
FACES = 128
NB = 4096
N_ROW = 8
N_COL = 16


def draw_diag_inverse(key, part):
    key = jax.random.fold_in(key, 7)
    spread = 0.6 / math.sqrt(BLOCK)
    ident = jnp.eye(BLOCK, dtype=jnp.float32).reshape(BLOCK * BLOCK)
    offdiag = spread * jnp.clip(jax.random.normal(key, (PANELS, NB, BLOCK * BLOCK), jnp.float32), -3.0, 3.0)
    return ident + offdiag


def touch_ends(entries, stream_key, low, largest):
    longest = entries.shape.index(max(entries.shape))
    spots = []
    for shift in (0, 1):
        where = [jax.random.randint(jax.random.fold_in(stream_key, axis), (), 0, length) for axis, length in enumerate(entries.shape)]
        where[longest] = (where[longest] + shift) % entries.shape[longest]
        spots.append(tuple(where))
    return entries.at[spots[0]].set(low).at[spots[1]].set(largest)


def shard_levels(stream_key, shape, split, low, high):
    def one(position, shards_of):
        steps = jax.random.uniform(jax.random.fold_in(jax.random.fold_in(stream_key, 6), position), (shards_of,), jnp.float32, low / len(split), high / len(split))
        return jnp.repeat(jnp.exp(steps), shape[position] // shards_of).reshape((-1,) + (1,) * (len(shape) - position - 1))

    factor_of = one(*split[0])
    for cut in split[1:]:
        factor_of = factor_of * one(*cut)
    return factor_of


def noise(stream_key, extent, scale, limit, shards=(), held_as=jnp.bfloat16):
    values = jax.random.normal(stream_key, extent, jnp.float32) * scale
    if len(shards) > 0:
        values = shard_levels(stream_key, extent, shards, -0.22, 0.18) * values
    return jnp.clip(values, min=-limit, max=limit).astype(held_as)


def setup_inputs(seed: int = 0) -> dict:
    streams_of = jax.random.split(jax.random.key(seed), 7)
    return {
        "rhs": noise(streams_of[0], (PANELS, NB, RHS * BLOCK), 1.0, 8.0, ((0, 2), (1, 128)), jnp.float32),
        "factor_blocks": noise(streams_of[1], (PANELS, N_ROW, N_COL, NZ, BLOCK * BLOCK), (0.25 / BLOCK ** 0.5), 0.1875, ((0, 2), (1, 8), (2, 16)), jnp.float32),
        "block_rows": touch_ends(jax.random.randint(streams_of[2], (PANELS, N_ROW, N_COL, NZ), 0, N_COL * NBF), jax.random.fold_in(streams_of[2], 1), 0, (N_COL * NBF) - 1).astype(jnp.int32),
        "block_cols": touch_ends(jax.random.randint(streams_of[3], (PANELS, N_ROW, N_COL, NZ), 0, N_ROW * NBF), jax.random.fold_in(streams_of[3], 1), 0, (N_ROW * NBF) - 1).astype(jnp.int32),
        "diag_inverse": draw_diag_inverse(jax.random.fold_in(streams_of[6], 71), 0),
        "coupling": noise(streams_of[5], (PANELS, FACES, BLOCK * BLOCK), (1.0 / BLOCK ** 0.5), 2.0, ((0, 2), (1, 128)), jnp.float32),
    }


def mix(mats, vecs):
    count = vecs.shape[0]
    shaped = vecs.reshape(count, RHS, BLOCK)
    out = jnp.einsum("kab,krb->kra", mats, shaped, precision=lax.Precision.HIGHEST)
    return out.reshape(count, RHS * BLOCK)


def mix_back(mats, vecs):
    count = vecs.shape[0]
    shaped = vecs.reshape(count, RHS, BLOCK)
    out = jnp.einsum("kab,kra->krb", mats, shaped, precision=lax.Precision.HIGHEST)
    return out.reshape(count, RHS * BLOCK)


def reference(rhs, factor_blocks, block_rows, block_cols, diag_inverse, coupling):
    row_pos = jnp.arange(N_ROW, dtype=jnp.int32).reshape(1, N_ROW, 1, 1)
    col_pos = jnp.arange(N_COL, dtype=jnp.int32).reshape(1, 1, N_COL, 1)
    global_rows = (row_pos * N_COL + block_rows // NBF) * NBF + block_rows % NBF
    global_cols = ((block_cols // NBF) * N_COL + col_pos) * NBF + block_cols % NBF

    def solve(panel, field):
        mats = factor_blocks[panel].reshape(-1, BLOCK, BLOCK)
        targets = global_rows[panel].reshape(-1)
        sources = global_cols[panel].reshape(-1)
        summed = field + jax.ops.segment_sum(mix(mats, field[sources]), targets, num_segments=NB)
        scaled = mix(diag_inverse[panel].reshape(NB, BLOCK, BLOCK), summed)
        return scaled + jax.ops.segment_sum(mix_back(mats, scaled[targets]), sources, num_segments=NB)

    front = jnp.arange(FACES, dtype=jnp.int32) * NBF
    backs = front + NBF - 1
    fields = []
    previous = None
    for panel in range(PANELS):
        field = rhs[panel]
        if panel > 0:
            couple = coupling[panel].reshape(FACES, BLOCK, BLOCK)
            pushed = mix(couple, previous[backs])
            field = field.at[front].add(-pushed)
        fields.append(field)
        if panel < PANELS - 1:
            previous = solve(panel, field)
    outs = [None] * PANELS
    current = solve(PANELS - 1, fields[PANELS - 1])
    outs[PANELS - 1] = current
    for panel in range(PANELS - 2, -1, -1):
        couple = coupling[panel + 1].reshape(FACES, BLOCK, BLOCK)
        pulled = mix_back(couple, current[front])
        current = solve(panel, fields[panel].at[backs].add(-pulled))
        outs[panel] = current
    return jnp.stack(outs)
```

```python
import functools

import jax
import jax.numpy as jnp
from jax import lax
from jax.experimental import pallas as pl
from jax.experimental.pallas import tpu as pltpu
from jax.sharding import PartitionSpec as P

MESH = pl.DeviceIdType.MESH
F32 = jnp.float32
BF16 = jnp.bfloat16

BLOCK = 64
LANES = 128
STREAMS = 2
CHUNKS = 8


def halves(x):
    hi = x.astype(BF16)
    return hi, (x - hi.astype(F32)).astype(BF16)


def picked(x, table):
    hi, lo = halves(x)
    return jnp.dot(hi, table, preferred_element_type=F32) + jnp.dot(lo, table, preferred_element_type=F32)


def placed(table, x):
    hi, lo = halves(x)
    dims = (((1,), (1,)), ((), ()))
    return lax.dot_general(table, hi, dims, preferred_element_type=F32) + lax.dot_general(
        table, lo, dims, preferred_element_type=F32
    )


def column_sums(parts):
    at = lax.broadcasted_iota(jnp.int32, parts[0].shape, 0)
    low = at < 4
    four = [
        jnp.where(low, parts[s], parts[s + 4]) + pltpu.roll(jnp.where(low, parts[s + 4], parts[s]), 4, 0)
        for s in range(4)
    ]
    low = (at & 2) == 0
    two = [
        jnp.where(low, four[s], pltpu.roll(four[s + 2], 2, 0)) + jnp.where(low, pltpu.roll(four[s], 6, 0), four[s + 2])
        for s in range(2)
    ]
    low = (at & 1) == 0
    return jnp.where(low, two[0], pltpu.roll(two[1], 1, 0)) + jnp.where(low, pltpu.roll(two[0], 7, 0), two[1])


def total(terms):
    while len(terms) > 1:
        terms = [terms[i] + terms[i + 1] if i + 1 < len(terms) else terms[i] for i in range(0, len(terms), 2)]
    return terms[0]


def act(mats, vecs, outs, count, width):
    def tile(t, _):
        lanes = pl.ds(pl.multiple_of(t * LANES, LANES), LANES)
        x = [[vecs[pl.ds(r * BLOCK + 8 * g, 8), lanes] for g in range(8)] for r in range(count)]

        def group(q, _):
            parts = [[] for _ in range(count)]
            for a in range(8):
                first = pl.multiple_of(q * (8 * BLOCK) + a * BLOCK, BLOCK)
                m = [mats[pl.ds(first + 8 * g, 8), lanes] for g in range(8)]
                for r in range(count):
                    parts[r].append(total([m[g] * x[r][g] for g in range(8)]))
            for r in range(count):
                outs[pl.ds(pl.multiple_of(r * BLOCK + 8 * q, 8), 8), lanes] = column_sums(parts[r])
            return 0

        return lax.fori_loop(0, 8, group, 0)

    lax.fori_loop(0, width // LANES, tile, 0)


def act_back(mats, vecs, outs, count, width):
    def tile(t, _):
        lanes = pl.ds(pl.multiple_of(t * LANES, LANES), LANES)

        def group(q, sums):
            sums = list(sums)
            v = [vecs[pl.ds(pl.multiple_of(r * BLOCK + 8 * q, 8), 8), lanes] for r in range(count)]
            for a in range(8):
                first = pl.multiple_of(q * (8 * BLOCK) + a * BLOCK, BLOCK)
                z = [jnp.broadcast_to(v[r][a : a + 1], (8, LANES)) for r in range(count)]
                for g in range(8):
                    m = mats[pl.ds(first + 8 * g, 8), lanes]
                    for r in range(count):
                        sums[r * 8 + g] = sums[r * 8 + g] + m * z[r]
            return tuple(sums)

        zero = jnp.zeros((8, LANES), F32)
        sums = lax.fori_loop(0, 8, group, (zero,) * (8 * count))
        for r in range(count):
            for g in range(8):
                outs[pl.ds(r * BLOCK + 8 * g, 8), lanes] = sums[r * 8 + g]
        return 0

    lax.fori_loop(0, width // LANES, tile, 0)


def stood_up(v):
    n = v.shape[0]
    both = jnp.concatenate([v, pltpu.roll(v, BLOCK, 1), jnp.zeros((LANES - 2 * n, LANES), F32)], axis=0)
    return both.T[:BLOCK]


def laid_down(v, n):
    flat = jnp.concatenate([v, v], axis=0).T
    lane = lax.broadcasted_iota(jnp.int32, (n, LANES), 1)
    return jnp.where(lane < BLOCK, flat[:n], flat[n : 2 * n])


def kernel(
    nrow, ncol, rhs, mats, rows, cols, diag, couple, out,
    raw, mt, ohc, ohr, ohf, dt, ct, fields, xt, work, done, small, small_out, term, rs, ag, face, fx, wide, fin, cbuf,
    raw_sem, row_send, row_recv, rs_send, rs_recv, ag_send, ag_recv, fx_send, fx_recv, fin_send, fin_recv, c_send, c_recv,
):
    nbf = rhs.shape[0]
    nz = rows.shape[1]
    d, r, c = lax.axis_index("depth"), lax.axis_index("row"), lax.axis_index("col")

    def at_row(i):
        return lax.rem(r + i, nrow)

    def at_col(i):
        return lax.rem(c + i, ncol)

    def send(src, dst, send_sem, recv_sem, where):
        pltpu.make_async_remote_copy(
            src_ref=src, dst_ref=dst, send_sem=send_sem, recv_sem=recv_sem, device_id=where, device_id_type=MESH
        ).start()

    def await_bytes(ref, sem):
        pltpu.make_async_copy(ref, ref, sem).wait()

    def each(low, high, body):
        def step(i, _):
            body(i)
            return 0

        lax.fori_loop(low, high, step, 0)

    barrier = pltpu.get_barrier_semaphore()

    def greet(where):
        pl.semaphore_signal(barrier, inc=1, device_id=where, device_id_type=MESH)

    each(1, ncol, lambda i: greet((d, r, at_col(i))))
    each(1, nrow, lambda i: greet((d, at_row(i), c)))
    each(0, nrow, lambda i: greet((1 - d, at_row(i), c)))

    width = mats.shape[1] // CHUNKS
    pieces = [
        pltpu.make_async_copy(mats.at[:, pl.ds(i * width, width)], raw.at[:, pl.ds(i * width, width)], raw_sem.at[i])
        for i in range(CHUNKS)
    ]
    for piece in pieces:
        piece.start()

    pl.semaphore_wait(barrier, (ncol - 1) + (2 * nrow - 1))

    for s in range(STREAMS):
        part = pl.ds(s * LANES, LANES)
        fields[s, 0] = rhs[:, part]
        each(
            1, nrow,
            lambda i: send(rhs.at[:, part], fields.at[s, i], row_send.at[s], row_recv.at[s], (d, at_row(i), c)),
        )

    @pl.when(d == 1)
    def _():
        cbuf[pl.ds(r, 1)] = couple[...][None]
        each(1, nrow, lambda i: send(couple, cbuf.at[r], c_send, c_recv, (1, at_row(i), c)))
        each(0, nrow, lambda i: send(couple, cbuf.at[r], c_send, c_recv, (0, at_row(i), c)))

    brow, bcol = rows[...], cols[...]
    turned_row = (((c - (brow >> 5)) & (ncol - 1)) << 5) | (brow & 31)
    turned_col = (((r - (bcol >> 5)) & (nrow - 1)) << 5) | (bcol & 31)

    def table(position, count):
        return (lax.broadcasted_iota(jnp.int32, (count, nz), 0) == position).astype(BF16)

    ohr[...] = table(turned_row, ncol * nbf)
    ohc[...] = table(turned_col, nrow * nbf)
    at_face = (bcol & 31) == jnp.where(d == 0, nbf - 1, 0)
    ohf[...] = table(jnp.where(at_face, bcol >> 5, -1), LANES)

    def turn_diag(j):
        lanes = pl.ds(pl.multiple_of(j * LANES, LANES), LANES)
        two = diag[:, lanes]
        dt[lanes, :] = jnp.concatenate([two, two, jnp.zeros((LANES - 2 * nbf, LANES), F32)], axis=0).T

    each(0, diag.shape[1] // LANES, turn_diag)

    for i, piece in enumerate(pieces):
        piece.wait()

        def turn(j):
            lanes = pl.ds(pl.multiple_of(i * width + j * LANES, LANES), LANES)
            for t in range(nz // LANES):
                ks = pl.ds(t * LANES, LANES)
                mt[lanes, ks] = raw[ks, lanes].T

        each(0, width // LANES, turn)

    for s in range(STREAMS):
        await_bytes(fields.at[s, pl.ds(0, nrow - 1)], row_recv.at[s])
        xt[s] = picked(fields[s].reshape(nrow * nbf, LANES).T, ohc[...])

    def turn_couple():
        def one(j):
            two = cbuf[:, pl.ds(j, 1), :].reshape(nrow, LANES)
            full = jnp.concatenate([two, two, jnp.zeros((LANES - 2 * nrow, LANES), F32)], axis=0)
            ct[pl.ds(pl.multiple_of(j * LANES, LANES), LANES), :] = full.T

        each(0, ct.shape[0] // LANES, one)

    def forward(use, s, vecs):
        act(mt, vecs, done, 2, nz)
        term[use, s] = placed(ohr[...], done[...]).reshape(ncol, nbf, LANES)
        each(
            1, ncol,
            lambda i: send(
                term.at[use, s, i], rs.at[use, s, i - 1], rs_send.at[use, s], rs_recv.at[use, s],
                (d, r, at_col(ncol - i)),
            ),
        )

    def middle(use, s, field):
        await_bytes(rs.at[use, s], rs_recv.at[use, s])
        small[...] = stood_up(field + term[use, s, 0] + total([rs[use, s, i] for i in range(ncol - 1)]))
        act(dt, small, small_out, 1, LANES)
        ag[use, s, 0] = laid_down(small_out[...], nbf)
        each(
            1, ncol,
            lambda i: send(
                ag.at[use, s, 0], ag.at[use, s, i], ag_send.at[use, s], ag_recv.at[use, s], (d, r, at_col(i))
            ),
        )

    def backward(use, s):
        await_bytes(ag.at[use, s, pl.ds(0, ncol - 1)], ag_recv.at[use, s])
        work[...] = picked(ag[use, s].reshape(ncol * nbf, LANES).T, ohr[...])
        act_back(mt, work, done, 2, nz)

    def face_out(use, s, own):
        here = lax.broadcasted_iota(jnp.int32, (nrow, LANES), 0) == r
        face[s] = placed(ohf[...], done[...])[:nrow] + jnp.where(here, ag[use, s, 0, own : own + 1], 0.0)
        each(
            0, nrow,
            lambda i: send(face.at[s], fx.at[s, i], fx_send.at[s], fx_recv.at[s], (1 - d, at_row(i), c)),
        )

    def face_in(s, own, action):
        await_bytes(fx.at[s], fx_recv.at[s])
        small[...] = stood_up(total([fx[s, i] for i in range(nrow)]))
        action(ct, small, small_out, 1, LANES)
        moved = small_out[...]
        taken = jnp.concatenate([moved, pltpu.roll(moved, LANES - nrow, 1)], axis=0)
        work[...] = xt[s] - picked(taken, ohf[...])
        here = lax.broadcasted_iota(jnp.int32, (nrow, LANES), 0) == r
        mine = jnp.sum(jnp.where(here, laid_down(moved, nrow), 0.0), axis=0, keepdims=True)
        at_own = lax.broadcasted_iota(jnp.int32, (nbf, LANES), 0) == own
        return fields[s, 0] - jnp.where(at_own, mine, 0.0)

    def widen(s):
        wide[s] = placed(ohc[...], done[...]).reshape(nrow, nbf, LANES)
        each(
            1, nrow,
            lambda i: send(
                wide.at[s, i], fin.at[s, i - 1], fin_send.at[s], fin_recv.at[s], (d, at_row(nrow - i), c)
            ),
        )

    def finish(use, s):
        await_bytes(fin.at[s], fin_recv.at[s])
        out[:, pl.ds(s * LANES, LANES)] = ag[use, s, 0] + wide[s, 0] + total([fin[s, i] for i in range(nrow - 1)])

    every = range(STREAMS)

    @pl.when(d == 0)
    def _():
        for s in every:
            forward(0, s, xt.at[s])
        for s in every:
            middle(0, s, fields[s, 0])
        for s in every:
            backward(0, s)
            face_out(0, s, nbf - 1)
        await_bytes(cbuf, c_recv)
        turn_couple()
        held = []
        for s in every:
            held.append(face_in(s, nbf - 1, act_back))
            forward(1, s, work)
        for s in every:
            middle(1, s, held[s])
        for s in every:
            backward(1, s)
            widen(s)
        for s in every:
            finish(1, s)
        for s in every:
            await_bytes(term.at[1, s, pl.ds(0, ncol - 1)], rs_send.at[1, s])
            await_bytes(ag.at[1, s, pl.ds(0, ncol - 1)], ag_send.at[1, s])

    @pl.when(d == 1)
    def _():
        await_bytes(cbuf.at[pl.ds(0, nrow - 1)], c_recv)
        turn_couple()
        held = []
        for s in every:
            held.append(face_in(s, 0, act))
            forward(0, s, work)
        for s in every:
            middle(0, s, held[s])
        for s in every:
            backward(0, s)
            face_out(0, s, 0)
            widen(s)
        for s in every:
            finish(0, s)
        await_bytes(cbuf.at[pl.ds(0, nrow - 1)], c_send)
        await_bytes(cbuf, c_send)

    for s in every:
        await_bytes(fields.at[s, pl.ds(0, nrow - 1)], row_send.at[s])
        await_bytes(term.at[0, s, pl.ds(0, ncol - 1)], rs_send.at[0, s])
        await_bytes(ag.at[0, s, pl.ds(0, ncol - 1)], ag_send.at[0, s])
        await_bytes(fx.at[s], fx_send.at[s])
        await_bytes(wide.at[s, pl.ds(0, nrow - 1)], fin_send.at[s])


def per_device(nrow, ncol, rhs, factor_blocks, block_rows, block_cols, diag_inverse, coupling):
    nbf = rhs.shape[1]
    nz, size = factor_blocks.shape[-2:]
    vm = pl.BlockSpec(memory_space=pltpu.VMEM)
    dma = pltpu.SemaphoreType.DMA
    got = pl.pallas_call(
        functools.partial(kernel, nrow, ncol),
        out_shape=jax.ShapeDtypeStruct((nbf, rhs.shape[2]), F32),
        in_specs=[vm, pl.BlockSpec(memory_space=pl.ANY), vm, vm, vm, vm],
        out_specs=vm,
        scratch_shapes=[
            pltpu.VMEM((nz, size), F32),
            pltpu.VMEM((size, nz), F32),
            pltpu.VMEM((nrow * nbf, nz), BF16),
            pltpu.VMEM((ncol * nbf, nz), BF16),
            pltpu.VMEM((LANES, nz), BF16),
            pltpu.VMEM((size, LANES), F32),
            pltpu.VMEM((size, LANES), F32),
            pltpu.VMEM((STREAMS, nrow, nbf, LANES), F32),
            pltpu.VMEM((STREAMS, LANES, nz), F32),
            pltpu.VMEM((LANES, nz), F32),
            pltpu.VMEM((LANES, nz), F32),
            pltpu.VMEM((BLOCK, LANES), F32),
            pltpu.VMEM((BLOCK, LANES), F32),
            pltpu.VMEM((2, STREAMS, ncol, nbf, LANES), F32),
            pltpu.VMEM((2, STREAMS, ncol - 1, nbf, LANES), F32),
            pltpu.VMEM((2, STREAMS, ncol, nbf, LANES), F32),
            pltpu.VMEM((STREAMS, nrow, LANES), F32),
            pltpu.VMEM((STREAMS, nrow, nrow, LANES), F32),
            pltpu.VMEM((STREAMS, nrow, nbf, LANES), F32),
            pltpu.VMEM((STREAMS, nrow - 1, nbf, LANES), F32),
            pltpu.VMEM((nrow, size // LANES, LANES), F32),
            dma((CHUNKS,)),
            dma((STREAMS,)), dma((STREAMS,)),
            dma((2, STREAMS)), dma((2, STREAMS)),
            dma((2, STREAMS)), dma((2, STREAMS)),
            dma((STREAMS,)), dma((STREAMS,)),
            dma((STREAMS,)), dma((STREAMS,)),
            dma, dma,
        ],
        compiler_params=pltpu.CompilerParams(
            collective_id=0, has_side_effects=True, vmem_limit_bytes=56 * 1024 * 1024
        ),
    )(
        rhs[0],
        factor_blocks.reshape(nz, size),
        block_rows.reshape(1, nz),
        block_cols.reshape(1, nz),
        diag_inverse[0],
        coupling.reshape(size // LANES, LANES),
    )
    return got[None]


def solution(mesh):
    placed_as = (
        P("depth", ("row", "col"), None),
        P("depth", "row", "col", None, None),
        P("depth", "row", "col", None),
        P("depth", "row", "col", None),
        P("depth", ("row", "col"), None),
        P("depth", ("row", "col"), None),
    )
    return jax.shard_map(
        functools.partial(per_device, mesh.shape["row"], mesh.shape["col"]),
        mesh=mesh,
        in_specs=placed_as,
        out_specs=P("depth", ("row", "col"), None),
        check_vma=False,
    )
```

```python
import functools

import jax
import jax.numpy as jnp
from jax import lax
from jax.experimental import pallas as pl
from jax.experimental.pallas import tpu as pltpu
from jax.sharding import PartitionSpec as P

MESH = pl.DeviceIdType.MESH
F32 = jnp.float32
BF16 = jnp.bfloat16

BLOCK = 64
LANES = 128
STREAMS = 2
TURNED = 4


def halves(x):
    hi = x.astype(BF16)
    return hi, (x - hi.astype(F32)).astype(BF16)


def picked(x, table):
    hi, lo = halves(x)
    return jnp.dot(hi, table, preferred_element_type=F32) + jnp.dot(lo, table, preferred_element_type=F32)


def placed(table, x):
    hi, lo = halves(x)
    dims = (((1,), (1,)), ((), ()))
    return lax.dot_general(table, hi, dims, preferred_element_type=F32) + lax.dot_general(
        table, lo, dims, preferred_element_type=F32
    )


def column_sums(parts):
    at = lax.broadcasted_iota(jnp.int32, parts[0].shape, 0)
    low = at < 4
    four = [
        jnp.where(low, parts[s], parts[s + 4]) + pltpu.roll(jnp.where(low, parts[s + 4], parts[s]), 4, 0)
        for s in range(4)
    ]
    low = (at & 2) == 0
    two = [
        jnp.where(low, four[s], pltpu.roll(four[s + 2], 2, 0)) + jnp.where(low, pltpu.roll(four[s], 6, 0), four[s + 2])
        for s in range(2)
    ]
    low = (at & 1) == 0
    return jnp.where(low, two[0], pltpu.roll(two[1], 1, 0)) + jnp.where(low, pltpu.roll(two[0], 7, 0), two[1])


def total(terms):
    while len(terms) > 1:
        terms = [terms[i] + terms[i + 1] if i + 1 < len(terms) else terms[i] for i in range(0, len(terms), 2)]
    return terms[0]


def act(mats, vecs, outs, count):
    def tile(t, _):
        x = [[vecs[t, pl.ds(r * BLOCK + 8 * g, 8), :] for g in range(8)] for r in range(count)]

        def group(q, _):
            parts = [[] for _ in range(count)]
            for a in range(8):
                first = pl.multiple_of(q * (8 * BLOCK) + a * BLOCK, BLOCK)
                m = [mats[t, pl.ds(first + 8 * g, 8), :] for g in range(8)]
                for r in range(count):
                    parts[r].append(total([m[g] * x[r][g] for g in range(8)]))
            for r in range(count):
                outs[t, pl.ds(pl.multiple_of(r * BLOCK + 8 * q, 8), 8), :] = column_sums(parts[r])
            return 0

        return lax.fori_loop(0, 8, group, 0)

    lax.fori_loop(0, mats.shape[0], tile, 0)


def act_back(mats, vecs, outs, count):
    def tile(t, _):
        def group(q, sums):
            sums = list(sums)
            v = [vecs[t, pl.ds(pl.multiple_of(r * BLOCK + 8 * q, 8), 8), :] for r in range(count)]
            for a in range(8):
                first = pl.multiple_of(q * (8 * BLOCK) + a * BLOCK, BLOCK)
                z = [jnp.broadcast_to(v[r][a : a + 1], (8, LANES)) for r in range(count)]
                for g in range(8):
                    m = mats[t, pl.ds(first + 8 * g, 8), :]
                    for r in range(count):
                        sums[r * 8 + g] = sums[r * 8 + g] + m * z[r]
            return tuple(sums)

        zero = jnp.zeros((8, LANES), F32)
        sums = lax.fori_loop(0, 8, group, (zero,) * (8 * count))
        for r in range(count):
            for g in range(8):
                outs[t, pl.ds(r * BLOCK + 8 * g, 8), :] = sums[r * 8 + g]
        return 0

    lax.fori_loop(0, mats.shape[0], tile, 0)


def tiles(x):
    return [x[:, LANES * t : LANES * (t + 1)] for t in range(x.shape[1] // LANES)]


def joined(ref):
    return jnp.concatenate([ref[t] for t in range(ref.shape[0])], axis=1)


def stood_up(v):
    n = v.shape[0]
    both = jnp.concatenate([v, pltpu.roll(v, BLOCK, 1), jnp.zeros((LANES - 2 * n, LANES), F32)], axis=0)
    return both.T[:BLOCK]


def laid_down(v, n):
    flat = jnp.concatenate([v, v], axis=0).T
    lane = lax.broadcasted_iota(jnp.int32, (n, LANES), 1)
    return jnp.where(lane < BLOCK, flat[:n], flat[n : 2 * n])


def kernel(
    nrow, ncol, rhs, mats, rows, cols, diag, couple, out,
    raw, mt, ohc, ohr, ohf, dt, ct, fields, xt, work, done, small, small_out, term, rs, ag, face, fx, wide, fin, cbuf,
    raw_sem, row_send, row_recv, rs_send, rs_recv, ag_send, ag_recv, fx_send, fx_recv, fin_send, fin_recv, c_send, c_recv,
):
    nbf = rhs.shape[0]
    nz = rows.shape[1]
    d, r, c = lax.axis_index("depth"), lax.axis_index("row"), lax.axis_index("col")

    def at_row(i):
        return lax.rem(r + i, nrow)

    def at_col(i):
        return lax.rem(c + i, ncol)

    def send(src, dst, send_sem, recv_sem, where):
        pltpu.make_async_remote_copy(
            src_ref=src, dst_ref=dst, send_sem=send_sem, recv_sem=recv_sem, device_id=where, device_id_type=MESH
        ).start()

    def await_bytes(ref, sem):
        pltpu.make_async_copy(ref, ref, sem).wait()

    def each(low, high, body):
        def step(i, _):
            body(i)
            return 0

        lax.fori_loop(low, high, step, 0)

    barrier = pltpu.get_barrier_semaphore()

    def greet(where):
        pl.semaphore_signal(barrier, inc=1, device_id=where, device_id_type=MESH)

    each(1, ncol, lambda i: greet((d, r, at_col(i))))
    each(1, nrow, lambda i: greet((d, at_row(i), c)))
    each(0, nrow, lambda i: greet((1 - d, at_row(i), c)))

    pieces = raw.shape[0]

    def piece(j):
        lanes = pl.ds(pl.multiple_of(j * LANES, LANES), LANES)
        return pltpu.make_async_copy(mats.at[:, lanes], raw.at[j], raw_sem.at[j])

    each(0, pieces, lambda j: piece(j).start())

    pl.semaphore_wait(barrier, (ncol - 1) + (2 * nrow - 1))

    for s in range(STREAMS):
        part = pl.ds(s * LANES, LANES)
        fields[s, 0] = rhs[:, part]
        each(
            1, nrow,
            lambda i: send(rhs.at[:, part], fields.at[s, i], row_send.at[s], row_recv.at[s], (d, at_row(i), c)),
        )

    @pl.when(d == 1)
    def _():
        cbuf[pl.ds(r, 1)] = couple[...][None]
        each(1, nrow, lambda i: send(couple, cbuf.at[r], c_send, c_recv, (1, at_row(i), c)))
        each(0, nrow, lambda i: send(couple, cbuf.at[r], c_send, c_recv, (0, at_row(i), c)))

    brow, bcol = rows[...], cols[...]
    turned_row = (((c - (brow >> 5)) & (ncol - 1)) << 5) | (brow & 31)
    turned_col = (((r - (bcol >> 5)) & (nrow - 1)) << 5) | (bcol & 31)

    def table(position, count):
        return (lax.broadcasted_iota(jnp.int32, (count, nz), 0) == position).astype(BF16)

    ohr[...] = table(turned_row, ncol * nbf)
    ohc[...] = table(turned_col, nrow * nbf)
    at_face = (bcol & 31) == jnp.where(d == 0, nbf - 1, 0)
    ohf[...] = table(jnp.where(at_face, bcol >> 5, -1), LANES)

    def turn(i):
        group = [i * TURNED + u for u in range(TURNED)]
        for j in group:
            piece(j).wait()
        for j in group:
            for t in range(nz // LANES):
                mt[t, pl.ds(pl.multiple_of(j * LANES, LANES), LANES), :] = raw[j, pl.ds(t * LANES, LANES), :].T

    each(0, pieces // TURNED, turn)

    def fill(ref, x):
        for t, part in enumerate(tiles(x)):
            ref[t] = part

    for s in range(STREAMS):
        await_bytes(fields.at[s, pl.ds(0, nrow - 1)], row_recv.at[s])
        fill(xt.at[s], picked(fields[s].reshape(nrow * nbf, LANES).T, ohc[...]))

    def turn_diag():
        def some(i):
            for u in range(TURNED):
                lanes = pl.ds(pl.multiple_of((i * TURNED + u) * LANES, LANES), LANES)
                two = diag[:, lanes]
                dt[0, lanes, :] = jnp.concatenate([two, two, jnp.zeros((LANES - 2 * nbf, LANES), F32)], axis=0).T

        each(0, dt.shape[1] // (TURNED * LANES), some)

    def turn_couple():
        def some(i):
            for u in range(TURNED):
                j = i * TURNED + u
                two = cbuf[:, pl.ds(j, 1), :].reshape(nrow, LANES)
                full = jnp.concatenate([two, two, jnp.zeros((LANES - 2 * nrow, LANES), F32)], axis=0)
                ct[0, pl.ds(pl.multiple_of(j * LANES, LANES), LANES), :] = full.T

        each(0, ct.shape[1] // (TURNED * LANES), some)

    def forward(use, s, vecs):
        act(mt, vecs, done, 2)
        term[use, s] = placed(ohr[...], joined(done)).reshape(ncol, nbf, LANES)
        each(
            1, ncol,
            lambda i: send(
                term.at[use, s, i], rs.at[use, s, i - 1], rs_send.at[use, s], rs_recv.at[use, s],
                (d, r, at_col(ncol - i)),
            ),
        )

    def middle(use, s, field):
        await_bytes(rs.at[use, s], rs_recv.at[use, s])
        small[0] = stood_up(field + term[use, s, 0] + total([rs[use, s, i] for i in range(ncol - 1)]))
        act(dt, small, small_out, 1)
        ag[use, s, 0] = laid_down(small_out[0], nbf)
        each(
            1, ncol,
            lambda i: send(
                ag.at[use, s, 0], ag.at[use, s, i], ag_send.at[use, s], ag_recv.at[use, s], (d, r, at_col(i))
            ),
        )

    def backward(use, s):
        await_bytes(ag.at[use, s, pl.ds(0, ncol - 1)], ag_recv.at[use, s])
        fill(work, picked(ag[use, s].reshape(ncol * nbf, LANES).T, ohr[...]))
        act_back(mt, work, done, 2)

    def face_out(use, s, own):
        here = lax.broadcasted_iota(jnp.int32, (nrow, LANES), 0) == r
        face[s] = placed(ohf[...], joined(done))[:nrow] + jnp.where(here, ag[use, s, 0, own : own + 1], 0.0)
        each(
            0, nrow,
            lambda i: send(face.at[s], fx.at[s, i], fx_send.at[s], fx_recv.at[s], (1 - d, at_row(i), c)),
        )

    def face_in(s, own, action):
        await_bytes(fx.at[s], fx_recv.at[s])
        small[0] = stood_up(total([fx[s, i] for i in range(nrow)]))
        action(ct, small, small_out, 1)
        moved = small_out[0]
        taken = jnp.concatenate([moved, pltpu.roll(moved, LANES - nrow, 1)], axis=0)
        for t, part in enumerate(tiles(picked(taken, ohf[...]))):
            work[t] = xt[s, t] - part
        here = lax.broadcasted_iota(jnp.int32, (nrow, LANES), 0) == r
        mine = jnp.sum(jnp.where(here, laid_down(moved, nrow), 0.0), axis=0, keepdims=True)
        at_own = lax.broadcasted_iota(jnp.int32, (nbf, LANES), 0) == own
        return fields[s, 0] - jnp.where(at_own, mine, 0.0)

    def widen(s):
        wide[s] = placed(ohc[...], joined(done)).reshape(nrow, nbf, LANES)
        each(
            1, nrow,
            lambda i: send(
                wide.at[s, i], fin.at[s, i - 1], fin_send.at[s], fin_recv.at[s], (d, at_row(nrow - i), c)
            ),
        )

    def finish(use, s):
        await_bytes(fin.at[s], fin_recv.at[s])
        out[:, pl.ds(s * LANES, LANES)] = ag[use, s, 0] + wide[s, 0] + total([fin[s, i] for i in range(nrow - 1)])

    every = range(STREAMS)

    @pl.when(d == 0)
    def _():
        for s in every:
            forward(0, s, xt.at[s])
        turn_diag()
        for s in every:
            middle(0, s, fields[s, 0])
        for s in every:
            backward(0, s)
            face_out(0, s, nbf - 1)
        await_bytes(cbuf, c_recv)
        turn_couple()
        held = []
        for s in every:
            held.append(face_in(s, nbf - 1, act_back))
            forward(1, s, work)
        for s in every:
            middle(1, s, held[s])
        for s in every:
            backward(1, s)
            widen(s)
        for s in every:
            finish(1, s)
        for s in every:
            await_bytes(term.at[1, s, pl.ds(0, ncol - 1)], rs_send.at[1, s])
            await_bytes(ag.at[1, s, pl.ds(0, ncol - 1)], ag_send.at[1, s])

    @pl.when(d == 1)
    def _():
        await_bytes(cbuf.at[pl.ds(0, nrow - 1)], c_recv)
        turn_couple()
        turn_diag()
        held = []
        for s in every:
            held.append(face_in(s, 0, act))
            forward(0, s, work)
        for s in every:
            middle(0, s, held[s])
        for s in every:
            backward(0, s)
            face_out(0, s, 0)
            widen(s)
        for s in every:
            finish(0, s)
        await_bytes(cbuf.at[pl.ds(0, nrow - 1)], c_send)
        await_bytes(cbuf, c_send)

    for s in every:
        await_bytes(fields.at[s, pl.ds(0, nrow - 1)], row_send.at[s])
        await_bytes(term.at[0, s, pl.ds(0, ncol - 1)], rs_send.at[0, s])
        await_bytes(ag.at[0, s, pl.ds(0, ncol - 1)], ag_send.at[0, s])
        await_bytes(fx.at[s], fx_send.at[s])
        await_bytes(wide.at[s, pl.ds(0, nrow - 1)], fin_send.at[s])


def per_device(nrow, ncol, rhs, factor_blocks, block_rows, block_cols, diag_inverse, coupling):
    nbf = rhs.shape[1]
    nz, size = factor_blocks.shape[-2:]
    vm = pl.BlockSpec(memory_space=pltpu.VMEM)
    dma = pltpu.SemaphoreType.DMA
    got = pl.pallas_call(
        functools.partial(kernel, nrow, ncol),
        out_shape=jax.ShapeDtypeStruct((nbf, rhs.shape[2]), F32),
        in_specs=[vm, pl.BlockSpec(memory_space=pl.ANY), vm, vm, vm, vm],
        out_specs=vm,
        scratch_shapes=[
            pltpu.VMEM((size // LANES, nz, LANES), F32),
            pltpu.VMEM((nz // LANES, size, LANES), F32),
            pltpu.VMEM((nrow * nbf, nz), BF16),
            pltpu.VMEM((ncol * nbf, nz), BF16),
            pltpu.VMEM((LANES, nz), BF16),
            pltpu.VMEM((1, size, LANES), F32),
            pltpu.VMEM((1, size, LANES), F32),
            pltpu.VMEM((STREAMS, nrow, nbf, LANES), F32),
            pltpu.VMEM((STREAMS, nz // LANES, LANES, LANES), F32),
            pltpu.VMEM((nz // LANES, LANES, LANES), F32),
            pltpu.VMEM((nz // LANES, LANES, LANES), F32),
            pltpu.VMEM((1, BLOCK, LANES), F32),
            pltpu.VMEM((1, BLOCK, LANES), F32),
            pltpu.VMEM((2, STREAMS, ncol, nbf, LANES), F32),
            pltpu.VMEM((2, STREAMS, ncol - 1, nbf, LANES), F32),
            pltpu.VMEM((2, STREAMS, ncol, nbf, LANES), F32),
            pltpu.VMEM((STREAMS, nrow, LANES), F32),
            pltpu.VMEM((STREAMS, nrow, nrow, LANES), F32),
            pltpu.VMEM((STREAMS, nrow, nbf, LANES), F32),
            pltpu.VMEM((STREAMS, nrow - 1, nbf, LANES), F32),
            pltpu.VMEM((nrow, size // LANES, LANES), F32),
            dma((size // LANES,)),
            dma((STREAMS,)), dma((STREAMS,)),
            dma((2, STREAMS)), dma((2, STREAMS)),
            dma((2, STREAMS)), dma((2, STREAMS)),
            dma((STREAMS,)), dma((STREAMS,)),
            dma((STREAMS,)), dma((STREAMS,)),
            dma, dma,
        ],
        compiler_params=pltpu.CompilerParams(
            collective_id=0, has_side_effects=True, vmem_limit_bytes=56 * 1024 * 1024
        ),
    )(
        rhs[0],
        factor_blocks.reshape(nz, size),
        block_rows.reshape(1, nz),
        block_cols.reshape(1, nz),
        diag_inverse[0],
        coupling.reshape(size // LANES, LANES),
    )
    return got[None]


def solution(mesh):
    placed_as = (
        P("depth", ("row", "col"), None),
        P("depth", "row", "col", None, None),
        P("depth", "row", "col", None),
        P("depth", "row", "col", None),
        P("depth", ("row", "col"), None),
        P("depth", ("row", "col"), None),
    )
    return jax.shard_map(
        functools.partial(per_device, mesh.shape["row"], mesh.shape["col"]),
        mesh=mesh,
        in_specs=placed_as,
        out_specs=P("depth", ("row", "col"), None),
        check_vma=False,
    )
```

```python
import functools
import math

import jax
import jax.numpy as jnp
from jax import lax
from jax.experimental import pallas as pl
from jax.experimental.pallas import tpu as pltpu
from jax.sharding import PartitionSpec as P

MESH = pl.DeviceIdType.MESH
F32 = jnp.float32
BF16 = jnp.bfloat16

BLOCK = 64
LANES = 128
STREAMS = 2
TURNED = 4


def halves(x):
    hi = x.astype(BF16)
    return hi, (x - hi.astype(F32)).astype(BF16)


def picked(x, table):
    hi, lo = halves(x)
    return jnp.dot(hi, table, preferred_element_type=F32) + jnp.dot(lo, table, preferred_element_type=F32)


def placed(table, x):
    hi, lo = halves(x)
    dims = (((1,), (1,)), ((), ()))
    return lax.dot_general(table, hi, dims, preferred_element_type=F32) + lax.dot_general(
        table, lo, dims, preferred_element_type=F32
    )


def column_sums(parts):
    at = lax.broadcasted_iota(jnp.int32, parts[0].shape, 0)
    low = at < 4
    four = [
        jnp.where(low, parts[s], parts[s + 4]) + pltpu.roll(jnp.where(low, parts[s + 4], parts[s]), 4, 0)
        for s in range(4)
    ]
    low = (at & 2) == 0
    two = [
        jnp.where(low, four[s], pltpu.roll(four[s + 2], 2, 0)) + jnp.where(low, pltpu.roll(four[s], 6, 0), four[s + 2])
        for s in range(2)
    ]
    low = (at & 1) == 0
    return jnp.where(low, two[0], pltpu.roll(two[1], 1, 0)) + jnp.where(low, pltpu.roll(two[0], 7, 0), two[1])


def total(terms):
    while len(terms) > 1:
        terms = [terms[i] + terms[i + 1] if i + 1 < len(terms) else terms[i] for i in range(0, len(terms), 2)]
    return terms[0]


def act(mats, vecs, outs, count):
    def tile(t, _):
        x = [[vecs[t, pl.ds(r * BLOCK + 8 * g, 8), :] for g in range(8)] for r in range(count)]

        def group(q, _):
            parts = [[] for _ in range(count)]
            for a in range(8):
                first = pl.multiple_of(q * (8 * BLOCK) + a * BLOCK, BLOCK)
                m = [mats[t, pl.ds(first + 8 * g, 8), :] for g in range(8)]
                for r in range(count):
                    parts[r].append(total([m[g] * x[r][g] for g in range(8)]))
            for r in range(count):
                outs[t, pl.ds(pl.multiple_of(r * BLOCK + 8 * q, 8), 8), :] = column_sums(parts[r])
            return 0

        return lax.fori_loop(0, 8, group, 0)

    lax.fori_loop(0, mats.shape[0], tile, 0)


def act_back(mats, vecs, outs, count):
    def tile(t, _):
        def group(q, sums):
            sums = list(sums)
            v = [vecs[t, pl.ds(pl.multiple_of(r * BLOCK + 8 * q, 8), 8), :] for r in range(count)]
            for a in range(8):
                first = pl.multiple_of(q * (8 * BLOCK) + a * BLOCK, BLOCK)
                z = [jnp.broadcast_to(v[r][a : a + 1], (8, LANES)) for r in range(count)]
                for g in range(8):
                    m = mats[t, pl.ds(first + 8 * g, 8), :]
                    for r in range(count):
                        sums[r * 8 + g] = sums[r * 8 + g] + m * z[r]
            return tuple(sums)

        zero = jnp.zeros((8, LANES), F32)
        sums = lax.fori_loop(0, 8, group, (zero,) * (8 * count))
        for r in range(count):
            for g in range(8):
                outs[t, pl.ds(r * BLOCK + 8 * g, 8), :] = sums[r * 8 + g]
        return 0

    lax.fori_loop(0, mats.shape[0], tile, 0)


def tiles(x):
    return [x[:, LANES * t : LANES * (t + 1)] for t in range(x.shape[1] // LANES)]


def joined(ref):
    return jnp.concatenate([ref[t] for t in range(ref.shape[0])], axis=1)


def stood_up(v):
    n = v.shape[0]
    both = jnp.concatenate([v, pltpu.roll(v, BLOCK, 1), jnp.zeros((LANES - 2 * n, LANES), F32)], axis=0)
    return both.T[:BLOCK]


def laid_down(v, n):
    flat = jnp.concatenate([v, v], axis=0).T
    lane = lax.broadcasted_iota(jnp.int32, (n, LANES), 1)
    return jnp.where(lane < BLOCK, flat[:n], flat[n : 2 * n])


def kernel(
    nrow, ncol, rhs, mats, rows, cols, diag, couple, out,
    raw, mt, ohc, ohr, ohf, dt, ct, fields, xt, work, done, small, small_out, term, rs, ag, face, fx, wide, fin, cbuf, diag0,
    index0, raw_sem, row_send, row_recv, rs_send, rs_recv, ag_send, ag_recv, fx_send, fx_recv, fin_send, fin_recv, c_send,
    c_recv, early_send, early_recv, late_send, late_recv,
):
    nbf = rhs.shape[0]
    nz = rows.shape[1]
    side = math.isqrt(ncol)
    d, r, c = lax.axis_index("depth"), lax.axis_index("row"), lax.axis_index("col")
    cy, cx = lax.div(c, side), lax.rem(c, side)

    def at_row(i):
        return lax.rem(r + i, nrow)

    def at_col(i):
        return lax.rem(cy + lax.div(i, side), side) * side + lax.rem(cx + lax.rem(i, side), side)

    def back_col(i):
        return lax.rem(cy - lax.div(i, side) + side, side) * side + lax.rem(cx - lax.rem(i, side) + side, side)

    def far_row(j):
        return nrow // 2 + lax.div(j + 1, 2) * (1 - 2 * lax.rem(j, 2))

    def far_side(j):
        return lax.rem(side // 2 + lax.div(j * (j + 1), 2), side)

    def far_col(j):
        return far_side(lax.div(j, side)) * side + far_side(lax.rem(j, side))

    def send(src, dst, send_sem, recv_sem, where):
        pltpu.make_async_remote_copy(
            src_ref=src, dst_ref=dst, send_sem=send_sem, recv_sem=recv_sem, device_id=where, device_id_type=MESH
        ).start()

    def await_bytes(ref, sem):
        pltpu.make_async_copy(ref, ref, sem).wait()

    def each(low, high, body):
        def step(i, _):
            body(i)
            return 0

        lax.fori_loop(low, high, step, 0)

    def each_col(body):
        each(0, ncol - 1, lambda j: body(far_col(j)))

    def each_row(body):
        each(0, nrow - 1, lambda j: body(far_row(j)))

    barrier = pltpu.get_barrier_semaphore()

    def greet(where):
        pl.semaphore_signal(barrier, inc=1, device_id=where, device_id_type=MESH)

    each_row(lambda i: greet((d, at_row(i), c)))
    each_row(lambda i: greet((1 - d, at_row(i), c)))
    each_col(lambda i: greet((d, r, at_col(i))))
    greet((1 - d, r, c))

    pieces = raw.shape[0]

    def piece(j):
        lanes = pl.ds(pl.multiple_of(j * LANES, LANES), LANES)
        return pltpu.make_async_copy(mats.at[:, lanes], raw.at[j], raw_sem.at[j])

    each(0, pieces, lambda j: piece(j).start())

    pl.semaphore_wait(barrier, (ncol - 1) + (2 * nrow - 1))

    for s in range(STREAMS):
        part = pl.ds(s * LANES, LANES)
        fields[0, s, 0] = rhs[:, part]
        each_row(lambda i: send(rhs.at[:, part], fields.at[0, s, i], row_send.at[s], row_recv.at[s], (d, at_row(i), c)))

    @pl.when(d == 0)
    def _():
        index0[0, 0:1] = rows[...]
        index0[0, 1:2] = cols[...]
        send(index0.at[0], index0.at[1], early_send.at[0], early_recv.at[0], (1, r, c))
        send(diag, diag0, early_send.at[1], early_recv.at[1], (1, r, c))

    @pl.when(d == 1)
    def _():
        cbuf[pl.ds(r, 1)] = couple[...][None]
        each_row(lambda i: send(couple, cbuf.at[r], c_send, c_recv, (1, at_row(i), c)))

    def tables(use, brow, bcol, own_face):
        oy, ox = (brow >> 5) // side, (brow >> 5) % side
        slot_row = ((cy - oy) & (side - 1)) * side + ((cx - ox) & (side - 1))
        slot_col = (r - (bcol >> 5)) & (nrow - 1)

        def table(position, count):
            return (lax.broadcasted_iota(jnp.int32, (count, nz), 0) == position).astype(BF16)

        ohr[use] = table((slot_row << 5) | (brow & 31), ncol * nbf)
        ohc[use] = table((slot_col << 5) | (bcol & 31), nrow * nbf)
        ohf[use] = table(jnp.where((bcol & 31) == own_face, bcol >> 5, -1), LANES)

    tables(0, rows[...], cols[...], jnp.where(d == 0, nbf - 1, 0))

    def turn(i):
        group = [i * TURNED + u for u in range(TURNED)]
        for j in group:
            piece(j).wait()
        for j in group:
            for t in range(nz // LANES):
                mt[0, t, pl.ds(pl.multiple_of(j * LANES, LANES), LANES), :] = raw[j, pl.ds(t * LANES, LANES), :].T

    each(0, pieces // TURNED, turn)

    def fill(ref, x):
        for t, part in enumerate(tiles(x)):
            ref[t] = part

    for s in range(STREAMS):
        await_bytes(fields.at[0, s, pl.ds(0, nrow - 1)], row_recv.at[s])
        fill(xt.at[0, s], picked(fields[0, s].reshape(nrow * nbf, LANES).T, ohc[0]))

    def turn_diag(use, given):
        def some(i):
            for u in range(TURNED):
                lanes = pl.ds(pl.multiple_of((i * TURNED + u) * LANES, LANES), LANES)
                two = given[:, lanes]
                full = jnp.concatenate([two, two, jnp.zeros((LANES - 2 * nbf, LANES), F32)], axis=0)
                dt[use, 0, lanes, :] = full.T

        each(0, dt.shape[2] // (TURNED * LANES), some)

    def turn_couple():
        def some(i):
            for u in range(TURNED):
                j = i * TURNED + u
                two = cbuf[:, pl.ds(j, 1), :].reshape(nrow, LANES)
                full = jnp.concatenate([two, two, jnp.zeros((LANES - 2 * nrow, LANES), F32)], axis=0)
                ct[0, pl.ds(pl.multiple_of(j * LANES, LANES), LANES), :] = full.T

        each(0, ct.shape[1] // (TURNED * LANES), some)

    def forward(use, s, vecs):
        act(mt.at[use], vecs, done.at[s], 2)
        term[use, s] = placed(ohr[use], joined(done.at[s])).reshape(ncol, nbf, LANES)
        each_col(
            lambda i: send(
                term.at[use, s, i], rs.at[use, s, i - 1], rs_send.at[use, s], rs_recv.at[use, s], (d, r, back_col(i))
            )
        )

    def middle(use, s, field):
        await_bytes(rs.at[use, s], rs_recv.at[use, s])
        small[0] = stood_up(field + term[use, s, 0] + total([rs[use, s, i] for i in range(ncol - 1)]))
        act(dt.at[use], small, small_out, 1)
        ag[use, s, 0] = laid_down(small_out[0], nbf)
        each_col(
            lambda i: send(
                ag.at[use, s, 0], ag.at[use, s, i], ag_send.at[use, s], ag_recv.at[use, s], (d, r, at_col(i))
            )
        )

    def backward(use, s):
        await_bytes(ag.at[use, s, pl.ds(0, ncol - 1)], ag_recv.at[use, s])
        fill(work, picked(ag[use, s].reshape(ncol * nbf, LANES).T, ohr[use]))
        act_back(mt.at[use], work, done.at[s], 2)

    def face_out(use, s, own):
        here = lax.broadcasted_iota(jnp.int32, (nrow, LANES), 0) == r
        face[s] = placed(ohf[use], joined(done.at[s]))[:nrow] + jnp.where(here, ag[use, s, 0, own : own + 1], 0.0)

    def face_in(use, s, own, action, take):
        small[0] = stood_up(total([fx[take, s, i] for i in range(nrow)]))
        action(ct, small, small_out, 1)
        moved = small_out[0]
        taken = jnp.concatenate([moved, pltpu.roll(moved, LANES - nrow, 1)], axis=0)
        for t, part in enumerate(tiles(picked(taken, ohf[use]))):
            work[t] = xt[use, s, t] - part
        here = lax.broadcasted_iota(jnp.int32, (nrow, LANES), 0) == r
        mine = jnp.sum(jnp.where(here, laid_down(moved, nrow), 0.0), axis=0, keepdims=True)
        at_own = lax.broadcasted_iota(jnp.int32, (nbf, LANES), 0) == own
        return fields[use, s, 0] - jnp.where(at_own, mine, 0.0)

    def widen(use, s):
        wide[use, s] = placed(ohc[use], joined(done.at[s])).reshape(nrow, nbf, LANES)

    every = range(STREAMS)

    @pl.when(d == 0)
    def _():
        for s in every:
            forward(0, s, xt.at[0, s])
        turn_diag(0, diag)
        for s in every:
            middle(0, s, fields[0, s, 0])
        for s in every:
            backward(0, s)
            face_out(0, s, nbf - 1)
            each_row(lambda i: send(face.at[s], fx.at[0, s, i], fx_send.at[0, s], fx_recv.at[0, s], (1, at_row(i), c)))
            send(face.at[s], fx.at[0, s, 0], fx_send.at[0, s], fx_recv.at[0, s], (1, r, c))
        send(xt.at[0], xt.at[1], late_send.at[0], late_recv.at[0], (1, r, c))
        send(fields.at[0, :, 0], fields.at[1, :, 0], late_send.at[1], late_recv.at[1], (1, r, c))
        for t in range(nz // LANES):
            send(mt.at[0, t], mt.at[1, t], late_send.at[2 + t], late_recv.at[2 + t], (1, r, c))
        for s in every:
            await_bytes(fin.at[s], fin_recv.at[s])
            out[:, pl.ds(s * LANES, LANES)] = total([fin[s, i] for i in range(nrow)])
        for s in every:
            await_bytes(fx.at[0, s], fx_send.at[0, s])
        pltpu.make_async_copy(index0.at[0], index0.at[0], early_send.at[0]).wait()
        await_bytes(diag, early_send.at[1])
        await_bytes(xt.at[0], late_send.at[0])
        await_bytes(fields.at[0, :, 0], late_send.at[1])
        for t in range(nz // LANES):
            await_bytes(mt.at[0, t], late_send.at[2 + t])

    @pl.when(d == 1)
    def _():
        await_bytes(cbuf.at[pl.ds(0, nrow - 1)], c_recv)
        turn_couple()
        turn_diag(0, diag)
        await_bytes(index0.at[1], early_recv.at[0])
        tables(1, index0[1, 0:1], index0[1, 1:2], nbf - 1)
        await_bytes(diag0, early_recv.at[1])
        turn_diag(1, diag0)
        held = []
        for s in every:
            await_bytes(fx.at[0, s], fx_recv.at[0, s])
            held.append(face_in(0, s, 0, act, 0))
            forward(0, s, work)
        for s in every:
            middle(0, s, held[s])
        for s in every:
            backward(0, s)
            face_out(0, s, 0)
            each_row(lambda i: send(face.at[s], fx.at[1, s, i], fx_send.at[1, s], fx_recv.at[1, s], (1, at_row(i), c)))
            fx[1, s, 0] = face[s]
        for s in every:
            widen(0, s)
            each_row(
                lambda i: send(
                    wide.at[0, s, i], fin.at[s, i], fin_send.at[0, s], fin_recv.at[s], (1, at_row(nrow - i), c)
                )
            )
        await_bytes(xt.at[1], late_recv.at[0])
        await_bytes(fields.at[1, :, 0], late_recv.at[1])
        for t in range(nz // LANES):
            await_bytes(mt.at[1, t], late_recv.at[2 + t])
        held = []
        for s in every:
            await_bytes(fx.at[1, s, pl.ds(0, nrow - 1)], fx_recv.at[1, s])
            held.append(face_in(1, s, nbf - 1, act_back, 1))
            forward(1, s, work)
        for s in every:
            await_bytes(fin.at[s, pl.ds(0, nrow - 1)], fin_recv.at[s])
            out[:, pl.ds(s * LANES, LANES)] = (
                ag[0, s, 0] + wide[0, s, 0] + total([fin[s, i] for i in range(1, nrow)])
            )
        for s in every:
            middle(1, s, held[s])
        for s in every:
            backward(1, s)
            widen(1, s)
            wide[1, s, 0] += ag[1, s, 0]
            each_row(
                lambda i: send(
                    wide.at[1, s, i], fin.at[s, i], fin_send.at[1, s], fin_recv.at[s], (0, at_row(nrow - i), c)
                )
            )
            send(wide.at[1, s, 0], fin.at[s, 0], fin_send.at[1, s], fin_recv.at[s], (0, r, c))
        await_bytes(cbuf.at[pl.ds(0, nrow - 1)], c_send)
        for s in every:
            await_bytes(fx.at[1, s, pl.ds(0, nrow - 1)], fx_send.at[1, s])
            await_bytes(wide.at[0, s, pl.ds(0, nrow - 1)], fin_send.at[0, s])
            await_bytes(wide.at[1, s], fin_send.at[1, s])
            await_bytes(term.at[1, s, pl.ds(0, ncol - 1)], rs_send.at[1, s])
            await_bytes(ag.at[1, s, pl.ds(0, ncol - 1)], ag_send.at[1, s])

    for s in every:
        await_bytes(fields.at[0, s, pl.ds(0, nrow - 1)], row_send.at[s])
        await_bytes(term.at[0, s, pl.ds(0, ncol - 1)], rs_send.at[0, s])
        await_bytes(ag.at[0, s, pl.ds(0, ncol - 1)], ag_send.at[0, s])


def per_device(nrow, ncol, rhs, factor_blocks, block_rows, block_cols, diag_inverse, coupling):
    nbf = rhs.shape[1]
    nz, size = factor_blocks.shape[-2:]
    vm = pl.BlockSpec(memory_space=pltpu.VMEM)
    dma = pltpu.SemaphoreType.DMA
    got = pl.pallas_call(
        functools.partial(kernel, nrow, ncol),
        out_shape=jax.ShapeDtypeStruct((nbf, rhs.shape[2]), F32),
        in_specs=[vm, pl.BlockSpec(memory_space=pl.ANY), vm, vm, vm, vm],
        out_specs=vm,
        scratch_shapes=[
            pltpu.VMEM((size // LANES, nz, LANES), F32),
            pltpu.VMEM((2, nz // LANES, size, LANES), F32),
            pltpu.VMEM((2, nrow * nbf, nz), BF16),
            pltpu.VMEM((2, ncol * nbf, nz), BF16),
            pltpu.VMEM((2, LANES, nz), BF16),
            pltpu.VMEM((2, 1, size, LANES), F32),
            pltpu.VMEM((1, size, LANES), F32),
            pltpu.VMEM((2, STREAMS, nrow, nbf, LANES), F32),
            pltpu.VMEM((2, STREAMS, nz // LANES, LANES, LANES), F32),
            pltpu.VMEM((nz // LANES, LANES, LANES), F32),
            pltpu.VMEM((STREAMS, nz // LANES, LANES, LANES), F32),
            pltpu.VMEM((1, BLOCK, LANES), F32),
            pltpu.VMEM((1, BLOCK, LANES), F32),
            pltpu.VMEM((2, STREAMS, ncol, nbf, LANES), F32),
            pltpu.VMEM((2, STREAMS, ncol - 1, nbf, LANES), F32),
            pltpu.VMEM((2, STREAMS, ncol, nbf, LANES), F32),
            pltpu.VMEM((STREAMS, nrow, LANES), F32),
            pltpu.VMEM((2, STREAMS, nrow, nrow, LANES), F32),
            pltpu.VMEM((2, STREAMS, nrow, nbf, LANES), F32),
            pltpu.VMEM((STREAMS, nrow, nbf, LANES), F32),
            pltpu.VMEM((nrow, size // LANES, LANES), F32),
            pltpu.VMEM((nbf, size), F32),
            pltpu.VMEM((2, 2, nz), jnp.int32),
            dma((size // LANES,)),
            dma((STREAMS,)), dma((STREAMS,)),
            dma((2, STREAMS)), dma((2, STREAMS)),
            dma((2, STREAMS)), dma((2, STREAMS)),
            dma((2, STREAMS)), dma((2, STREAMS)),
            dma((2, STREAMS)), dma((STREAMS,)),
            dma, dma,
            dma((2,)), dma((2,)),
            dma((2 + nz // LANES,)), dma((2 + nz // LANES,)),
        ],
        compiler_params=pltpu.CompilerParams(
            collective_id=0, has_side_effects=True, vmem_limit_bytes=56 * 1024 * 1024
        ),
    )(
        rhs[0],
        factor_blocks.reshape(nz, size),
        block_rows.reshape(1, nz),
        block_cols.reshape(1, nz),
        diag_inverse[0],
        coupling.reshape(size // LANES, LANES),
    )
    return got[None]


def solution(mesh):
    placed_as = (
        P("depth", ("row", "col"), None),
        P("depth", "row", "col", None, None),
        P("depth", "row", "col", None),
        P("depth", "row", "col", None),
        P("depth", ("row", "col"), None),
        P("depth", ("row", "col"), None),
    )
    return jax.shard_map(
        functools.partial(per_device, mesh.shape["row"], mesh.shape["col"]),
        mesh=mesh,
        in_specs=placed_as,
        out_specs=P("depth", ("row", "col"), None),
        check_vma=False,
    )
```

```python
import functools
import math

import jax
import jax.numpy as jnp
from jax import lax
from jax.experimental import pallas as pl
from jax.experimental.pallas import tpu as pltpu
from jax.sharding import PartitionSpec as P

MESH = pl.DeviceIdType.MESH
F32 = jnp.float32
BF16 = jnp.bfloat16

BLOCK = 64
LANES = 128
STREAMS = 2
TURNED = 4


def halves(x):
    hi = x.astype(BF16)
    return hi, (x - hi.astype(F32)).astype(BF16)


def picked(x, table):
    n = x.shape[0]
    both = jnp.dot(jnp.concatenate(halves(x), axis=0), table, preferred_element_type=F32)
    return both[:n] + both[n:]


def placed(table, x):
    n = x.shape[0]
    dims = (((1,), (1,)), ((), ()))
    both = lax.dot_general(table, jnp.concatenate(halves(x), axis=0), dims, preferred_element_type=F32)
    return both[:, :n] + both[:, n:]


def column_sums(parts):
    at = lax.broadcasted_iota(jnp.int32, parts[0].shape, 0)
    low = at < 4
    four = [
        jnp.where(low, parts[s], parts[s + 4]) + pltpu.roll(jnp.where(low, parts[s + 4], parts[s]), 4, 0)
        for s in range(4)
    ]
    low = (at & 2) == 0
    two = [
        jnp.where(low, four[s], pltpu.roll(four[s + 2], 2, 0)) + jnp.where(low, pltpu.roll(four[s], 6, 0), four[s + 2])
        for s in range(2)
    ]
    low = (at & 1) == 0
    return jnp.where(low, two[0], pltpu.roll(two[1], 1, 0)) + jnp.where(low, pltpu.roll(two[0], 7, 0), two[1])


def total(terms):
    while len(terms) > 1:
        terms = [terms[i] + terms[i + 1] if i + 1 < len(terms) else terms[i] for i in range(0, len(terms), 2)]
    return terms[0]


def act(mats, vecs, outs, count):
    def tile(t, _):
        x = [[vecs[t, pl.ds(r * BLOCK + 8 * g, 8), :] for g in range(8)] for r in range(count)]

        def group(q, _):
            parts = [[] for _ in range(count)]
            for a in range(8):
                first = pl.multiple_of(q * (8 * BLOCK) + a * BLOCK, BLOCK)
                m = [mats[t, pl.ds(first + 8 * g, 8), :] for g in range(8)]
                for r in range(count):
                    parts[r].append(total([m[g] * x[r][g] for g in range(8)]))
            for r in range(count):
                outs[t, pl.ds(pl.multiple_of(r * BLOCK + 8 * q, 8), 8), :] = column_sums(parts[r])
            return 0

        return lax.fori_loop(0, mats.shape[1] // (8 * BLOCK), group, 0)

    lax.fori_loop(0, mats.shape[0], tile, 0)


def act_back(mats, vecs, outs, count):
    def tile(t, _):
        def group(q, sums):
            sums = list(sums)
            v = [vecs[t, pl.ds(pl.multiple_of(r * BLOCK + 8 * q, 8), 8), :] for r in range(count)]
            for a in range(8):
                first = pl.multiple_of(q * (8 * BLOCK) + a * BLOCK, BLOCK)
                z = [jnp.broadcast_to(v[r][a : a + 1], (8, LANES)) for r in range(count)]
                for g in range(8):
                    m = mats[t, pl.ds(first + 8 * g, 8), :]
                    for r in range(count):
                        sums[r * 8 + g] = sums[r * 8 + g] + m * z[r]
            return tuple(sums)

        zero = jnp.zeros((8, LANES), F32)
        sums = lax.fori_loop(0, 8, group, (zero,) * (8 * count))
        for r in range(count):
            for g in range(8):
                outs[t, pl.ds(r * BLOCK + 8 * g, 8), :] = sums[r * 8 + g]
        return 0

    lax.fori_loop(0, mats.shape[0], tile, 0)


def tiles(x):
    return [x[:, LANES * t : LANES * (t + 1)] for t in range(x.shape[1] // LANES)]


def joined(ref):
    return jnp.concatenate([ref[t] for t in range(ref.shape[0])], axis=1)


def stood_up(v):
    n = v.shape[0]
    both = jnp.concatenate([v, pltpu.roll(v, BLOCK, 1), jnp.zeros((LANES - 2 * n, LANES), F32)], axis=0)
    return both.T[:BLOCK]


def laid_down(v, n):
    flat = jnp.concatenate([v, v], axis=0).T
    lane = lax.broadcasted_iota(jnp.int32, (n, LANES), 1)
    return jnp.where(lane < BLOCK, flat[:n], flat[n : 2 * n])


def stood_up_twice(v):
    pair = [v, pltpu.roll(v, BLOCK, 1)]
    return jnp.concatenate(pair + pair, axis=0).T[:BLOCK]


def laid_down_halves(v, n):
    flat = jnp.concatenate([v] * 4, axis=0).T
    quarter = lax.broadcasted_iota(jnp.int32, (n, LANES), 1) // (BLOCK // 2)
    low = jnp.where(quarter == 0, flat[:n], flat[2 * n : 3 * n])
    high = jnp.where(quarter == 2, flat[n : 2 * n], flat[3 * n :])
    return jnp.where(quarter < 2, low, high)


def kernel(
    nrow, ncol, rhs_in, mats, rows_in, cols_in, diag_in, couple_in, out,
    rhs, rows, cols, diag, couple, raw, mt, ohc, ohr, ohf, dt, ct, fields, xt, work, done, small, small_out, term, rs, ag, face, fx, wide, fin, cbuf, diag0,
    index0, raw_sem, row_send, row_recv, rs_send, rs_recv, ag_send, ag_recv, fx_send, fx_recv, fin_send, fin_recv, c_send,
    c_recv, early_send, early_recv, late_send, late_recv, in_sem,
):
    nbf = rhs.shape[0]
    nz = rows.shape[1]
    side = math.isqrt(ncol)
    d, r, c = lax.axis_index("depth"), lax.axis_index("row"), lax.axis_index("col")
    cy, cx = lax.div(c, side), lax.rem(c, side)

    def at_row(i):
        return lax.rem(r + i, nrow)

    def at_col(i):
        return lax.rem(cy + lax.div(i, side), side) * side + lax.rem(cx + lax.rem(i, side), side)

    def back_col(i):
        return lax.rem(cy - lax.div(i, side) + side, side) * side + lax.rem(cx - lax.rem(i, side) + side, side)

    def far_row(j):
        return nrow // 2 + lax.div(j + 1, 2) * (1 - 2 * lax.rem(j, 2))

    def far_side(j):
        return lax.rem(side // 2 + lax.div(j * (j + 1), 2), side)

    def far_col(j):
        return far_side(lax.div(j, side)) * side + far_side(lax.rem(j, side))

    def send(src, dst, send_sem, recv_sem, where):
        pltpu.make_async_remote_copy(
            src_ref=src, dst_ref=dst, send_sem=send_sem, recv_sem=recv_sem, device_id=where, device_id_type=MESH
        ).start()

    def await_bytes(ref, sem):
        pltpu.make_async_copy(ref, ref, sem).wait()

    def each(low, high, body):
        def step(i, _):
            body(i)
            return 0

        lax.fori_loop(low, high, step, 0)

    def each_col(body):
        each(0, ncol - 1, lambda j: body(far_col(j)))

    def each_row(body):
        each(0, nrow - 1, lambda j: body(far_row(j)))

    barrier = pltpu.get_barrier_semaphore()

    def greet(where):
        pl.semaphore_signal(barrier, inc=1, device_id=where, device_id_type=MESH)

    each_row(lambda i: greet((d, at_row(i), c)))
    each_row(lambda i: greet((1 - d, at_row(i), c)))
    each_col(lambda i: greet((d, r, at_col(i))))
    greet((1 - d, r, c))

    pieces = raw.shape[0]

    def piece(j):
        lanes = pl.ds(pl.multiple_of(j * LANES, LANES), LANES)
        return pltpu.make_async_copy(mats.at[:, lanes], raw.at[j], raw_sem.at[j])

    inputs = [
        pltpu.make_async_copy(src, dst, in_sem.at[i])
        for i, (src, dst) in enumerate(
            ((rhs_in, rhs), (rows_in, rows), (cols_in, cols), (couple_in, couple), (diag_in, diag))
        )
    ]
    for copy in inputs:
        copy.start()
    each(0, pieces, lambda j: piece(j).start())
    for copy in inputs:
        copy.wait()
    pl.semaphore_wait(barrier, (ncol - 1) + (2 * nrow - 1))

    def share_field(s):
        part = pl.ds(s * LANES, LANES)
        fields[0, s, 0] = rhs[:, part]
        each_row(lambda i: send(rhs.at[:, part], fields.at[0, s, i], row_send.at[s], row_recv.at[s], (d, at_row(i), c)))

    @pl.when(d == 0)
    def _():
        for s in range(STREAMS):
            share_field(s)

    def tables(use, brow, bcol, own_face):
        oy, ox = (brow >> 5) // side, (brow >> 5) % side
        slot_row = ((cy - oy) & (side - 1)) * side + ((cx - ox) & (side - 1))
        slot_col = (r - (bcol >> 5)) & (nrow - 1)

        def table(position, count):
            return (lax.broadcasted_iota(jnp.int32, (count, nz), 0) == position).astype(BF16)

        ohr[use] = table((slot_row << 5) | (brow & 31), ncol * nbf)
        ohc[use] = table((slot_col << 5) | (bcol & 31), nrow * nbf)
        ohf[use] = table(jnp.where((bcol & 31) == own_face, bcol >> 5, -1), LANES)

    tables(0, rows[...], cols[...], jnp.where(d == 0, nbf - 1, 0))

    def turn(i):
        group = [i * TURNED + u for u in range(TURNED)]
        for j in group:
            piece(j).wait()
        for j in group:
            for t in range(nz // LANES):
                mt[0, t, pl.ds(pl.multiple_of(j * LANES, LANES), LANES), :] = raw[j, pl.ds(t * LANES, LANES), :].T

    each(0, pieces // TURNED, turn)

    @pl.when(d == 1)
    def _():
        for s in range(STREAMS):
            share_field(s)
        cbuf[pl.ds(r, 1)] = couple[...][None]
        each_row(lambda i: send(couple, cbuf.at[r], c_send, c_recv, (1, at_row(i), c)))

    def fill(ref, x):
        for t, part in enumerate(tiles(x)):
            ref[t] = part

    for s in range(STREAMS):
        await_bytes(fields.at[0, s, pl.ds(0, nrow - 1)], row_recv.at[s])
        fill(xt.at[0, s], picked(fields[0, s].reshape(nrow * nbf, LANES).T, ohc[0]))

    def turn_diag(use, given):
        apart = given.shape[1] // (2 * LANES)

        def some(i):
            for u in range(TURNED):
                j = i * TURNED + u
                low, high = (given[:, pl.ds(pl.multiple_of(k * LANES, LANES), LANES)] for k in (j, j + apart))
                full = jnp.concatenate([low, low, high, high], axis=0)
                dt[use, 0, pl.ds(pl.multiple_of(j * LANES, LANES), LANES), :] = full.T

        each(0, apart // TURNED, some)

    def turn_couple():
        def some(i):
            for u in range(TURNED):
                j = i * TURNED + u
                two = cbuf[:, pl.ds(j, 1), :].reshape(nrow, LANES)
                full = jnp.concatenate([two, two, jnp.zeros((LANES - 2 * nrow, LANES), F32)], axis=0)
                ct[0, pl.ds(pl.multiple_of(j * LANES, LANES), LANES), :] = full.T

        each(0, ct.shape[1] // (TURNED * LANES), some)

    def forward(use, s, vecs):
        act(mt.at[use], vecs, done.at[s], 2)
        term[use, s] = placed(ohr[use], joined(done.at[s])).reshape(ncol, nbf, LANES)
        each_col(
            lambda i: send(
                term.at[use, s, i], rs.at[use, s, i - 1], rs_send.at[use, s], rs_recv.at[use, s], (d, r, back_col(i))
            )
        )

    def middle(use, s, field):
        await_bytes(rs.at[use, s], rs_recv.at[use, s])
        small[0] = stood_up_twice(field + term[use, s, 0] + total([rs[use, s, i] for i in range(ncol - 1)]))
        act(dt.at[use], small, small_out, 1)
        ag[use, s, 0] = laid_down_halves(small_out[0, : BLOCK // 2], nbf)
        each_col(
            lambda i: send(
                ag.at[use, s, 0], ag.at[use, s, i], ag_send.at[use, s], ag_recv.at[use, s], (d, r, at_col(i))
            )
        )

    def backward(use, s):
        await_bytes(ag.at[use, s, pl.ds(0, ncol - 1)], ag_recv.at[use, s])
        fill(work, picked(ag[use, s].reshape(ncol * nbf, LANES).T, ohr[use]))
        act_back(mt.at[use], work, done.at[s], 2)

    def face_out(use, s, own):
        here = lax.broadcasted_iota(jnp.int32, (nrow, LANES), 0) == r
        face[s] = placed(ohf[use], joined(done.at[s]))[:nrow] + jnp.where(here, ag[use, s, 0, own : own + 1], 0.0)

    def face_in(use, s, own, action, take):
        small[0] = stood_up(total([fx[take, s, i] for i in range(nrow)]))
        action(ct, small, small_out, 1)
        moved = small_out[0]
        taken = jnp.concatenate([moved, pltpu.roll(moved, LANES - nrow, 1)], axis=0)
        for t, part in enumerate(tiles(picked(taken, ohf[use]))):
            work[t] = xt[use, s, t] - part
        here = lax.broadcasted_iota(jnp.int32, (nrow, LANES), 0) == r
        mine = jnp.sum(jnp.where(here, laid_down(moved, nrow), 0.0), axis=0, keepdims=True)
        at_own = lax.broadcasted_iota(jnp.int32, (nbf, LANES), 0) == own
        return fields[use, s, 0] - jnp.where(at_own, mine, 0.0)

    def widen(use, s):
        wide[use, s] = placed(ohc[use], joined(done.at[s])).reshape(nrow, nbf, LANES)

    every = range(STREAMS)

    @pl.when(d == 0)
    def _():
        for s in every:
            forward(0, s, xt.at[0, s])
        index0[0, 0:1] = rows[...]
        index0[0, 1:2] = cols[...]
        send(index0.at[0], index0.at[1], early_send.at[0], early_recv.at[0], (1, r, c))
        send(diag, diag0, early_send.at[1], early_recv.at[1], (1, r, c))
        turn_diag(0, diag)
        for s in every:
            middle(0, s, fields[0, s, 0])
        for s in every:
            backward(0, s)
            face_out(0, s, nbf - 1)
            each_row(lambda i: send(face.at[s], fx.at[0, s, i], fx_send.at[0, s], fx_recv.at[0, s], (1, at_row(i), c)))
            send(face.at[s], fx.at[0, s, 0], fx_send.at[0, s], fx_recv.at[0, s], (1, r, c))
        send(xt.at[0], xt.at[1], late_send.at[0], late_recv.at[0], (1, r, c))
        send(fields.at[0, :, 0], fields.at[1, :, 0], late_send.at[1], late_recv.at[1], (1, r, c))
        for t in range(nz // LANES):
            send(mt.at[0, t], mt.at[1, t], late_send.at[2 + t], late_recv.at[2 + t], (1, r, c))
        for s in every:
            await_bytes(fin.at[s], fin_recv.at[s])
            out[:, pl.ds(s * LANES, LANES)] = total([fin[s, i] for i in range(nrow)])
        for s in every:
            await_bytes(fx.at[0, s], fx_send.at[0, s])
        pltpu.make_async_copy(index0.at[0], index0.at[0], early_send.at[0]).wait()
        await_bytes(diag, early_send.at[1])
        await_bytes(xt.at[0], late_send.at[0])
        await_bytes(fields.at[0, :, 0], late_send.at[1])
        for t in range(nz // LANES):
            await_bytes(mt.at[0, t], late_send.at[2 + t])

    @pl.when(d == 1)
    def _():
        await_bytes(cbuf.at[pl.ds(0, nrow - 1)], c_recv)
        turn_couple()
        turn_diag(0, diag)
        await_bytes(index0.at[1], early_recv.at[0])
        tables(1, index0[1, 0:1], index0[1, 1:2], nbf - 1)
        await_bytes(diag0, early_recv.at[1])
        turn_diag(1, diag0)
        held = []
        for s in every:
            await_bytes(fx.at[0, s], fx_recv.at[0, s])
            held.append(face_in(0, s, 0, act, 0))
            forward(0, s, work)
        for s in every:
            middle(0, s, held[s])
        for s in every:
            backward(0, s)
            face_out(0, s, 0)
            each_row(lambda i: send(face.at[s], fx.at[1, s, i], fx_send.at[1, s], fx_recv.at[1, s], (1, at_row(i), c)))
            fx[1, s, 0] = face[s]
        for s in every:
            widen(0, s)
            each_row(
                lambda i: send(
                    wide.at[0, s, i], fin.at[s, i], fin_send.at[0, s], fin_recv.at[s], (1, at_row(nrow - i), c)
                )
            )
        await_bytes(xt.at[1], late_recv.at[0])
        await_bytes(fields.at[1, :, 0], late_recv.at[1])
        for t in range(nz // LANES):
            await_bytes(mt.at[1, t], late_recv.at[2 + t])
        held = []
        for s in every:
            await_bytes(fx.at[1, s, pl.ds(0, nrow - 1)], fx_recv.at[1, s])
            held.append(face_in(1, s, nbf - 1, act_back, 1))
            forward(1, s, work)
        for s in every:
            await_bytes(fin.at[s, pl.ds(0, nrow - 1)], fin_recv.at[s])
            out[:, pl.ds(s * LANES, LANES)] = (
                ag[0, s, 0] + wide[0, s, 0] + total([fin[s, i] for i in range(1, nrow)])
            )
        for s in every:
            middle(1, s, held[s])
        for s in every:
            backward(1, s)
            widen(1, s)
            wide[1, s, 0] += ag[1, s, 0]
            each_row(
                lambda i: send(
                    wide.at[1, s, i], fin.at[s, i], fin_send.at[1, s], fin_recv.at[s], (0, at_row(nrow - i), c)
                )
            )
            send(wide.at[1, s, 0], fin.at[s, 0], fin_send.at[1, s], fin_recv.at[s], (0, r, c))
        await_bytes(cbuf.at[pl.ds(0, nrow - 1)], c_send)
        for s in every:
            await_bytes(fx.at[1, s, pl.ds(0, nrow - 1)], fx_send.at[1, s])
            await_bytes(wide.at[0, s, pl.ds(0, nrow - 1)], fin_send.at[0, s])
            await_bytes(wide.at[1, s], fin_send.at[1, s])
            await_bytes(term.at[1, s, pl.ds(0, ncol - 1)], rs_send.at[1, s])
            await_bytes(ag.at[1, s, pl.ds(0, ncol - 1)], ag_send.at[1, s])

    for s in every:
        await_bytes(fields.at[0, s, pl.ds(0, nrow - 1)], row_send.at[s])
        await_bytes(term.at[0, s, pl.ds(0, ncol - 1)], rs_send.at[0, s])
        await_bytes(ag.at[0, s, pl.ds(0, ncol - 1)], ag_send.at[0, s])


def per_device(nrow, ncol, rhs, factor_blocks, block_rows, block_cols, diag_inverse, coupling):
    nbf = rhs.shape[1]
    nz, size = factor_blocks.shape[-2:]
    vm = pl.BlockSpec(memory_space=pltpu.VMEM)
    dma = pltpu.SemaphoreType.DMA
    got = pl.pallas_call(
        functools.partial(kernel, nrow, ncol),
        out_shape=jax.ShapeDtypeStruct((nbf, rhs.shape[2]), F32),
        in_specs=[pl.BlockSpec(memory_space=pl.ANY)] * 6,
        out_specs=vm,
        scratch_shapes=[
            pltpu.VMEM((nbf, rhs.shape[2]), F32),
            pltpu.VMEM((1, nz), jnp.int32),
            pltpu.VMEM((1, nz), jnp.int32),
            pltpu.VMEM((nbf, size), F32),
            pltpu.VMEM((size // LANES, LANES), F32),
            pltpu.VMEM((size // LANES, nz, LANES), F32),
            pltpu.VMEM((2, nz // LANES, size, LANES), F32),
            pltpu.VMEM((2, nrow * nbf, nz), BF16),
            pltpu.VMEM((2, ncol * nbf, nz), BF16),
            pltpu.VMEM((2, LANES, nz), BF16),
            pltpu.VMEM((2, 1, size // 2, LANES), F32),
            pltpu.VMEM((1, size, LANES), F32),
            pltpu.VMEM((2, STREAMS, nrow, nbf, LANES), F32),
            pltpu.VMEM((2, STREAMS, nz // LANES, LANES, LANES), F32),
            pltpu.VMEM((nz // LANES, LANES, LANES), F32),
            pltpu.VMEM((STREAMS, nz // LANES, LANES, LANES), F32),
            pltpu.VMEM((1, BLOCK, LANES), F32),
            pltpu.VMEM((1, BLOCK, LANES), F32),
            pltpu.VMEM((2, STREAMS, ncol, nbf, LANES), F32),
            pltpu.VMEM((2, STREAMS, ncol - 1, nbf, LANES), F32),
            pltpu.VMEM((2, STREAMS, ncol, nbf, LANES), F32),
            pltpu.VMEM((STREAMS, nrow, LANES), F32),
            pltpu.VMEM((2, STREAMS, nrow, nrow, LANES), F32),
            pltpu.VMEM((2, STREAMS, nrow, nbf, LANES), F32),
            pltpu.VMEM((STREAMS, nrow, nbf, LANES), F32),
            pltpu.VMEM((nrow, size // LANES, LANES), F32),
            pltpu.VMEM((nbf, size), F32),
            pltpu.VMEM((2, 2, nz), jnp.int32),
            dma((size // LANES,)),
            dma((STREAMS,)), dma((STREAMS,)),
            dma((2, STREAMS)), dma((2, STREAMS)),
            dma((2, STREAMS)), dma((2, STREAMS)),
            dma((2, STREAMS)), dma((2, STREAMS)),
            dma((2, STREAMS)), dma((STREAMS,)),
            dma, dma,
            dma((2,)), dma((2,)),
            dma((2 + nz // LANES,)), dma((2 + nz // LANES,)),
            dma((5,)),
        ],
        compiler_params=pltpu.CompilerParams(
            collective_id=0, has_side_effects=True, vmem_limit_bytes=56 * 1024 * 1024
        ),
    )(
        rhs[0],
        factor_blocks.reshape(nz, size),
        block_rows.reshape(1, nz),
        block_cols.reshape(1, nz),
        diag_inverse[0],
        coupling.reshape(size // LANES, LANES),
    )
    return got[None]


def solution(mesh):
    placed_as = (
        P("depth", ("row", "col"), None),
        P("depth", "row", "col", None, None),
        P("depth", "row", "col", None),
        P("depth", "row", "col", None),
        P("depth", ("row", "col"), None),
        P("depth", ("row", "col"), None),
    )
    return jax.shard_map(
        functools.partial(per_device, mesh.shape["row"], mesh.shape["col"]),
        mesh=mesh,
        in_specs=placed_as,
        out_specs=P("depth", ("row", "col"), None),
        check_vma=False,
    )
```

```python
import functools
import math

import jax
import jax.numpy as jnp
from jax import lax
from jax.experimental import pallas as pl
from jax.experimental.pallas import tpu as pltpu
from jax.sharding import PartitionSpec as P

MESH = pl.DeviceIdType.MESH
F32 = jnp.float32
BF16 = jnp.bfloat16

BLOCK = 64
LANES = 128
STREAMS = 2
TURNED = 4


def halves(x):
    hi = x.astype(BF16)
    return hi, (x - hi.astype(F32)).astype(BF16)


def picked(x, table):
    n = x.shape[0]
    both = jnp.dot(jnp.concatenate(halves(x), axis=0), table, preferred_element_type=F32)
    return both[:n] + both[n:]


def placed(table, x):
    n = x.shape[0]
    dims = (((1,), (1,)), ((), ()))
    both = lax.dot_general(table, jnp.concatenate(halves(x), axis=0), dims, preferred_element_type=F32)
    return both[:, :n] + both[:, n:]


def column_sums(parts):
    at = lax.broadcasted_iota(jnp.int32, parts[0].shape, 0)
    low = at < 4
    four = [
        jnp.where(low, parts[s], parts[s + 4]) + pltpu.roll(jnp.where(low, parts[s + 4], parts[s]), 4, 0)
        for s in range(4)
    ]
    low = (at & 2) == 0
    two = [
        jnp.where(low, four[s], pltpu.roll(four[s + 2], 2, 0)) + jnp.where(low, pltpu.roll(four[s], 6, 0), four[s + 2])
        for s in range(2)
    ]
    low = (at & 1) == 0
    return jnp.where(low, two[0], pltpu.roll(two[1], 1, 0)) + jnp.where(low, pltpu.roll(two[0], 7, 0), two[1])


def total(terms):
    while len(terms) > 1:
        terms = [terms[i] + terms[i + 1] if i + 1 < len(terms) else terms[i] for i in range(0, len(terms), 2)]
    return terms[0]


def act(mats, vecs, outs, count):
    def tile(t, _):
        x = [[vecs[t, pl.ds(r * BLOCK + 8 * g, 8), :] for g in range(8)] for r in range(count)]

        def group(q, _):
            parts = [[] for _ in range(count)]
            for a in range(8):
                first = pl.multiple_of(q * (8 * BLOCK) + a * BLOCK, BLOCK)
                m = [mats[t, pl.ds(first + 8 * g, 8), :] for g in range(8)]
                for r in range(count):
                    parts[r].append(total([m[g] * x[r][g] for g in range(8)]))
            for r in range(count):
                outs[t, pl.ds(pl.multiple_of(r * BLOCK + 8 * q, 8), 8), :] = column_sums(parts[r])
            return 0

        return lax.fori_loop(0, mats.shape[1] // (8 * BLOCK), group, 0)

    lax.fori_loop(0, mats.shape[0], tile, 0)


def act_back(mats, vecs, outs, count):
    def tile(t, _):
        def group(q, sums):
            sums = list(sums)
            v = [vecs[t, pl.ds(pl.multiple_of(r * BLOCK + 8 * q, 8), 8), :] for r in range(count)]
            for a in range(8):
                first = pl.multiple_of(q * (8 * BLOCK) + a * BLOCK, BLOCK)
                z = [jnp.broadcast_to(v[r][a : a + 1], (8, LANES)) for r in range(count)]
                for g in range(8):
                    m = mats[t, pl.ds(first + 8 * g, 8), :]
                    for r in range(count):
                        sums[r * 8 + g] = sums[r * 8 + g] + m * z[r]
            return tuple(sums)

        zero = jnp.zeros((8, LANES), F32)
        sums = lax.fori_loop(0, 8, group, (zero,) * (8 * count))
        for r in range(count):
            for g in range(8):
                outs[t, pl.ds(r * BLOCK + 8 * g, 8), :] = sums[r * 8 + g]
        return 0

    lax.fori_loop(0, mats.shape[0], tile, 0)


def tiles(x):
    return [x[:, LANES * t : LANES * (t + 1)] for t in range(x.shape[1] // LANES)]


def joined(ref):
    return jnp.concatenate([ref[t] for t in range(ref.shape[0])], axis=1)


def stood_up(v):
    n = v.shape[0]
    both = jnp.concatenate([v, pltpu.roll(v, BLOCK, 1), jnp.zeros((LANES - 2 * n, LANES), F32)], axis=0)
    return both.T[:BLOCK]


def laid_down(v, n):
    flat = jnp.concatenate([v, v], axis=0).T
    lane = lax.broadcasted_iota(jnp.int32, (n, LANES), 1)
    return jnp.where(lane < BLOCK, flat[:n], flat[n : 2 * n])


def stood_up_twice(v):
    pair = [v, pltpu.roll(v, BLOCK, 1)]
    return jnp.concatenate(pair + pair, axis=0).T[:BLOCK]


def laid_down_halves(v, n):
    flat = jnp.concatenate([v] * 4, axis=0).T
    quarter = lax.broadcasted_iota(jnp.int32, (n, LANES), 1) // (BLOCK // 2)
    low = jnp.where(quarter == 0, flat[:n], flat[2 * n : 3 * n])
    high = jnp.where(quarter == 2, flat[n : 2 * n], flat[3 * n :])
    return jnp.where(quarter < 2, low, high)


def kernel(
    nrow, ncol, rhs_in, mats, rows_in, cols_in, diag_in, couple_in, out,
    rhs, rows, cols, diag, couple, raw, mt, ohc, ohr, ohf, dt, ct, fields, xt, work, done, small, small_out, term, rs, ag, face, fx, wide, fin, cbuf, diag0,
    index0, raw_sem, row_send, row_recv, rs_send, rs_recv, ag_send, ag_recv, fx_send, fx_recv, fin_send, fin_recv, c_send,
    c_recv, early_send, early_recv, late_send, late_recv, in_sem,
):
    nbf = rhs.shape[0]
    nz = rows.shape[1]
    side = math.isqrt(ncol)
    d, r, c = lax.axis_index("depth"), lax.axis_index("row"), lax.axis_index("col")
    cy, cx = lax.div(c, side), lax.rem(c, side)

    def at_row(i):
        return lax.rem(r + i, nrow)

    def at_col(i):
        return lax.rem(cy + lax.div(i, side), side) * side + lax.rem(cx + lax.rem(i, side), side)

    def back_col(i):
        return lax.rem(cy - lax.div(i, side) + side, side) * side + lax.rem(cx - lax.rem(i, side) + side, side)

    def far_row(j):
        return nrow // 2 + lax.div(j + 1, 2) * (1 - 2 * lax.rem(j, 2))

    def far_side(j):
        return lax.rem(side // 2 + lax.div(j * (j + 1), 2), side)

    def far_col(j):
        return far_side(lax.div(j, side)) * side + far_side(lax.rem(j, side))

    def send(src, dst, send_sem, recv_sem, where):
        pltpu.make_async_remote_copy(
            src_ref=src, dst_ref=dst, send_sem=send_sem, recv_sem=recv_sem, device_id=where, device_id_type=MESH
        ).start()

    def await_bytes(ref, sem):
        pltpu.make_async_copy(ref, ref, sem).wait()

    def each(low, high, body):
        def step(i, _):
            body(i)
            return 0

        lax.fori_loop(low, high, step, 0)

    def each_col(body):
        each(0, ncol - 1, lambda j: body(far_col(j)))

    def each_row(body):
        each(0, nrow - 1, lambda j: body(far_row(j)))

    barrier = pltpu.get_barrier_semaphore()

    def greet(where):
        pl.semaphore_signal(barrier, inc=1, device_id=where, device_id_type=MESH)

    each_row(lambda i: greet((d, at_row(i), c)))
    each_row(lambda i: greet((1 - d, at_row(i), c)))
    each_col(lambda i: greet((1 - d, r, at_col(i))))
    greet((1 - d, r, c))

    @pl.when(d == 1)
    def _():
        each_col(lambda i: greet((1, r, at_col(i))))


    pieces = raw.shape[0]

    def piece(j):
        lanes = pl.ds(pl.multiple_of(j * LANES, LANES), LANES)
        return pltpu.make_async_copy(mats.at[:, lanes], raw.at[j], raw_sem.at[j])

    inputs = [
        pltpu.make_async_copy(src, dst, in_sem.at[i])
        for i, (src, dst) in enumerate(
            ((rhs_in, rhs), (rows_in, rows), (cols_in, cols), (couple_in, couple), (diag_in, diag))
        )
    ]
    for copy in inputs:
        copy.start()
    each(0, pieces, lambda j: piece(j).start())
    for copy in inputs:
        copy.wait()
    pl.semaphore_wait(barrier, 2 * (nrow - 1) + ncol + (ncol - 1) * d)

    def share_field(s):
        part = pl.ds(s * LANES, LANES)
        fields[0, s, 0] = rhs[:, part]
        each_row(lambda i: send(rhs.at[:, part], fields.at[0, s, i], row_send.at[s], row_recv.at[s], (d, at_row(i), c)))

    @pl.when(d == 0)
    def _():
        for s in range(STREAMS):
            share_field(s)

    def tables(use, brow, bcol, own_face):
        oy, ox = (brow >> 5) // side, (brow >> 5) % side
        slot_row = ((cy - oy) & (side - 1)) * side + ((cx - ox) & (side - 1))
        slot_col = (r - (bcol >> 5)) & (nrow - 1)

        def table(position, count):
            return (lax.broadcasted_iota(jnp.int32, (count, nz), 0) == position).astype(BF16)

        ohr[use] = table((slot_row << 5) | (brow & 31), ncol * nbf)
        ohc[use] = table((slot_col << 5) | (bcol & 31), nrow * nbf)
        ohf[use] = table(jnp.where((bcol & 31) == own_face, bcol >> 5, -1), LANES)

    tables(0, rows[...], cols[...], jnp.where(d == 0, nbf - 1, 0))

    def turn(i):
        group = [i * TURNED + u for u in range(TURNED)]
        for j in group:
            piece(j).wait()
        for j in group:
            for t in range(nz // LANES):
                mt[0, t, pl.ds(pl.multiple_of(j * LANES, LANES), LANES), :] = raw[j, pl.ds(t * LANES, LANES), :].T

    each(0, pieces // TURNED, turn)

    def fill(ref, x):
        for t, part in enumerate(tiles(x)):
            ref[t] = part

    def gather_field(s):
        await_bytes(fields.at[0, s, pl.ds(0, nrow - 1)], row_recv.at[s])
        fill(xt.at[0, s], picked(fields[0, s].reshape(nrow * nbf, LANES).T, ohc[0]))

    def turn_diag(use, given):
        apart = given.shape[1] // (2 * LANES)

        def some(i):
            for u in range(TURNED):
                j = i * TURNED + u
                low, high = (given[:, pl.ds(pl.multiple_of(k * LANES, LANES), LANES)] for k in (j, j + apart))
                full = jnp.concatenate([low, low, high, high], axis=0)
                dt[use, 0, pl.ds(pl.multiple_of(j * LANES, LANES), LANES), :] = full.T

        each(0, apart // TURNED, some)

    def turn_couple():
        def some(i):
            for u in range(TURNED):
                j = i * TURNED + u
                two = cbuf[:, pl.ds(j, 1), :].reshape(nrow, LANES)
                full = jnp.concatenate([two, two, jnp.zeros((LANES - 2 * nrow, LANES), F32)], axis=0)
                ct[0, pl.ds(pl.multiple_of(j * LANES, LANES), LANES), :] = full.T

        each(0, ct.shape[1] // (TURNED * LANES), some)

    def forward(p, u, s, vecs):
        act(mt.at[p], vecs, done.at[s], 2)
        term[u, s] = placed(ohr[p], joined(done.at[s])).reshape(ncol, nbf, LANES)
        each_col(
            lambda i: send(term.at[u, s, i], rs.at[u, s, i], rs_send.at[u, s], rs_recv.at[u, s], (1, r, back_col(i)))
        )

    def middle(p, u, s, summed):
        small[0] = stood_up_twice(summed)
        act(dt.at[p], small, small_out, 1)
        ag[u, s, 0] = laid_down_halves(small_out[0, : BLOCK // 2], nbf)
        each_col(
            lambda i: send(ag.at[u, s, 0], ag.at[u, s, i], ag_send.at[u, s], ag_recv.at[u, s], (1, r, at_col(i)))
        )

    def own_sum(u, s, field):
        await_bytes(rs.at[u, s, pl.ds(0, ncol - 1)], rs_recv.at[u, s])
        return field + term[u, s, 0] + total([rs[u, s, i] for i in range(1, ncol)])

    def backward(p, u, s):
        await_bytes(ag.at[u, s, pl.ds(0, ncol - 1)], ag_recv.at[u, s])
        fill(work, picked(ag[u, s].reshape(ncol * nbf, LANES).T, ohr[p]))
        act_back(mt.at[p], work, done.at[s], 2)

    def face_out(p, u, s, own, take):
        here = lax.broadcasted_iota(jnp.int32, (nrow, LANES), 0) == r
        face[take, s] = placed(ohf[p], joined(done.at[s]))[:nrow] + jnp.where(here, ag[u, s, 0, own : own + 1], 0.0)
        each_row(
            lambda i: send(
                face.at[take, s], fx.at[take, s, i], fx_send.at[take, s], fx_recv.at[take, s], (1, at_row(i), c)
            )
        )
        fx[take, s, 0] = face[take, s]

    def face_in(p, s, own, action, take):
        await_bytes(fx.at[take, s, pl.ds(0, nrow - 1)], fx_recv.at[take, s])
        small[0] = stood_up(total([fx[take, s, i] for i in range(nrow)]))
        action(ct, small, small_out, 1)
        moved = small_out[0]
        taken = jnp.concatenate([moved, pltpu.roll(moved, LANES - nrow, 1)], axis=0)
        for t, part in enumerate(tiles(picked(taken, ohf[p]))):
            work[t] = xt[p, s, t] - part
        here = lax.broadcasted_iota(jnp.int32, (nrow, LANES), 0) == r
        mine = jnp.sum(jnp.where(here, laid_down(moved, nrow), 0.0), axis=0, keepdims=True)
        at_own = lax.broadcasted_iota(jnp.int32, (nbf, LANES), 0) == own
        return fields[p, s, 0] - jnp.where(at_own, mine, 0.0)

    def widen(p, s):
        wide[p, s] = placed(ohc[p], joined(done.at[s])).reshape(nrow, nbf, LANES)

    every = range(STREAMS)
    factor = range(nz // LANES)

    @pl.when(d == 0)
    def _():
        for t in factor[0:2]:
            send(mt.at[0, t], mt.at[1, t], late_send.at[2 + t], late_recv.at[2 + t], (1, r, c))
        gather_field(0)
        index0[0, 0:1] = rows[...]
        index0[0, 1:2] = cols[...]
        send(index0.at[0], index0.at[1], early_send.at[0], early_recv.at[0], (1, r, c))
        send(diag, diag0, early_send.at[1], early_recv.at[1], (1, r, c))
        send(fields.at[0, :, 0], fields.at[1, :, 0], late_send.at[1], late_recv.at[1], (1, r, c))
        for s in every:
            if s > 0:
                gather_field(s)
            forward(0, 2, s, xt.at[0, s])
            send(term.at[2, s, 0], rs.at[2, s, 0], rs_send.at[2, s], rs_recv.at[2, s], (1, r, c))
        for t in factor[2:4]:
            send(mt.at[0, t], mt.at[1, t], late_send.at[2 + t], late_recv.at[2 + t], (1, r, c))
        send(xt.at[0], xt.at[1], late_send.at[0], late_recv.at[0], (1, r, c))
        for s in every:
            await_bytes(fin.at[s], fin_recv.at[s])
            out[:, pl.ds(s * LANES, LANES)] = total([fin[s, i] for i in range(nrow)])
        pltpu.make_async_copy(index0.at[0], index0.at[0], early_send.at[0]).wait()
        await_bytes(diag, early_send.at[1])
        await_bytes(xt.at[0], late_send.at[0])
        await_bytes(fields.at[0, :, 0], late_send.at[1])
        for t in factor:
            await_bytes(mt.at[0, t], late_send.at[2 + t])
        for s in every:
            await_bytes(term.at[2, s], rs_send.at[2, s])

    @pl.when(d == 1)
    def _():
        await_bytes(index0.at[1], early_recv.at[0])
        for s in every:
            share_field(s)
        cbuf[pl.ds(r, 1)] = couple[...][None]
        each_row(lambda i: send(couple, cbuf.at[r], c_send, c_recv, (1, at_row(i), c)))
        tables(1, index0[1, 0:1], index0[1, 1:2], nbf - 1)
        await_bytes(diag0, early_recv.at[1])
        turn_diag(1, diag0)
        await_bytes(fields.at[1, :, 0], late_recv.at[1])
        for s in every:
            await_bytes(rs.at[2, s], rs_recv.at[2, s])
            middle(1, 2, s, fields[1, s, 0] + total([rs[2, s, i] for i in range(ncol)]))
        turn_diag(0, diag)
        for s in every:
            gather_field(s)
        await_bytes(cbuf.at[pl.ds(0, nrow - 1)], c_recv)
        turn_couple()
        for t in factor:
            await_bytes(mt.at[1, t], late_recv.at[2 + t])
        for s in every:
            backward(1, 2, s)
            face_out(1, 2, s, nbf - 1, 0)
        held = []
        for s in every:
            held.append(face_in(0, s, 0, act, 0))
            forward(0, 0, s, work)
        for s in every:
            middle(0, 0, s, own_sum(0, s, held[s]))
        for s in every:
            backward(0, 0, s)
            face_out(0, 0, s, 0, 1)
        for s in every:
            widen(0, s)
            each_row(
                lambda i: send(
                    wide.at[0, s, i], fin.at[s, i], fin_send.at[0, s], fin_recv.at[s], (1, at_row(nrow - i), c)
                )
            )
        await_bytes(xt.at[1], late_recv.at[0])
        held = []
        for s in every:
            held.append(face_in(1, s, nbf - 1, act_back, 1))
            forward(1, 1, s, work)
        for s in every:
            await_bytes(fin.at[s, pl.ds(0, nrow - 1)], fin_recv.at[s])
            out[:, pl.ds(s * LANES, LANES)] = (
                ag[0, s, 0] + wide[0, s, 0] + total([fin[s, i] for i in range(1, nrow)])
            )
        for s in every:
            middle(1, 1, s, own_sum(1, s, held[s]))
        for s in every:
            backward(1, 1, s)
            widen(1, s)
            wide[1, s, 0] += ag[1, s, 0]
            each_row(
                lambda i: send(
                    wide.at[1, s, i], fin.at[s, i], fin_send.at[1, s], fin_recv.at[s], (0, at_row(nrow - i), c)
                )
            )
            send(wide.at[1, s, 0], fin.at[s, 0], fin_send.at[1, s], fin_recv.at[s], (0, r, c))
        await_bytes(cbuf.at[pl.ds(0, nrow - 1)], c_send)
        for s in every:
            await_bytes(wide.at[0, s, pl.ds(0, nrow - 1)], fin_send.at[0, s])
            await_bytes(wide.at[1, s], fin_send.at[1, s])
            for take in range(2):
                await_bytes(fx.at[take, s, pl.ds(0, nrow - 1)], fx_send.at[take, s])
                await_bytes(term.at[take, s, pl.ds(0, ncol - 1)], rs_send.at[take, s])
            for u in range(3):
                await_bytes(ag.at[u, s, pl.ds(0, ncol - 1)], ag_send.at[u, s])

    for s in every:
        await_bytes(fields.at[0, s, pl.ds(0, nrow - 1)], row_send.at[s])


def per_device(nrow, ncol, rhs, factor_blocks, block_rows, block_cols, diag_inverse, coupling):
    nbf = rhs.shape[1]
    nz, size = factor_blocks.shape[-2:]
    vm = pl.BlockSpec(memory_space=pltpu.VMEM)
    dma = pltpu.SemaphoreType.DMA
    got = pl.pallas_call(
        functools.partial(kernel, nrow, ncol),
        out_shape=jax.ShapeDtypeStruct((nbf, rhs.shape[2]), F32),
        in_specs=[pl.BlockSpec(memory_space=pl.ANY)] * 6,
        out_specs=vm,
        scratch_shapes=[
            pltpu.VMEM((nbf, rhs.shape[2]), F32),
            pltpu.VMEM((1, nz), jnp.int32),
            pltpu.VMEM((1, nz), jnp.int32),
            pltpu.VMEM((nbf, size), F32),
            pltpu.VMEM((size // LANES, LANES), F32),
            pltpu.VMEM((size // LANES, nz, LANES), F32),
            pltpu.VMEM((2, nz // LANES, size, LANES), F32),
            pltpu.VMEM((2, nrow * nbf, nz), BF16),
            pltpu.VMEM((2, ncol * nbf, nz), BF16),
            pltpu.VMEM((2, LANES, nz), BF16),
            pltpu.VMEM((2, 1, size // 2, LANES), F32),
            pltpu.VMEM((1, size, LANES), F32),
            pltpu.VMEM((2, STREAMS, nrow, nbf, LANES), F32),
            pltpu.VMEM((2, STREAMS, nz // LANES, LANES, LANES), F32),
            pltpu.VMEM((nz // LANES, LANES, LANES), F32),
            pltpu.VMEM((STREAMS, nz // LANES, LANES, LANES), F32),
            pltpu.VMEM((1, BLOCK, LANES), F32),
            pltpu.VMEM((1, BLOCK, LANES), F32),
            pltpu.VMEM((3, STREAMS, ncol, nbf, LANES), F32),
            pltpu.VMEM((3, STREAMS, ncol, nbf, LANES), F32),
            pltpu.VMEM((3, STREAMS, ncol, nbf, LANES), F32),
            pltpu.VMEM((2, STREAMS, nrow, LANES), F32),
            pltpu.VMEM((2, STREAMS, nrow, nrow, LANES), F32),
            pltpu.VMEM((2, STREAMS, nrow, nbf, LANES), F32),
            pltpu.VMEM((STREAMS, nrow, nbf, LANES), F32),
            pltpu.VMEM((nrow, size // LANES, LANES), F32),
            pltpu.VMEM((nbf, size), F32),
            pltpu.VMEM((2, 2, nz), jnp.int32),
            dma((size // LANES,)),
            dma((STREAMS,)), dma((STREAMS,)),
            dma((3, STREAMS)), dma((3, STREAMS)),
            dma((3, STREAMS)), dma((3, STREAMS)),
            dma((2, STREAMS)), dma((2, STREAMS)),
            dma((2, STREAMS)), dma((STREAMS,)),
            dma, dma,
            dma((2,)), dma((2,)),
            dma((2 + nz // LANES,)), dma((2 + nz // LANES,)),
            dma((5,)),
        ],
        compiler_params=pltpu.CompilerParams(
            collective_id=0, has_side_effects=True, vmem_limit_bytes=56 * 1024 * 1024
        ),
    )(
        rhs[0],
        factor_blocks.reshape(nz, size),
        block_rows.reshape(1, nz),
        block_cols.reshape(1, nz),
        diag_inverse[0],
        coupling.reshape(size // LANES, LANES),
    )
    return got[None]


def solution(mesh):
    placed_as = (
        P("depth", ("row", "col"), None),
        P("depth", "row", "col", None, None),
        P("depth", "row", "col", None),
        P("depth", "row", "col", None),
        P("depth", ("row", "col"), None),
        P("depth", ("row", "col"), None),
    )
    return jax.shard_map(
        functools.partial(per_device, mesh.shape["row"], mesh.shape["col"]),
        mesh=mesh,
        in_specs=placed_as,
        out_specs=P("depth", ("row", "col"), None),
        check_vma=False,
    )
```

```python
import functools
import math

import jax
import jax.numpy as jnp
from jax import lax
from jax.experimental import pallas as pl
from jax.experimental.pallas import tpu as pltpu
from jax.sharding import PartitionSpec as P

MESH = pl.DeviceIdType.MESH
F32 = jnp.float32
BF16 = jnp.bfloat16

BLOCK = 64
LANES = 128
STREAMS = 2
TURNED = 4


def halves(x):
    hi = x.astype(BF16)
    return hi, (x - hi.astype(F32)).astype(BF16)


def picked(x, table):
    n = x.shape[0]
    both = jnp.dot(jnp.concatenate(halves(x), axis=0), table, preferred_element_type=F32)
    return both[:n] + both[n:]


def placed(table, x):
    n = x.shape[0]
    dims = (((1,), (1,)), ((), ()))
    both = lax.dot_general(table, jnp.concatenate(halves(x), axis=0), dims, preferred_element_type=F32)
    return both[:, :n] + both[:, n:]


def total(terms):
    while len(terms) > 1:
        terms = [terms[i] + terms[i + 1] if i + 1 < len(terms) else terms[i] for i in range(0, len(terms), 2)]
    return terms[0]


def act(mats, vecs, outs, count, parts):
    def tile(t, _):
        x = [[vecs[t, pl.ds(r * BLOCK + 8 * g, 8), :] for g in range(8)] for r in range(count)]

        def group(q, _):
            for a in range(8):
                first = pl.multiple_of(q * (8 * BLOCK) + a * BLOCK, BLOCK)
                m = [mats[t, pl.ds(first + 8 * g, 8), :] for g in range(8)]
                for r in range(count):
                    parts[r, pl.ds(8 * a, 8), :] = total([m[g] * x[r][g] for g in range(8)])
            for r in range(count):
                rows = total([parts[r, pl.ds(i, 8, stride=8), :] for i in range(8)])
                outs[t, pl.ds(pl.multiple_of(r * BLOCK + 8 * q, 8), 8), :] = rows
            return 0

        return lax.fori_loop(0, mats.shape[1] // (8 * BLOCK), group, 0)

    lax.fori_loop(0, mats.shape[0], tile, 0)


def act_back(mats, vecs, outs, count):
    def tile(t, _):
        def group(q, sums):
            sums = list(sums)
            v = [vecs[t, pl.ds(pl.multiple_of(r * BLOCK + 8 * q, 8), 8), :] for r in range(count)]
            for a in range(8):
                first = pl.multiple_of(q * (8 * BLOCK) + a * BLOCK, BLOCK)
                z = [jnp.broadcast_to(v[r][a : a + 1], (8, LANES)) for r in range(count)]
                for g in range(8):
                    m = mats[t, pl.ds(first + 8 * g, 8), :]
                    for r in range(count):
                        sums[r * 8 + g] = sums[r * 8 + g] + m * z[r]
            return tuple(sums)

        zero = jnp.zeros((8, LANES), F32)
        sums = lax.fori_loop(0, mats.shape[1] // (8 * BLOCK), group, (zero,) * (8 * count))
        for r in range(count):
            for g in range(8):
                outs[t, pl.ds(r * BLOCK + 8 * g, 8), :] = sums[r * 8 + g]
        return 0

    lax.fori_loop(0, mats.shape[0], tile, 0)


def tiles(x):
    return [x[:, LANES * t : LANES * (t + 1)] for t in range(x.shape[1] // LANES)]


def joined(ref):
    return jnp.concatenate([ref[t] for t in range(ref.shape[0])], axis=1)


def stood_up(v):
    n = v.shape[0]
    eighths = [v, pltpu.roll(v, BLOCK, 1)] * 8
    if 16 * n < LANES:
        eighths.append(jnp.zeros((LANES - 16 * n, LANES), F32))
    return jnp.concatenate(eighths, axis=0).T[:BLOCK]


def couple_on(ct, small, small_out, parts, x, n):
    small[0] = x
    act(ct, small, small_out, 1, parts)
    o = small_out[0, :8]
    return jnp.concatenate([o] + [pltpu.roll(o, LANES - 2 * n * i, 1) for i in range(1, 8)], axis=0)


def couple_back(ct, small, small_out, parts, z, n):
    eighth = lax.broadcasted_iota(jnp.int32, (8, LANES), 1) // (2 * n)
    small[0, :8] = total([jnp.where(eighth == i, z[8 * i : 8 * i + 8], 0.0) for i in range(8)])
    act_back(ct, small, small_out, 1)
    o = small_out[0]
    for i in (4, 2, 1):
        o = o + pltpu.roll(o, LANES - 2 * n * i, 1)
    return o


def laid_down(v, n):
    flat = jnp.concatenate([v, v], axis=0).T
    lane = lax.broadcasted_iota(jnp.int32, (n, LANES), 1)
    return jnp.where(lane < BLOCK, flat[:n], flat[n : 2 * n])


def stood_up_twice(v):
    pair = [v, pltpu.roll(v, BLOCK, 1)]
    return jnp.concatenate(pair + pair, axis=0).T[:BLOCK]


def laid_down_halves(v, n):
    flat = jnp.concatenate([v] * 4, axis=0).T
    quarter = lax.broadcasted_iota(jnp.int32, (n, LANES), 1) // (BLOCK // 2)
    low = jnp.where(quarter == 0, flat[:n], flat[2 * n : 3 * n])
    high = jnp.where(quarter == 2, flat[n : 2 * n], flat[3 * n :])
    return jnp.where(quarter < 2, low, high)


def kernel(
    nrow, ncol, rhs_in, mats, rows_in, cols_in, diag_in, couple_in, out,
    rhs, rows, cols, diag, couple, raw, mt, ohc, ohr, ohf, dt, ct, fields, xt, work, done, small, small_out, parts, term, rs, ag, face, fx, wide, fin, cbuf, diag0,
    index0, raw_sem, row_send, row_recv, rs_send, rs_recv, ag_send, ag_recv, fx_send, fx_recv, fin_send, fin_recv, c_send,
    c_recv, early_send, early_recv, late_send, late_recv, in_sem,
):
    nbf = rhs.shape[0]
    nz = rows.shape[1]
    side = math.isqrt(ncol)
    d, r, c = lax.axis_index("depth"), lax.axis_index("row"), lax.axis_index("col")
    cy, cx = lax.div(c, side), lax.rem(c, side)

    def at_row(i):
        return lax.rem(r + i, nrow)

    def at_col(i):
        return lax.rem(cy + i // side, side) * side + lax.rem(cx + i % side, side)

    def back_col(i):
        return lax.rem(cy - i // side + side, side) * side + lax.rem(cx - i % side + side, side)

    rows_away = sorted(range(1, nrow), key=lambda i: -min(i, nrow - i))
    cols_away = sorted(
        range(1, ncol), key=lambda i: -min(i // side, side - i // side) - min(i % side, side - i % side)
    )

    def send(src, dst, send_sem, recv_sem, where):
        pltpu.make_async_remote_copy(
            src_ref=src, dst_ref=dst, send_sem=send_sem, recv_sem=recv_sem, device_id=where, device_id_type=MESH
        ).start()

    def await_bytes(ref, sem):
        pltpu.make_async_copy(ref, ref, sem).wait()

    def each(low, high, body):
        def step(i, _):
            body(i)
            return 0

        lax.fori_loop(low, high, step, 0)

    def each_col(body):
        for i in cols_away:
            body(i)

    def each_row(body):
        for i in rows_away:
            body(i)

    barrier = pltpu.get_barrier_semaphore()

    def greet(where):
        pl.semaphore_signal(barrier, inc=1, device_id=where, device_id_type=MESH)

    each_row(lambda i: greet((d, at_row(i), c)))
    each_row(lambda i: greet((1 - d, at_row(i), c)))
    each_col(lambda i: greet((1 - d, r, at_col(i))))
    greet((1 - d, r, c))

    @pl.when(d == 1)
    def _():
        each_col(lambda i: greet((1, r, at_col(i))))


    pieces = raw.shape[0]

    def piece(j):
        lanes = pl.ds(pl.multiple_of(j * LANES, LANES), LANES)
        return pltpu.make_async_copy(mats.at[:, lanes], raw.at[j], raw_sem.at[j])

    inputs = [
        pltpu.make_async_copy(src, dst, in_sem.at[i])
        for i, (src, dst) in enumerate(
            ((rhs_in, rhs), (rows_in, rows), (cols_in, cols), (couple_in, couple), (diag_in, diag))
        )
    ]
    for copy in inputs:
        copy.start()
    each(0, pieces, lambda j: piece(j).start())
    for copy in inputs:
        copy.wait()
    pl.semaphore_wait(barrier, 2 * (nrow - 1) + ncol + (ncol - 1) * d)

    def share_field(s):
        part = pl.ds(s * LANES, LANES)
        fields[0, s, 0] = rhs[:, part]
        each_row(lambda i: send(rhs.at[:, part], fields.at[0, s, i], row_send.at[s], row_recv.at[s], (d, at_row(i), c)))

    @pl.when(d == 0)
    def _():
        for s in range(STREAMS):
            share_field(s)

    def tables(use, brow, bcol, own_face):
        oy, ox = (brow >> 5) // side, (brow >> 5) % side
        slot_row = ((cy - oy) & (side - 1)) * side + ((cx - ox) & (side - 1))
        slot_col = (r - (bcol >> 5)) & (nrow - 1)

        def table(position, count):
            return (lax.broadcasted_iota(jnp.int32, (count, nz), 0) == position).astype(BF16)

        ohr[use] = table((slot_row << 5) | (brow & 31), ncol * nbf)
        ohc[use] = table((slot_col << 5) | (bcol & 31), nrow * nbf)
        ohf[use] = table(jnp.where((bcol & 31) == own_face, bcol >> 5, -1), LANES)

    tables(0, rows[...], cols[...], jnp.where(d == 0, nbf - 1, 0))

    def turn(i):
        group = [i * TURNED + u for u in range(TURNED)]
        for j in group:
            piece(j).wait()
        for j in group:
            for t in range(nz // LANES):
                mt[0, t, pl.ds(pl.multiple_of(j * LANES, LANES), LANES), :] = raw[j, pl.ds(t * LANES, LANES), :].T

    each(0, pieces // TURNED, turn)

    def fill(ref, x):
        for t, part in enumerate(tiles(x)):
            ref[t] = part

    def gather_field(s):
        await_bytes(fields.at[0, s, pl.ds(0, nrow - 1)], row_recv.at[s])
        fill(xt.at[0, s], picked(fields[0, s].reshape(nrow * nbf, LANES).T, ohc[0]))

    def turn_diag(use, given):
        apart = given.shape[1] // (2 * LANES)

        def some(i):
            for u in range(TURNED):
                j = i * TURNED + u
                low, high = (given[:, pl.ds(pl.multiple_of(k * LANES, LANES), LANES)] for k in (j, j + apart))
                full = jnp.concatenate([low, low, high, high], axis=0)
                dt[use, 0, pl.ds(pl.multiple_of(j * LANES, LANES), LANES), :] = full.T

        each(0, apart // TURNED, some)

    def turn_couple():
        apart = ct.shape[1] // LANES
        for j in range(apart):
            lots = []
            for i in range(8):
                two = cbuf[:, pl.ds(i * apart + j, 1), :].reshape(nrow, LANES)
                lots += [two, two]
            if 16 * nrow < LANES:
                lots.append(jnp.zeros((LANES - 16 * nrow, LANES), F32))
            ct[0, pl.ds(j * LANES, LANES), :] = jnp.concatenate(lots, axis=0).T

    def forward(p, u, s, vecs):
        act(mt.at[p], vecs, done.at[s], 2, parts)
        term[u, s] = placed(ohr[p], joined(done.at[s])).reshape(ncol, nbf, LANES)
        each_col(
            lambda i: send(term.at[u, s, i], rs.at[u, s, i], rs_send.at[u, s], rs_recv.at[u, s], (1, r, back_col(i)))
        )

    def middle(p, u, s, summed):
        small[0] = stood_up_twice(summed)
        act(dt.at[p], small, small_out, 1, parts)
        ag[u, s, 0] = laid_down_halves(small_out[0, : BLOCK // 2], nbf)
        each_col(
            lambda i: send(ag.at[u, s, 0], ag.at[u, s, i], ag_send.at[u, s], ag_recv.at[u, s], (1, r, at_col(i)))
        )

    def own_sum(u, s, field):
        await_bytes(rs.at[u, s, pl.ds(0, ncol - 1)], rs_recv.at[u, s])
        return field + term[u, s, 0] + total([rs[u, s, i] for i in range(1, ncol)])

    def backward(p, u, s):
        await_bytes(ag.at[u, s, pl.ds(0, ncol - 1)], ag_recv.at[u, s])
        fill(work, picked(ag[u, s].reshape(ncol * nbf, LANES).T, ohr[p]))
        act_back(mt.at[p], work, done.at[s], 2)

    def face_out(p, u, s, own, take):
        here = lax.broadcasted_iota(jnp.int32, (nrow, LANES), 0) == r
        face[take, s] = placed(ohf[p, :16], joined(done.at[s]))[:nrow] + jnp.where(here, ag[u, s, 0, own : own + 1], 0.0)
        each_row(
            lambda i: send(
                face.at[take, s], fx.at[take, s, i], fx_send.at[take, s], fx_recv.at[take, s], (1, at_row(i), c)
            )
        )
        fx[take, s, 0] = face[take, s]

    def face_in(p, s, own, action, take):
        await_bytes(fx.at[take, s, pl.ds(0, nrow - 1)], fx_recv.at[take, s])
        moved = action(ct, small, small_out, parts, stood_up(total([fx[take, s, i] for i in range(nrow)])), nrow)
        taken = jnp.concatenate([moved, pltpu.roll(moved, LANES - nrow, 1)], axis=0)
        for t, part in enumerate(tiles(picked(taken, ohf[p]))):
            work[t] = xt[p, s, t] - part
        here = lax.broadcasted_iota(jnp.int32, (nrow, LANES), 0) == r
        mine = jnp.sum(jnp.where(here, laid_down(moved, nrow), 0.0), axis=0, keepdims=True)
        at_own = lax.broadcasted_iota(jnp.int32, (nbf, LANES), 0) == own
        return fields[p, s, 0] - jnp.where(at_own, mine, 0.0)

    def widen(p, s):
        wide[p, s] = placed(ohc[p], joined(done.at[s])).reshape(nrow, nbf, LANES)

    every = range(STREAMS)
    factor = range(nz // LANES)

    @pl.when(d == 0)
    def _():
        for t in factor[0:2]:
            send(mt.at[0, t], mt.at[1, t], late_send.at[2 + t], late_recv.at[2 + t], (1, r, c))
        gather_field(0)
        index0[0, 0:1] = rows[...]
        index0[0, 1:2] = cols[...]
        send(index0.at[0], index0.at[1], early_send.at[0], early_recv.at[0], (1, r, c))
        send(diag, diag0, early_send.at[1], early_recv.at[1], (1, r, c))
        send(fields.at[0, :, 0], fields.at[1, :, 0], late_send.at[1], late_recv.at[1], (1, r, c))
        for s in every:
            if s > 0:
                gather_field(s)
            forward(0, 2, s, xt.at[0, s])
            send(term.at[2, s, 0], rs.at[2, s, 0], rs_send.at[2, s], rs_recv.at[2, s], (1, r, c))
        for t in factor[2:4]:
            send(mt.at[0, t], mt.at[1, t], late_send.at[2 + t], late_recv.at[2 + t], (1, r, c))
        send(xt.at[0], xt.at[1], late_send.at[0], late_recv.at[0], (1, r, c))
        for s in every:
            await_bytes(fin.at[s], fin_recv.at[s])
            out[:, pl.ds(s * LANES, LANES)] = total([fin[s, i] for i in range(nrow)])
        pltpu.make_async_copy(index0.at[0], index0.at[0], early_send.at[0]).wait()
        await_bytes(diag, early_send.at[1])
        await_bytes(xt.at[0], late_send.at[0])
        await_bytes(fields.at[0, :, 0], late_send.at[1])
        for t in factor:
            await_bytes(mt.at[0, t], late_send.at[2 + t])
        for s in every:
            await_bytes(term.at[2, s], rs_send.at[2, s])

    @pl.when(d == 1)
    def _():
        await_bytes(index0.at[1], early_recv.at[0])
        for s in every:
            share_field(s)
        cbuf[pl.ds(r, 1)] = couple[...][None]
        each_row(lambda i: send(couple, cbuf.at[r], c_send, c_recv, (1, at_row(i), c)))
        tables(1, index0[1, 0:1], index0[1, 1:2], nbf - 1)
        await_bytes(diag0, early_recv.at[1])
        turn_diag(1, diag0)
        await_bytes(fields.at[1, :, 0], late_recv.at[1])
        for s in every:
            await_bytes(rs.at[2, s], rs_recv.at[2, s])
            middle(1, 2, s, fields[1, s, 0] + total([rs[2, s, i] for i in range(ncol)]))
        turn_diag(0, diag)
        for s in every:
            gather_field(s)
        await_bytes(cbuf.at[pl.ds(0, nrow - 1)], c_recv)
        turn_couple()
        for t in factor:
            await_bytes(mt.at[1, t], late_recv.at[2 + t])
        for s in every:
            backward(1, 2, s)
            face_out(1, 2, s, nbf - 1, 0)
        held = []
        for s in every:
            held.append(face_in(0, s, 0, couple_on, 0))
            forward(0, 0, s, work)
        for s in every:
            middle(0, 0, s, own_sum(0, s, held[s]))
        for s in every:
            backward(0, 0, s)
            face_out(0, 0, s, 0, 1)
        for s in every:
            widen(0, s)
            each_row(
                lambda i: send(
                    wide.at[0, s, i], fin.at[s, i], fin_send.at[0, s], fin_recv.at[s], (1, at_row(nrow - i), c)
                )
            )
        await_bytes(xt.at[1], late_recv.at[0])
        held = []
        for s in every:
            held.append(face_in(1, s, nbf - 1, couple_back, 1))
            forward(1, 1, s, work)
        for s in every:
            await_bytes(fin.at[s, pl.ds(0, nrow - 1)], fin_recv.at[s])
            out[:, pl.ds(s * LANES, LANES)] = (
                ag[0, s, 0] + wide[0, s, 0] + total([fin[s, i] for i in range(1, nrow)])
            )
        for s in every:
            middle(1, 1, s, own_sum(1, s, held[s]))
        for s in every:
            backward(1, 1, s)
            widen(1, s)
            wide[1, s, 0] += ag[1, s, 0]
            each_row(
                lambda i: send(
                    wide.at[1, s, i], fin.at[s, i], fin_send.at[1, s], fin_recv.at[s], (0, at_row(nrow - i), c)
                )
            )
            send(wide.at[1, s, 0], fin.at[s, 0], fin_send.at[1, s], fin_recv.at[s], (0, r, c))
        await_bytes(cbuf.at[pl.ds(0, nrow - 1)], c_send)
        for s in every:
            await_bytes(wide.at[0, s, pl.ds(0, nrow - 1)], fin_send.at[0, s])
            await_bytes(wide.at[1, s], fin_send.at[1, s])
            for take in range(2):
                await_bytes(fx.at[take, s, pl.ds(0, nrow - 1)], fx_send.at[take, s])
                await_bytes(term.at[take, s, pl.ds(0, ncol - 1)], rs_send.at[take, s])
            for u in range(3):
                await_bytes(ag.at[u, s, pl.ds(0, ncol - 1)], ag_send.at[u, s])

    for s in every:
        await_bytes(fields.at[0, s, pl.ds(0, nrow - 1)], row_send.at[s])


def per_device(nrow, ncol, rhs, factor_blocks, block_rows, block_cols, diag_inverse, coupling):
    nbf = rhs.shape[1]
    nz, size = factor_blocks.shape[-2:]
    vm = pl.BlockSpec(memory_space=pltpu.VMEM)
    dma = pltpu.SemaphoreType.DMA
    got = pl.pallas_call(
        functools.partial(kernel, nrow, ncol),
        out_shape=jax.ShapeDtypeStruct((nbf, rhs.shape[2]), F32),
        in_specs=[pl.BlockSpec(memory_space=pl.ANY)] * 6,
        out_specs=vm,
        scratch_shapes=[
            pltpu.VMEM((nbf, rhs.shape[2]), F32),
            pltpu.VMEM((1, nz), jnp.int32),
            pltpu.VMEM((1, nz), jnp.int32),
            pltpu.VMEM((nbf, size), F32),
            pltpu.VMEM((size // LANES, LANES), F32),
            pltpu.VMEM((size // LANES, nz, LANES), F32),
            pltpu.VMEM((2, nz // LANES, size, LANES), F32),
            pltpu.VMEM((2, nrow * nbf, nz), BF16),
            pltpu.VMEM((2, ncol * nbf, nz), BF16),
            pltpu.VMEM((2, LANES, nz), BF16),
            pltpu.VMEM((2, 1, size // 2, LANES), F32),
            pltpu.VMEM((1, size // 8, LANES), F32),
            pltpu.VMEM((2, STREAMS, nrow, nbf, LANES), F32),
            pltpu.VMEM((2, STREAMS, nz // LANES, LANES, LANES), F32),
            pltpu.VMEM((nz // LANES, LANES, LANES), F32),
            pltpu.VMEM((STREAMS, nz // LANES, LANES, LANES), F32),
            pltpu.VMEM((1, BLOCK, LANES), F32),
            pltpu.VMEM((1, BLOCK, LANES), F32),
            pltpu.VMEM((2, BLOCK, LANES), F32),
            pltpu.VMEM((3, STREAMS, ncol, nbf, LANES), F32),
            pltpu.VMEM((3, STREAMS, ncol, nbf, LANES), F32),
            pltpu.VMEM((3, STREAMS, ncol, nbf, LANES), F32),
            pltpu.VMEM((2, STREAMS, nrow, LANES), F32),
            pltpu.VMEM((2, STREAMS, nrow, nrow, LANES), F32),
            pltpu.VMEM((2, STREAMS, nrow, nbf, LANES), F32),
            pltpu.VMEM((STREAMS, nrow, nbf, LANES), F32),
            pltpu.VMEM((nrow, size // LANES, LANES), F32),
            pltpu.VMEM((nbf, size), F32),
            pltpu.VMEM((2, 2, nz), jnp.int32),
            dma((size // LANES,)),
            dma((STREAMS,)), dma((STREAMS,)),
            dma((3, STREAMS)), dma((3, STREAMS)),
            dma((3, STREAMS)), dma((3, STREAMS)),
            dma((2, STREAMS)), dma((2, STREAMS)),
            dma((2, STREAMS)), dma((STREAMS,)),
            dma, dma,
            dma((2,)), dma((2,)),
            dma((2 + nz // LANES,)), dma((2 + nz // LANES,)),
            dma((5,)),
        ],
        compiler_params=pltpu.CompilerParams(
            collective_id=0, has_side_effects=True, vmem_limit_bytes=56 * 1024 * 1024
        ),
    )(
        rhs[0],
        factor_blocks.reshape(nz, size),
        block_rows.reshape(1, nz),
        block_cols.reshape(1, nz),
        diag_inverse[0],
        coupling.reshape(size // LANES, LANES),
    )
    return got[None]


def solution(mesh):
    placed_as = (
        P("depth", ("row", "col"), None),
        P("depth", "row", "col", None, None),
        P("depth", "row", "col", None),
        P("depth", "row", "col", None),
        P("depth", ("row", "col"), None),
        P("depth", ("row", "col"), None),
    )
    return jax.shard_map(
        functools.partial(per_device, mesh.shape["row"], mesh.shape["col"]),
        mesh=mesh,
        in_specs=placed_as,
        out_specs=P("depth", ("row", "col"), None),
        check_vma=False,
    )
```

```python
import functools
import math

import jax
import jax.numpy as jnp
from jax import lax
from jax.experimental import pallas as pl
from jax.experimental.pallas import tpu as pltpu
from jax.sharding import PartitionSpec as P

MESH = pl.DeviceIdType.MESH
F32 = jnp.float32
BF16 = jnp.bfloat16

BLOCK = 64
LANES = 128
STREAMS = 2
TURNED = 4


def halves(x):
    hi = x.astype(BF16)
    return hi, (x - hi.astype(F32)).astype(BF16)


def picked(x, table):
    n = x.shape[0]
    both = jnp.dot(jnp.concatenate(halves(x), axis=0), table, preferred_element_type=F32)
    return both[:n] + both[n:]


def placed(table, x):
    n = x.shape[0]
    dims = (((1,), (1,)), ((), ()))
    both = lax.dot_general(table, jnp.concatenate(halves(x), axis=0), dims, preferred_element_type=F32)
    return both[:, :n] + both[:, n:]


def total(terms):
    while len(terms) > 1:
        terms = [terms[i] + terms[i + 1] if i + 1 < len(terms) else terms[i] for i in range(0, len(terms), 2)]
    return terms[0]


def act(mats, vecs, outs, count, parts):
    def tile(t, _):
        x = [[vecs[t, pl.ds(r * BLOCK + 8 * g, 8), :] for g in range(8)] for r in range(count)]

        def group(q, _):
            for a in range(8):
                first = pl.multiple_of(q * (8 * BLOCK) + a * BLOCK, BLOCK)
                m = [mats[t, pl.ds(first + 8 * g, 8), :] for g in range(8)]
                for r in range(count):
                    parts[r, pl.ds(8 * a, 8), :] = total([m[g] * x[r][g] for g in range(8)])
            for r in range(count):
                rows = total([parts[r, pl.ds(i, 8, stride=8), :] for i in range(8)])
                outs[t, pl.ds(pl.multiple_of(r * BLOCK + 8 * q, 8), 8), :] = rows
            return 0

        return lax.fori_loop(0, mats.shape[1] // (8 * BLOCK), group, 0)

    lax.fori_loop(0, mats.shape[0], tile, 0)


def act_back(mats, vecs, outs, count):
    def tile(t, _):
        def group(q, sums):
            sums = list(sums)
            v = [vecs[t, pl.ds(pl.multiple_of(r * BLOCK + 8 * q, 8), 8), :] for r in range(count)]
            for a in range(8):
                first = pl.multiple_of(q * (8 * BLOCK) + a * BLOCK, BLOCK)
                z = [jnp.broadcast_to(v[r][a : a + 1], (8, LANES)) for r in range(count)]
                for g in range(8):
                    m = mats[t, pl.ds(first + 8 * g, 8), :]
                    for r in range(count):
                        sums[r * 8 + g] = sums[r * 8 + g] + m * z[r]
            return tuple(sums)

        zero = jnp.zeros((8, LANES), F32)
        sums = lax.fori_loop(0, mats.shape[1] // (8 * BLOCK), group, (zero,) * (8 * count))
        for r in range(count):
            for g in range(8):
                outs[t, pl.ds(r * BLOCK + 8 * g, 8), :] = sums[r * 8 + g]
        return 0

    lax.fori_loop(0, mats.shape[0], tile, 0)


def tiles(x):
    return [x[:, LANES * t : LANES * (t + 1)] for t in range(x.shape[1] // LANES)]


def joined(ref):
    return jnp.concatenate([ref[t] for t in range(ref.shape[0])], axis=1)


def stood_up(v):
    n = v.shape[0]
    eighths = [v, pltpu.roll(v, BLOCK, 1)] * 8
    if 16 * n < LANES:
        eighths.append(jnp.zeros((LANES - 16 * n, LANES), F32))
    return jnp.concatenate(eighths, axis=0).T[:BLOCK]


def couple_on(ct, small, small_out, parts, x, n):
    small[0] = x
    act(ct, small, small_out, 1, parts)
    o = small_out[0, :8]
    return jnp.concatenate([o] + [pltpu.roll(o, LANES - 2 * n * i, 1) for i in range(1, 8)], axis=0)


def couple_back(ct, small, small_out, parts, z, n):
    eighth = lax.broadcasted_iota(jnp.int32, (8, LANES), 1) // (2 * n)
    small[0, :8] = total([jnp.where(eighth == i, z[8 * i : 8 * i + 8], 0.0) for i in range(8)])
    act_back(ct, small, small_out, 1)
    o = small_out[0]
    for i in (4, 2, 1):
        o = o + pltpu.roll(o, LANES - 2 * n * i, 1)
    return o


def laid_down(v, n):
    flat = jnp.concatenate([v, v], axis=0).T
    lane = lax.broadcasted_iota(jnp.int32, (n, LANES), 1)
    return jnp.where(lane < BLOCK, flat[:n], flat[n : 2 * n])


def stood_up_twice(v):
    pair = [v, pltpu.roll(v, BLOCK, 1)]
    return jnp.concatenate(pair + pair, axis=0).T[:BLOCK]


def laid_down_halves(v, n):
    flat = jnp.concatenate([v] * 4, axis=0).T
    quarter = lax.broadcasted_iota(jnp.int32, (n, LANES), 1) // (BLOCK // 2)
    low = jnp.where(quarter == 0, flat[:n], flat[2 * n : 3 * n])
    high = jnp.where(quarter == 2, flat[n : 2 * n], flat[3 * n :])
    return jnp.where(quarter < 2, low, high)


def kernel(
    nrow, ncol, rhs_in, mats, rows_in, cols_in, diag_in, couple_in, out,
    rhs, rows, cols, diag, couple, raw, mt, ohc, ohr, ohf, dt, ct, fields, xt, work, done, small, small_out, parts, term, rs, ag, face, fx, wide, fin, cbuf, diag0,
    index0, raw_sem, row_send, row_recv, rs_send, rs_recv, ag_send, ag_recv, fx_send, fx_recv, fin_send, fin_recv, c_send,
    c_recv, early_send, early_recv, late_send, late_recv, in_sem,
):
    nbf = rhs.shape[0]
    nz = rows.shape[1]
    side = math.isqrt(ncol)
    d, r, c = lax.axis_index("depth"), lax.axis_index("row"), lax.axis_index("col")
    cy, cx = lax.div(c, side), lax.rem(c, side)

    def at_row(i):
        return lax.rem(r + i, nrow)

    def at_col(i):
        return lax.rem(cy + i // side, side) * side + lax.rem(cx + i % side, side)

    def back_col(i):
        return lax.rem(cy - i // side + side, side) * side + lax.rem(cx - i % side + side, side)

    rows_away = sorted(range(1, nrow), key=lambda i: -min(i, nrow - i))
    cols_away = sorted(
        range(1, ncol), key=lambda i: -min(i // side, side - i // side) - min(i % side, side - i % side)
    )

    near = ncol // 2

    def send(src, dst, send_sem, recv_sem, where):
        pltpu.make_async_remote_copy(
            src_ref=src, dst_ref=dst, send_sem=send_sem, recv_sem=recv_sem, device_id=where, device_id_type=MESH
        ).start()

    def await_bytes(ref, sem):
        pltpu.make_async_copy(ref, ref, sem).wait()

    def each(low, high, body):
        def step(i, _):
            body(i)
            return 0

        lax.fori_loop(low, high, step, 0)

    def each_col(body):
        for i in cols_away:
            body(i)

    def each_row(body):
        for i in rows_away:
            body(i)

    barrier = pltpu.get_barrier_semaphore()

    def greet(where):
        pl.semaphore_signal(barrier, inc=1, device_id=where, device_id_type=MESH)

    each_row(lambda i: greet((d, at_row(i), c)))
    each_row(lambda i: greet((1 - d, at_row(i), c)))
    each_col(lambda i: greet((1 - d, r, at_col(i))))
    greet((1 - d, r, c))

    @pl.when(d == 1)
    def _():
        each_col(lambda i: greet((1, r, at_col(i))))


    pieces = raw.shape[0]

    def piece(j):
        lanes = pl.ds(pl.multiple_of(j * LANES, LANES), LANES)
        return pltpu.make_async_copy(mats.at[:, lanes], raw.at[j], raw_sem.at[j])

    inputs = [
        pltpu.make_async_copy(src, dst, in_sem.at[i])
        for i, (src, dst) in enumerate(
            ((rhs_in, rhs), (rows_in, rows), (cols_in, cols), (couple_in, couple), (diag_in, diag))
        )
    ]
    for copy in inputs:
        copy.start()
    each(0, pieces, lambda j: piece(j).start())
    for copy in inputs:
        copy.wait()
    pl.semaphore_wait(barrier, 2 * (nrow - 1) + ncol + (ncol - 1) * d)

    def share_field(s):
        part = pl.ds(s * LANES, LANES)
        fields[0, s, 0] = rhs[:, part]
        each_row(lambda i: send(rhs.at[:, part], fields.at[0, s, i], row_send.at[s], row_recv.at[s], (d, at_row(i), c)))

    @pl.when(d == 0)
    def _():
        for s in range(STREAMS):
            share_field(s)

    def tables(use, brow, bcol, own_face):
        oy, ox = (brow >> 5) // side, (brow >> 5) % side
        slot_row = ((cy - oy) & (side - 1)) * side + ((cx - ox) & (side - 1))
        slot_col = (r - (bcol >> 5)) & (nrow - 1)

        def table(position, count):
            return (lax.broadcasted_iota(jnp.int32, (count, nz), 0) == position).astype(BF16)

        ohr[use] = table((slot_row << 5) | (brow & 31), ncol * nbf)
        ohc[use] = table((slot_col << 5) | (bcol & 31), nrow * nbf)
        ohf[use] = table(jnp.where((bcol & 31) == own_face, bcol >> 5, -1), LANES)

    tables(0, rows[...], cols[...], jnp.where(d == 0, nbf - 1, 0))

    def turn(i):
        group = [i * TURNED + u for u in range(TURNED)]
        for j in group:
            piece(j).wait()
        for j in group:
            for t in range(nz // LANES):
                mt[0, t, pl.ds(pl.multiple_of(j * LANES, LANES), LANES), :] = raw[j, pl.ds(t * LANES, LANES), :].T

    each(0, pieces // TURNED, turn)

    def fill(ref, x):
        for t, part in enumerate(tiles(x)):
            ref[t] = part

    def gather_field(s):
        await_bytes(fields.at[0, s, pl.ds(0, nrow - 1)], row_recv.at[s])
        fill(xt.at[0, s], picked(fields[0, s].reshape(nrow * nbf, LANES).T, ohc[0]))

    def turn_diag(use, given):
        apart = given.shape[1] // (2 * LANES)

        def some(i):
            for u in range(TURNED):
                j = i * TURNED + u
                low, high = (given[:, pl.ds(pl.multiple_of(k * LANES, LANES), LANES)] for k in (j, j + apart))
                full = jnp.concatenate([low, low, high, high], axis=0)
                dt[use, 0, pl.ds(pl.multiple_of(j * LANES, LANES), LANES), :] = full.T

        each(0, apart // TURNED, some)

    def turn_couple():
        apart = ct.shape[1] // LANES
        for j in range(apart):
            lots = []
            for i in range(8):
                two = cbuf[:, pl.ds(i * apart + j, 1), :].reshape(nrow, LANES)
                lots += [two, two]
            if 16 * nrow < LANES:
                lots.append(jnp.zeros((LANES - 16 * nrow, LANES), F32))
            ct[0, pl.ds(j * LANES, LANES), :] = jnp.concatenate(lots, axis=0).T

    def forward(p, u, s, vecs):
        act(mt.at[p], vecs, done.at[s], 2, parts)
        both = joined(done.at[s])
        for first in (near, 0):
            part = placed(ohr[p, first * nbf : (first + near) * nbf], both)
            term[u, s, first : first + near] = part.reshape(near, nbf, LANES)
            for i in cols_away:
                if first <= i < first + near:
                    send(term.at[u, s, i], rs.at[u, s, i], rs_send.at[u, s], rs_recv.at[u, s], (1, r, back_col(i)))

    def middle(p, u, s, summed):
        small[0] = stood_up_twice(summed)
        act(dt.at[p], small, small_out, 1, parts)
        ag[u, s, 0] = laid_down_halves(small_out[0, : BLOCK // 2], nbf)
        each_col(
            lambda i: send(ag.at[u, s, 0], ag.at[u, s, i], ag_send.at[u, s], ag_recv.at[u, s], (1, r, at_col(i)))
        )

    def own_sum(u, s, field):
        await_bytes(rs.at[u, s, pl.ds(0, ncol - 1)], rs_recv.at[u, s])
        return field + term[u, s, 0] + total([rs[u, s, i] for i in range(1, ncol)])

    def backward(p, u, s):
        await_bytes(ag.at[u, s, pl.ds(0, ncol - 1)], ag_recv.at[u, s])
        fill(work, picked(ag[u, s].reshape(ncol * nbf, LANES).T, ohr[p]))
        act_back(mt.at[p], work, done.at[s], 2)

    def face_out(p, u, s, own, take):
        here = lax.broadcasted_iota(jnp.int32, (nrow, LANES), 0) == r
        face[take, s] = placed(ohf[p, :16], joined(done.at[s]))[:nrow] + jnp.where(here, ag[u, s, 0, own : own + 1], 0.0)
        each_row(
            lambda i: send(
                face.at[take, s], fx.at[take, s, i], fx_send.at[take, s], fx_recv.at[take, s], (1, at_row(i), c)
            )
        )
        fx[take, s, 0] = face[take, s]

    def face_in(p, s, own, action, take):
        await_bytes(fx.at[take, s, pl.ds(0, nrow - 1)], fx_recv.at[take, s])
        moved = action(ct, small, small_out, parts, stood_up(total([fx[take, s, i] for i in range(nrow)])), nrow)
        taken = jnp.concatenate([moved, pltpu.roll(moved, LANES - nrow, 1)], axis=0)
        for t, part in enumerate(tiles(picked(taken, ohf[p]))):
            work[t] = xt[p, s, t] - part
        here = lax.broadcasted_iota(jnp.int32, (nrow, LANES), 0) == r
        mine = jnp.sum(jnp.where(here, laid_down(moved, nrow), 0.0), axis=0, keepdims=True)
        at_own = lax.broadcasted_iota(jnp.int32, (nbf, LANES), 0) == own
        return fields[p, s, 0] - jnp.where(at_own, mine, 0.0)

    def widen(p, s):
        wide[p, s] = placed(ohc[p], joined(done.at[s])).reshape(nrow, nbf, LANES)

    every = range(STREAMS)
    factor = range(nz // LANES)

    @pl.when(d == 0)
    def _():
        for t in factor[0:2]:
            send(mt.at[0, t], mt.at[1, t], late_send.at[2 + t], late_recv.at[2 + t], (1, r, c))
        gather_field(0)
        index0[0, 0:1] = rows[...]
        index0[0, 1:2] = cols[...]
        send(index0.at[0], index0.at[1], early_send.at[0], early_recv.at[0], (1, r, c))
        send(diag, diag0, early_send.at[1], early_recv.at[1], (1, r, c))
        send(fields.at[0, :, 0], fields.at[1, :, 0], late_send.at[1], late_recv.at[1], (1, r, c))
        for s in every:
            if s > 0:
                gather_field(s)
            forward(0, 2, s, xt.at[0, s])
            send(term.at[2, s, 0], rs.at[2, s, 0], rs_send.at[2, s], rs_recv.at[2, s], (1, r, c))
        for t in factor[2:4]:
            send(mt.at[0, t], mt.at[1, t], late_send.at[2 + t], late_recv.at[2 + t], (1, r, c))
        send(xt.at[0], xt.at[1], late_send.at[0], late_recv.at[0], (1, r, c))
        for s in every:
            await_bytes(fin.at[s], fin_recv.at[s])
            out[:, pl.ds(s * LANES, LANES)] = total([fin[s, i] for i in range(nrow)])
        pltpu.make_async_copy(index0.at[0], index0.at[0], early_send.at[0]).wait()
        await_bytes(diag, early_send.at[1])
        await_bytes(xt.at[0], late_send.at[0])
        await_bytes(fields.at[0, :, 0], late_send.at[1])
        for t in factor:
            await_bytes(mt.at[0, t], late_send.at[2 + t])
        for s in every:
            await_bytes(term.at[2, s], rs_send.at[2, s])

    @pl.when(d == 1)
    def _():
        await_bytes(index0.at[1], early_recv.at[0])
        for s in every:
            share_field(s)
        cbuf[pl.ds(r, 1)] = couple[...][None]
        each_row(lambda i: send(couple, cbuf.at[r], c_send, c_recv, (1, at_row(i), c)))
        tables(1, index0[1, 0:1], index0[1, 1:2], nbf - 1)
        await_bytes(diag0, early_recv.at[1])
        turn_diag(1, diag0)
        await_bytes(fields.at[1, :, 0], late_recv.at[1])
        for s in every:
            await_bytes(rs.at[2, s], rs_recv.at[2, s])
            middle(1, 2, s, fields[1, s, 0] + total([rs[2, s, i] for i in range(ncol)]))
        turn_diag(0, diag)
        for s in every:
            gather_field(s)
        await_bytes(cbuf.at[pl.ds(0, nrow - 1)], c_recv)
        turn_couple()
        for t in factor:
            await_bytes(mt.at[1, t], late_recv.at[2 + t])
        for s in every:
            backward(1, 2, s)
            face_out(1, 2, s, nbf - 1, 0)
        held = []
        for s in every:
            held.append(face_in(0, s, 0, couple_on, 0))
            forward(0, 0, s, work)
        for s in every:
            middle(0, 0, s, own_sum(0, s, held[s]))
        for s in every:
            backward(0, 0, s)
            face_out(0, 0, s, 0, 1)
        for s in every:
            widen(0, s)
            each_row(
                lambda i: send(
                    wide.at[0, s, i], fin.at[s, i], fin_send.at[0, s], fin_recv.at[s], (1, at_row(nrow - i), c)
                )
            )
        await_bytes(xt.at[1], late_recv.at[0])
        held = []
        for s in every:
            held.append(face_in(1, s, nbf - 1, couple_back, 1))
            forward(1, 1, s, work)
        for s in every:
            await_bytes(fin.at[s, pl.ds(0, nrow - 1)], fin_recv.at[s])
            out[:, pl.ds(s * LANES, LANES)] = (
                ag[0, s, 0] + wide[0, s, 0] + total([fin[s, i] for i in range(1, nrow)])
            )
        for s in every:
            middle(1, 1, s, own_sum(1, s, held[s]))
        for s in every:
            backward(1, 1, s)
            widen(1, s)
            wide[1, s, 0] += ag[1, s, 0]
            each_row(
                lambda i: send(
                    wide.at[1, s, i], fin.at[s, i], fin_send.at[1, s], fin_recv.at[s], (0, at_row(nrow - i), c)
                )
            )
            send(wide.at[1, s, 0], fin.at[s, 0], fin_send.at[1, s], fin_recv.at[s], (0, r, c))
        await_bytes(cbuf.at[pl.ds(0, nrow - 1)], c_send)
        for s in every:
            await_bytes(wide.at[0, s, pl.ds(0, nrow - 1)], fin_send.at[0, s])
            await_bytes(wide.at[1, s], fin_send.at[1, s])
            for take in range(2):
                await_bytes(fx.at[take, s, pl.ds(0, nrow - 1)], fx_send.at[take, s])
                await_bytes(term.at[take, s, pl.ds(0, ncol - 1)], rs_send.at[take, s])
            for u in range(3):
                await_bytes(ag.at[u, s, pl.ds(0, ncol - 1)], ag_send.at[u, s])

    for s in every:
        await_bytes(fields.at[0, s, pl.ds(0, nrow - 1)], row_send.at[s])


def per_device(nrow, ncol, rhs, factor_blocks, block_rows, block_cols, diag_inverse, coupling):
    nbf = rhs.shape[1]
    nz, size = factor_blocks.shape[-2:]
    vm = pl.BlockSpec(memory_space=pltpu.VMEM)
    dma = pltpu.SemaphoreType.DMA
    got = pl.pallas_call(
        functools.partial(kernel, nrow, ncol),
        out_shape=jax.ShapeDtypeStruct((nbf, rhs.shape[2]), F32),
        in_specs=[pl.BlockSpec(memory_space=pl.ANY)] * 6,
        out_specs=vm,
        scratch_shapes=[
            pltpu.VMEM((nbf, rhs.shape[2]), F32),
            pltpu.VMEM((1, nz), jnp.int32),
            pltpu.VMEM((1, nz), jnp.int32),
            pltpu.VMEM((nbf, size), F32),
            pltpu.VMEM((size // LANES, LANES), F32),
            pltpu.VMEM((size // LANES, nz, LANES), F32),
            pltpu.VMEM((2, nz // LANES, size, LANES), F32),
            pltpu.VMEM((2, nrow * nbf, nz), BF16),
            pltpu.VMEM((2, ncol * nbf, nz), BF16),
            pltpu.VMEM((2, LANES, nz), BF16),
            pltpu.VMEM((2, 1, size // 2, LANES), F32),
            pltpu.VMEM((1, size // 8, LANES), F32),
            pltpu.VMEM((2, STREAMS, nrow, nbf, LANES), F32),
            pltpu.VMEM((2, STREAMS, nz // LANES, LANES, LANES), F32),
            pltpu.VMEM((nz // LANES, LANES, LANES), F32),
            pltpu.VMEM((STREAMS, nz // LANES, LANES, LANES), F32),
            pltpu.VMEM((1, BLOCK, LANES), F32),
            pltpu.VMEM((1, BLOCK, LANES), F32),
            pltpu.VMEM((2, BLOCK, LANES), F32),
            pltpu.VMEM((3, STREAMS, ncol, nbf, LANES), F32),
            pltpu.VMEM((3, STREAMS, ncol, nbf, LANES), F32),
            pltpu.VMEM((3, STREAMS, ncol, nbf, LANES), F32),
            pltpu.VMEM((2, STREAMS, nrow, LANES), F32),
            pltpu.VMEM((2, STREAMS, nrow, nrow, LANES), F32),
            pltpu.VMEM((2, STREAMS, nrow, nbf, LANES), F32),
            pltpu.VMEM((STREAMS, nrow, nbf, LANES), F32),
            pltpu.VMEM((nrow, size // LANES, LANES), F32),
            pltpu.VMEM((nbf, size), F32),
            pltpu.VMEM((2, 2, nz), jnp.int32),
            dma((size // LANES,)),
            dma((STREAMS,)), dma((STREAMS,)),
            dma((3, STREAMS)), dma((3, STREAMS)),
            dma((3, STREAMS)), dma((3, STREAMS)),
            dma((2, STREAMS)), dma((2, STREAMS)),
            dma((2, STREAMS)), dma((STREAMS,)),
            dma, dma,
            dma((2,)), dma((2,)),
            dma((2 + nz // LANES,)), dma((2 + nz // LANES,)),
            dma((5,)),
        ],
        compiler_params=pltpu.CompilerParams(
            collective_id=0, has_side_effects=True, vmem_limit_bytes=56 * 1024 * 1024
        ),
    )(
        rhs[0],
        factor_blocks.reshape(nz, size),
        block_rows.reshape(1, nz),
        block_cols.reshape(1, nz),
        diag_inverse[0],
        coupling.reshape(size // LANES, LANES),
    )
    return got[None]


def solution(mesh):
    placed_as = (
        P("depth", ("row", "col"), None),
        P("depth", "row", "col", None, None),
        P("depth", "row", "col", None),
        P("depth", "row", "col", None),
        P("depth", ("row", "col"), None),
        P("depth", ("row", "col"), None),
    )
    return jax.shard_map(
        functools.partial(per_device, mesh.shape["row"], mesh.shape["col"]),
        mesh=mesh,
        in_specs=placed_as,
        out_specs=P("depth", ("row", "col"), None),
        check_vma=False,
    )
```

```python
import functools
import math

import jax
import jax.numpy as jnp
from jax import lax
from jax.experimental import pallas as pl
from jax.experimental.pallas import tpu as pltpu
from jax.sharding import PartitionSpec as P

MESH = pl.DeviceIdType.MESH
F32 = jnp.float32
BF16 = jnp.bfloat16

BLOCK = 64
LANES = 128
STREAMS = 2
TURNED = 4


def halves(x):
    hi = x.astype(BF16)
    return hi, (x - hi.astype(F32)).astype(BF16)


def picked(x, table):
    n = x.shape[0]
    both = jnp.dot(jnp.concatenate(halves(x), axis=0), table, preferred_element_type=F32)
    return both[:n] + both[n:]


def placed(table, x):
    n = x.shape[0]
    dims = (((1,), (1,)), ((), ()))
    both = lax.dot_general(table, jnp.concatenate(halves(x), axis=0), dims, preferred_element_type=F32)
    return both[:, :n] + both[:, n:]


def total(terms):
    while len(terms) > 1:
        terms = [terms[i] + terms[i + 1] if i + 1 < len(terms) else terms[i] for i in range(0, len(terms), 2)]
    return terms[0]


def act(mats, vecs, outs, count, parts):
    def tile(t, _):
        x = [[vecs[t, pl.ds(r * BLOCK + 8 * g, 8), :] for g in range(8)] for r in range(count)]

        def group(q, _):
            for a in range(8):
                first = pl.multiple_of(q * (8 * BLOCK) + a * BLOCK, BLOCK)
                m = [mats[t, pl.ds(first + 8 * g, 8), :] for g in range(8)]
                for r in range(count):
                    parts[r, pl.ds(8 * a, 8), :] = total([m[g] * x[r][g] for g in range(8)])
            for r in range(count):
                rows = total([parts[r, pl.ds(i, 8, stride=8), :] for i in range(8)])
                outs[t, pl.ds(pl.multiple_of(r * BLOCK + 8 * q, 8), 8), :] = rows
            return 0

        return lax.fori_loop(0, mats.shape[1] // (8 * BLOCK), group, 0)

    lax.fori_loop(0, mats.shape[0], tile, 0)


def act_back(mats, vecs, outs, count):
    def tile(t, _):
        def group(q, sums):
            sums = list(sums)
            v = [vecs[t, pl.ds(pl.multiple_of(r * BLOCK + 8 * q, 8), 8), :] for r in range(count)]
            for a in range(8):
                first = pl.multiple_of(q * (8 * BLOCK) + a * BLOCK, BLOCK)
                z = [jnp.broadcast_to(v[r][a : a + 1], (8, LANES)) for r in range(count)]
                for g in range(8):
                    m = mats[t, pl.ds(first + 8 * g, 8), :]
                    for r in range(count):
                        sums[r * 8 + g] = sums[r * 8 + g] + m * z[r]
            return tuple(sums)

        zero = jnp.zeros((8, LANES), F32)
        sums = lax.fori_loop(0, mats.shape[1] // (8 * BLOCK), group, (zero,) * (8 * count))
        for r in range(count):
            for g in range(8):
                outs[t, pl.ds(r * BLOCK + 8 * g, 8), :] = sums[r * 8 + g]
        return 0

    lax.fori_loop(0, mats.shape[0], tile, 0)


def tiles(x):
    return [x[:, LANES * t : LANES * (t + 1)] for t in range(x.shape[1] // LANES)]


def joined(ref):
    return jnp.concatenate([ref[t] for t in range(ref.shape[0])], axis=1)


def stood_up(v):
    n = v.shape[0]
    eighths = [v, pltpu.roll(v, BLOCK, 1)] * 8
    if 16 * n < LANES:
        eighths.append(jnp.zeros((LANES - 16 * n, LANES), F32))
    return jnp.concatenate(eighths, axis=0).T[:BLOCK]


def couple_on(ct, small, small_out, parts, x, n):
    small[0] = x
    act(ct, small, small_out, 1, parts)
    o = small_out[0, :8]
    return jnp.concatenate([o] + [pltpu.roll(o, LANES - 2 * n * i, 1) for i in range(1, 8)], axis=0)


def couple_back(ct, small, small_out, parts, z, n):
    eighth = lax.broadcasted_iota(jnp.int32, (8, LANES), 1) // (2 * n)
    small[0, :8] = total([jnp.where(eighth == i, z[8 * i : 8 * i + 8], 0.0) for i in range(8)])
    act_back(ct, small, small_out, 1)
    o = small_out[0]
    for i in (4, 2, 1):
        o = o + pltpu.roll(o, LANES - 2 * n * i, 1)
    return o


def laid_down(v, n):
    flat = jnp.concatenate([v, v], axis=0).T
    lane = lax.broadcasted_iota(jnp.int32, (n, LANES), 1)
    return jnp.where(lane < BLOCK, flat[:n], flat[n : 2 * n])


def stood_up_twice(v):
    pair = [v, pltpu.roll(v, BLOCK, 1)]
    return jnp.concatenate(pair + pair, axis=0).T[:BLOCK]


def laid_down_halves(v, n):
    flat = jnp.concatenate([v] * 4, axis=0).T
    quarter = lax.broadcasted_iota(jnp.int32, (n, LANES), 1) // (BLOCK // 2)
    low = jnp.where(quarter == 0, flat[:n], flat[2 * n : 3 * n])
    high = jnp.where(quarter == 2, flat[n : 2 * n], flat[3 * n :])
    return jnp.where(quarter < 2, low, high)


def kernel(
    nrow, ncol, rhs_in, mats, rows_in, cols_in, diag_in, couple_in, out,
    rhs, rows, cols, diag, couple, raw, mt, ohc, ohr, ohf, dt, ct, fields, xt, work, done, small, small_out, parts, term, rs, ag, face, fx, wide, fin, cbuf, diag0,
    index0, raw_sem, row_send, row_recv, rs_send, rs_recv, ag_send, ag_recv, fx_send, fx_recv, fin_send, fin_recv, c_send,
    c_recv, early_send, early_recv, late_send, late_recv, in_sem,
):
    nbf = rhs.shape[0]
    nz = rows.shape[1]
    side = math.isqrt(ncol)
    d, r, c = lax.axis_index("depth"), lax.axis_index("row"), lax.axis_index("col")
    cy, cx = lax.div(c, side), lax.rem(c, side)

    def at_row(i):
        return lax.rem(r + i, nrow)

    def at_col(i):
        return lax.rem(cy + i // side, side) * side + lax.rem(cx + i % side, side)

    def back_col(i):
        return lax.rem(cy - i // side + side, side) * side + lax.rem(cx - i % side + side, side)

    rows_away = sorted(range(1, nrow), key=lambda i: -min(i, nrow - i))
    cols_away = sorted(
        range(1, ncol), key=lambda i: -min(i // side, side - i // side) - min(i % side, side - i % side)
    )

    near = ncol // 2

    def send(src, dst, send_sem, recv_sem, where):
        pltpu.make_async_remote_copy(
            src_ref=src, dst_ref=dst, send_sem=send_sem, recv_sem=recv_sem, device_id=where, device_id_type=MESH
        ).start()

    def await_bytes(ref, sem):
        pltpu.make_async_copy(ref, ref, sem).wait()

    def each(low, high, body):
        def step(i, _):
            body(i)
            return 0

        lax.fori_loop(low, high, step, 0)

    def each_col(body):
        for i in cols_away:
            body(i)

    def each_row(body):
        for i in rows_away:
            body(i)

    barrier = pltpu.get_barrier_semaphore()

    def greet(where):
        pl.semaphore_signal(barrier, inc=1, device_id=where, device_id_type=MESH)

    each_row(lambda i: greet((d, at_row(i), c)))
    each_row(lambda i: greet((1 - d, at_row(i), c)))
    each_col(lambda i: greet((1 - d, r, at_col(i))))
    greet((1 - d, r, c))

    @pl.when(d == 1)
    def _():
        each_col(lambda i: greet((1, r, at_col(i))))


    pieces = raw.shape[0]

    def piece(j):
        lanes = pl.ds(pl.multiple_of(j * LANES, LANES), LANES)
        return pltpu.make_async_copy(mats.at[:, lanes], raw.at[j], raw_sem.at[j])

    inputs = [
        pltpu.make_async_copy(src, dst, in_sem.at[i])
        for i, (src, dst) in enumerate(
            ((rhs_in, rhs), (rows_in, rows), (cols_in, cols), (couple_in, couple), (diag_in, diag))
        )
    ]
    for copy in inputs:
        copy.start()
    each(0, pieces, lambda j: piece(j).start())
    for copy in inputs:
        copy.wait()
    pl.semaphore_wait(barrier, 2 * (nrow - 1) + ncol + (ncol - 1) * d)

    def share_field(s):
        part = pl.ds(s * LANES, LANES)
        fields[0, s, 0] = rhs[:, part]
        each_row(lambda i: send(rhs.at[:, part], fields.at[0, s, i], row_send.at[s], row_recv.at[s], (d, at_row(i), c)))

    @pl.when(d == 0)
    def _():
        for s in range(STREAMS):
            share_field(s)

    def tables(use, brow, bcol, own_face):
        oy, ox = (brow >> 5) // side, (brow >> 5) % side
        slot_row = ((cy - oy) & (side - 1)) * side + ((cx - ox) & (side - 1))
        slot_col = (r - (bcol >> 5)) & (nrow - 1)

        def table(position, count):
            return (lax.broadcasted_iota(jnp.int32, (count, nz), 0) == position).astype(BF16)

        ohr[use] = table((slot_row << 5) | (brow & 31), ncol * nbf)
        ohc[use] = table((slot_col << 5) | (bcol & 31), nrow * nbf)
        ohf[use] = table(jnp.where((bcol & 31) == own_face, bcol >> 5, -1), LANES)

    tables(0, rows[...], cols[...], jnp.where(d == 0, nbf - 1, 0))

    def turn(i):
        group = [i * TURNED + u for u in range(TURNED)]
        for j in group:
            piece(j).wait()
        for j in group:
            for t in range(nz // LANES):
                mt[0, t, pl.ds(pl.multiple_of(j * LANES, LANES), LANES), :] = raw[j, pl.ds(t * LANES, LANES), :].T

    each(0, pieces // TURNED, turn)

    def fill(ref, x):
        for t, part in enumerate(tiles(x)):
            ref[t] = part

    def gather_field(s):
        await_bytes(fields.at[0, s, pl.ds(0, nrow - 1)], row_recv.at[s])
        fill(xt.at[0, s], picked(fields[0, s].reshape(nrow * nbf, LANES).T, ohc[0]))

    def turn_diag(use, given):
        apart = given.shape[1] // (2 * LANES)

        def some(i):
            for u in range(TURNED):
                j = i * TURNED + u
                low, high = (given[:, pl.ds(pl.multiple_of(k * LANES, LANES), LANES)] for k in (j, j + apart))
                full = jnp.concatenate([low, low, high, high], axis=0)
                dt[use, 0, pl.ds(pl.multiple_of(j * LANES, LANES), LANES), :] = full.T

        each(0, apart // TURNED, some)

    def turn_couple():
        apart = ct.shape[1] // LANES
        for j in range(apart):
            lots = []
            for i in range(8):
                two = cbuf[:, pl.ds(i * apart + j, 1), :].reshape(nrow, LANES)
                lots += [two, two]
            if 16 * nrow < LANES:
                lots.append(jnp.zeros((LANES - 16 * nrow, LANES), F32))
            ct[0, pl.ds(j * LANES, LANES), :] = jnp.concatenate(lots, axis=0).T

    def forward(p, u, s, vecs):
        act(mt.at[p], vecs, done.at[s], 2, parts)
        both = joined(done.at[s])
        for first in (near, 0):
            part = placed(ohr[p, first * nbf : (first + near) * nbf], both)
            term[u, s, first : first + near] = part.reshape(near, nbf, LANES)
            for i in cols_away:
                if first <= i < first + near:
                    send(term.at[u, s, i], rs.at[u, s, i], rs_send.at[u, s], rs_recv.at[u, s], (1, r, back_col(i)))

    def middle(p, u, s, summed):
        small[0] = stood_up_twice(summed)
        act(dt.at[p], small, small_out, 1, parts)
        ag[u, s, 0] = laid_down_halves(small_out[0, : BLOCK // 2], nbf)
        each_col(
            lambda i: send(ag.at[u, s, 0], ag.at[u, s, i], ag_send.at[u, s], ag_recv.at[u, s], (1, r, at_col(i)))
        )

    def own_sum(u, s, field):
        await_bytes(rs.at[u, s, pl.ds(0, ncol - 1)], rs_recv.at[u, s])
        return field + term[u, s, 0] + total([rs[u, s, i] for i in range(1, ncol)])

    def backward(p, u, s):
        await_bytes(ag.at[u, s, pl.ds(0, ncol - 1)], ag_recv.at[u, s])
        fill(work, picked(ag[u, s].reshape(ncol * nbf, LANES).T, ohr[p]))
        act_back(mt.at[p], work, done.at[s], 2)

    def face_out(p, u, s, own, take):
        here = lax.broadcasted_iota(jnp.int32, (nrow, LANES), 0) == r
        face[take, s] = placed(ohf[p, :16], joined(done.at[s]))[:nrow] + jnp.where(here, ag[u, s, 0, own : own + 1], 0.0)
        each_row(
            lambda i: send(
                face.at[take, s], fx.at[take, s, i], fx_send.at[take, s], fx_recv.at[take, s], (1, at_row(i), c)
            )
        )
        fx[take, s, 0] = face[take, s]

    def face_in(p, s, own, action, take):
        await_bytes(fx.at[take, s, pl.ds(0, nrow - 1)], fx_recv.at[take, s])
        moved = action(ct, small, small_out, parts, stood_up(total([fx[take, s, i] for i in range(nrow)])), nrow)
        taken = jnp.concatenate([moved, pltpu.roll(moved, LANES - nrow, 1)], axis=0)
        for t, part in enumerate(tiles(picked(taken, ohf[p]))):
            work[t] = xt[p, s, t] - part
        here = lax.broadcasted_iota(jnp.int32, (nrow, LANES), 0) == r
        mine = jnp.sum(jnp.where(here, laid_down(moved, nrow), 0.0), axis=0, keepdims=True)
        at_own = lax.broadcasted_iota(jnp.int32, (nbf, LANES), 0) == own
        return fields[p, s, 0] - jnp.where(at_own, mine, 0.0)

    def widen(p, s):
        wide[p, s] = placed(ohc[p], joined(done.at[s])).reshape(nrow, nbf, LANES)

    every = range(STREAMS)
    factor = range(nz // LANES)

    @pl.when(d == 0)
    def _():
        for t in factor[0:2]:
            send(mt.at[0, t], mt.at[1, t], late_send.at[2 + t], late_recv.at[2 + t], (1, r, c))
        gather_field(0)
        index0[0, 0:1] = rows[...]
        index0[0, 1:2] = cols[...]
        send(index0.at[0], index0.at[1], early_send.at[0], early_recv.at[0], (1, r, c))
        send(diag, diag0, early_send.at[1], early_recv.at[1], (1, r, c))
        send(fields.at[0, :, 0], fields.at[1, :, 0], late_send.at[1], late_recv.at[1], (1, r, c))
        for s in every:
            if s > 0:
                gather_field(s)
            forward(0, 2, s, xt.at[0, s])
            send(term.at[2, s, 0], rs.at[2, s, 0], rs_send.at[2, s], rs_recv.at[2, s], (1, r, c))
        for t in factor[2:4]:
            send(mt.at[0, t], mt.at[1, t], late_send.at[2 + t], late_recv.at[2 + t], (1, r, c))
        send(xt.at[0], xt.at[1], late_send.at[0], late_recv.at[0], (1, r, c))
        for s in every:
            await_bytes(fin.at[s], fin_recv.at[s])
            out[:, pl.ds(s * LANES, LANES)] = total([fin[s, i] for i in range(nrow)])
        pltpu.make_async_copy(index0.at[0], index0.at[0], early_send.at[0]).wait()
        await_bytes(diag, early_send.at[1])
        await_bytes(xt.at[0], late_send.at[0])
        await_bytes(fields.at[0, :, 0], late_send.at[1])
        for t in factor:
            await_bytes(mt.at[0, t], late_send.at[2 + t])
        for s in every:
            await_bytes(term.at[2, s], rs_send.at[2, s])

    @pl.when(d == 1)
    def _():
        await_bytes(index0.at[1], early_recv.at[0])
        for s in every:
            share_field(s)
        cbuf[pl.ds(r, 1)] = couple[...][None]
        each_row(lambda i: send(couple, cbuf.at[r], c_send, c_recv, (1, at_row(i), c)))
        tables(1, index0[1, 0:1], index0[1, 1:2], nbf - 1)
        await_bytes(diag0, early_recv.at[1])
        turn_diag(1, diag0)
        await_bytes(fields.at[1, :, 0], late_recv.at[1])
        for s in every:
            await_bytes(rs.at[2, s], rs_recv.at[2, s])
            middle(1, 2, s, fields[1, s, 0] + total([rs[2, s, i] for i in range(ncol)]))
        turn_diag(0, diag)
        for s in every:
            gather_field(s)
        await_bytes(cbuf.at[pl.ds(0, nrow - 1)], c_recv)
        turn_couple()
        for t in factor:
            await_bytes(mt.at[1, t], late_recv.at[2 + t])
        for s in every:
            backward(1, 2, s)
            face_out(1, 2, s, nbf - 1, 0)
        held = []
        for s in every:
            held.append(face_in(0, s, 0, couple_on, 0))
            forward(0, 0, s, work)
        for s in every:
            middle(0, 0, s, own_sum(0, s, held[s]))
        for s in every:
            backward(0, 0, s)
            face_out(0, 0, s, 0, 1)
        for s in every:
            widen(0, s)
            each_row(
                lambda i: send(
                    wide.at[0, s, i], fin.at[s, i], fin_send.at[0, s], fin_recv.at[s], (1, at_row(nrow - i), c)
                )
            )
        await_bytes(xt.at[1], late_recv.at[0])
        held = []
        for s in every:
            held.append(face_in(1, s, nbf - 1, couple_back, 1))
            forward(1, 1, s, work)
        for s in every:
            await_bytes(fin.at[s, pl.ds(0, nrow - 1)], fin_recv.at[s])
            out[:, pl.ds(s * LANES, LANES)] = (
                ag[0, s, 0] + wide[0, s, 0] + total([fin[s, i] for i in range(1, nrow)])
            )
        for s in every:
            middle(1, 1, s, own_sum(1, s, held[s]))
        for s in every:
            backward(1, 1, s)
            widen(1, s)
            wide[1, s, 0] += ag[1, s, 0]
            each_row(
                lambda i: send(
                    wide.at[1, s, i], fin.at[s, i], fin_send.at[1, s], fin_recv.at[s], (0, at_row(nrow - i), c)
                )
            )
            send(wide.at[1, s, 0], fin.at[s, 0], fin_send.at[1, s], fin_recv.at[s], (0, r, c))
        await_bytes(cbuf.at[pl.ds(0, nrow - 1)], c_send)
        for s in every:
            await_bytes(wide.at[0, s, pl.ds(0, nrow - 1)], fin_send.at[0, s])
            await_bytes(wide.at[1, s], fin_send.at[1, s])
            for take in range(2):
                await_bytes(fx.at[take, s, pl.ds(0, nrow - 1)], fx_send.at[take, s])
                await_bytes(term.at[take, s, pl.ds(0, ncol - 1)], rs_send.at[take, s])
            for u in range(3):
                await_bytes(ag.at[u, s, pl.ds(0, ncol - 1)], ag_send.at[u, s])

    for s in every:
        await_bytes(fields.at[0, s, pl.ds(0, nrow - 1)], row_send.at[s])


def per_device(nrow, ncol, rhs, factor_blocks, block_rows, block_cols, diag_inverse, coupling):
    nbf = rhs.shape[1]
    nz, size = factor_blocks.shape[-2:]
    vm = pl.BlockSpec(memory_space=pltpu.VMEM)
    dma = pltpu.SemaphoreType.DMA
    got = pl.pallas_call(
        functools.partial(kernel, nrow, ncol),
        out_shape=pltpu.VMEM((nbf, rhs.shape[2]), F32),
        in_specs=[pl.BlockSpec(memory_space=pl.ANY)] * 6,
        out_specs=vm,
        scratch_shapes=[
            pltpu.VMEM((nbf, rhs.shape[2]), F32),
            pltpu.VMEM((1, nz), jnp.int32),
            pltpu.VMEM((1, nz), jnp.int32),
            pltpu.VMEM((nbf, size), F32),
            pltpu.VMEM((size // LANES, LANES), F32),
            pltpu.VMEM((size // LANES, nz, LANES), F32),
            pltpu.VMEM((2, nz // LANES, size, LANES), F32),
            pltpu.VMEM((2, nrow * nbf, nz), BF16),
            pltpu.VMEM((2, ncol * nbf, nz), BF16),
            pltpu.VMEM((2, LANES, nz), BF16),
            pltpu.VMEM((2, 1, size // 2, LANES), F32),
            pltpu.VMEM((1, size // 8, LANES), F32),
            pltpu.VMEM((2, STREAMS, nrow, nbf, LANES), F32),
            pltpu.VMEM((2, STREAMS, nz // LANES, LANES, LANES), F32),
            pltpu.VMEM((nz // LANES, LANES, LANES), F32),
            pltpu.VMEM((STREAMS, nz // LANES, LANES, LANES), F32),
            pltpu.VMEM((1, BLOCK, LANES), F32),
            pltpu.VMEM((1, BLOCK, LANES), F32),
            pltpu.VMEM((2, BLOCK, LANES), F32),
            pltpu.VMEM((3, STREAMS, ncol, nbf, LANES), F32),
            pltpu.VMEM((3, STREAMS, ncol, nbf, LANES), F32),
            pltpu.VMEM((3, STREAMS, ncol, nbf, LANES), F32),
            pltpu.VMEM((2, STREAMS, nrow, LANES), F32),
            pltpu.VMEM((2, STREAMS, nrow, nrow, LANES), F32),
            pltpu.VMEM((2, STREAMS, nrow, nbf, LANES), F32),
            pltpu.VMEM((STREAMS, nrow, nbf, LANES), F32),
            pltpu.VMEM((nrow, size // LANES, LANES), F32),
            pltpu.VMEM((nbf, size), F32),
            pltpu.VMEM((2, 2, nz), jnp.int32),
            dma((size // LANES,)),
            dma((STREAMS,)), dma((STREAMS,)),
            dma((3, STREAMS)), dma((3, STREAMS)),
            dma((3, STREAMS)), dma((3, STREAMS)),
            dma((2, STREAMS)), dma((2, STREAMS)),
            dma((2, STREAMS)), dma((STREAMS,)),
            dma, dma,
            dma((2,)), dma((2,)),
            dma((2 + nz // LANES,)), dma((2 + nz // LANES,)),
            dma((5,)),
        ],
        compiler_params=pltpu.CompilerParams(
            collective_id=0, has_side_effects=True, vmem_limit_bytes=56 * 1024 * 1024
        ),
    )(
        rhs[0],
        factor_blocks.reshape(nz, size),
        block_rows.reshape(1, nz),
        block_cols.reshape(1, nz),
        diag_inverse[0],
        coupling.reshape(size // LANES, LANES),
    )
    return got[None]


def solution(mesh):
    placed_as = (
        P("depth", ("row", "col"), None),
        P("depth", "row", "col", None, None),
        P("depth", "row", "col", None),
        P("depth", "row", "col", None),
        P("depth", ("row", "col"), None),
        P("depth", ("row", "col"), None),
    )
    return jax.shard_map(
        functools.partial(per_device, mesh.shape["row"], mesh.shape["col"]),
        mesh=mesh,
        in_specs=placed_as,
        out_specs=P("depth", ("row", "col"), None),
        check_vma=False,
    )
```

```python
import functools
import math

import jax
import jax.numpy as jnp
from jax import lax
from jax.experimental import pallas as pl
from jax.experimental.pallas import tpu as pltpu
from jax.sharding import PartitionSpec as P

MESH = pl.DeviceIdType.MESH
F32 = jnp.float32
BF16 = jnp.bfloat16

BLOCK = 64
LANES = 128
STREAMS = 2
TURNED = 4


def halves(x):
    hi = x.astype(BF16)
    return hi, (x - hi.astype(F32)).astype(BF16)


def picked(x, table):
    n = x.shape[0]
    both = jnp.dot(jnp.concatenate(halves(x), axis=0), table, preferred_element_type=F32)
    return both[:n] + both[n:]


def placed(table, x):
    n = x.shape[0]
    dims = (((1,), (1,)), ((), ()))
    both = lax.dot_general(table, jnp.concatenate(halves(x), axis=0), dims, preferred_element_type=F32)
    return both[:, :n] + both[:, n:]


def total(terms):
    while len(terms) > 1:
        terms = [terms[i] + terms[i + 1] if i + 1 < len(terms) else terms[i] for i in range(0, len(terms), 2)]
    return terms[0]


def act(mats, vecs, outs, count, parts):
    def tile(t, _):
        x = [[vecs[t, pl.ds(r * BLOCK + 8 * g, 8), :] for g in range(8)] for r in range(count)]

        def group(q, _):
            for a in range(8):
                first = pl.multiple_of(q * (8 * BLOCK) + a * BLOCK, BLOCK)
                m = [mats[t, pl.ds(first + 8 * g, 8), :] for g in range(8)]
                for r in range(count):
                    parts[r, pl.ds(8 * a, 8), :] = total([m[g] * x[r][g] for g in range(8)])
            for r in range(count):
                rows = total([parts[r, pl.ds(i, 8, stride=8), :] for i in range(8)])
                outs[t, pl.ds(pl.multiple_of(r * BLOCK + 8 * q, 8), 8), :] = rows
            return 0

        return lax.fori_loop(0, mats.shape[1] // (8 * BLOCK), group, 0, unroll=4 if mats.shape[1] > 8 * BLOCK else 1)

    lax.fori_loop(0, mats.shape[0], tile, 0)


def act_back(mats, vecs, outs, count):
    def tile(t, _):
        def group(q, sums):
            sums = list(sums)
            v = [vecs[t, pl.ds(pl.multiple_of(r * BLOCK + 8 * q, 8), 8), :] for r in range(count)]
            for a in range(8):
                first = pl.multiple_of(q * (8 * BLOCK) + a * BLOCK, BLOCK)
                z = [jnp.broadcast_to(v[r][a : a + 1], (8, LANES)) for r in range(count)]
                for g in range(8):
                    m = mats[t, pl.ds(first + 8 * g, 8), :]
                    for r in range(count):
                        sums[r * 8 + g] = sums[r * 8 + g] + m * z[r]
            return tuple(sums)

        zero = jnp.zeros((8, LANES), F32)
        sums = lax.fori_loop(0, mats.shape[1] // (8 * BLOCK), group, (zero,) * (8 * count), unroll=4 if mats.shape[1] > 8 * BLOCK else 1)
        for r in range(count):
            for g in range(8):
                outs[t, pl.ds(r * BLOCK + 8 * g, 8), :] = sums[r * 8 + g]
        return 0

    lax.fori_loop(0, mats.shape[0], tile, 0)


def tiles(x):
    return [x[:, LANES * t : LANES * (t + 1)] for t in range(x.shape[1] // LANES)]


def joined(ref):
    return jnp.concatenate([ref[t] for t in range(ref.shape[0])], axis=1)


def stood_up(v):
    n = v.shape[0]
    eighths = [v, pltpu.roll(v, BLOCK, 1)] * 8
    if 16 * n < LANES:
        eighths.append(jnp.zeros((LANES - 16 * n, LANES), F32))
    return jnp.concatenate(eighths, axis=0).T[:BLOCK]


def couple_on(ct, small, small_out, parts, x, n):
    small[0] = x
    act(ct, small, small_out, 1, parts)
    o = small_out[0, :8]
    return jnp.concatenate([o] + [pltpu.roll(o, LANES - 2 * n * i, 1) for i in range(1, 8)], axis=0)


def couple_back(ct, small, small_out, parts, z, n):
    eighth = lax.broadcasted_iota(jnp.int32, (8, LANES), 1) // (2 * n)
    small[0, :8] = total([jnp.where(eighth == i, z[8 * i : 8 * i + 8], 0.0) for i in range(8)])
    act_back(ct, small, small_out, 1)
    o = small_out[0]
    for i in (4, 2, 1):
        o = o + pltpu.roll(o, LANES - 2 * n * i, 1)
    return o


def laid_down(v, n):
    flat = jnp.concatenate([v, v], axis=0).T
    lane = lax.broadcasted_iota(jnp.int32, (n, LANES), 1)
    return jnp.where(lane < BLOCK, flat[:n], flat[n : 2 * n])


def stood_up_twice(v):
    pair = [v, pltpu.roll(v, BLOCK, 1)]
    return jnp.concatenate(pair + pair, axis=0).T[:BLOCK]


def laid_down_halves(v, n):
    flat = jnp.concatenate([v] * 4, axis=0).T
    quarter = lax.broadcasted_iota(jnp.int32, (n, LANES), 1) // (BLOCK // 2)
    low = jnp.where(quarter == 0, flat[:n], flat[2 * n : 3 * n])
    high = jnp.where(quarter == 2, flat[n : 2 * n], flat[3 * n :])
    return jnp.where(quarter < 2, low, high)


def kernel(
    nrow, ncol, rhs_in, mats, rows_in, cols_in, diag_in, couple_in, out,
    rhs, rows, cols, diag, couple, raw, mt, ohc, ohr, ohf, dt, ct, fields, xt, work, done, small, small_out, parts, term, rs, ag, face, fx, wide, fin, cbuf, diag0,
    index0, raw_sem, row_send, row_recv, rs_send, rs_recv, ag_send, ag_recv, fx_send, fx_recv, fin_send, fin_recv, c_send,
    c_recv, early_send, early_recv, late_send, late_recv, in_sem,
):
    nbf = rhs.shape[0]
    nz = rows.shape[1]
    side = math.isqrt(ncol)
    d, r, c = lax.axis_index("depth"), lax.axis_index("row"), lax.axis_index("col")
    cy, cx = lax.div(c, side), lax.rem(c, side)

    def at_row(i):
        return lax.rem(r + i, nrow)

    def at_col(i):
        return lax.rem(cy + i // side, side) * side + lax.rem(cx + i % side, side)

    def back_col(i):
        return lax.rem(cy - i // side + side, side) * side + lax.rem(cx - i % side + side, side)

    rows_away = sorted(range(1, nrow), key=lambda i: -min(i, nrow - i))
    cols_away = sorted(
        range(1, ncol), key=lambda i: -min(i // side, side - i // side) - min(i % side, side - i % side)
    )

    near = ncol // 2

    def send(src, dst, send_sem, recv_sem, where):
        pltpu.make_async_remote_copy(
            src_ref=src, dst_ref=dst, send_sem=send_sem, recv_sem=recv_sem, device_id=where, device_id_type=MESH
        ).start()

    def await_bytes(ref, sem):
        pltpu.make_async_copy(ref, ref, sem).wait()

    def each(low, high, body):
        def step(i, _):
            body(i)
            return 0

        lax.fori_loop(low, high, step, 0)

    def each_col(body):
        for i in cols_away:
            body(i)

    def each_row(body):
        for i in rows_away:
            body(i)

    barrier = pltpu.get_barrier_semaphore()

    def greet(where):
        pl.semaphore_signal(barrier, inc=1, device_id=where, device_id_type=MESH)

    each_row(lambda i: greet((d, at_row(i), c)))
    each_row(lambda i: greet((1 - d, at_row(i), c)))
    each_col(lambda i: greet((1 - d, r, at_col(i))))
    greet((1 - d, r, c))

    @pl.when(d == 1)
    def _():
        each_col(lambda i: greet((1, r, at_col(i))))


    pieces = raw.shape[0]

    def piece(j):
        lanes = pl.ds(pl.multiple_of(j * LANES, LANES), LANES)
        return pltpu.make_async_copy(mats.at[:, lanes], raw.at[j], raw_sem.at[j])

    inputs = [
        pltpu.make_async_copy(src, dst, in_sem.at[i])
        for i, (src, dst) in enumerate(
            ((rhs_in, rhs), (rows_in, rows), (cols_in, cols), (couple_in, couple), (diag_in, diag))
        )
    ]
    for copy in inputs:
        copy.start()
    each(0, pieces, lambda j: piece(j).start())
    for copy in inputs:
        copy.wait()
    pl.semaphore_wait(barrier, 2 * (nrow - 1) + ncol + (ncol - 1) * d)

    def share_field(s):
        part = pl.ds(s * LANES, LANES)
        fields[0, s, 0] = rhs[:, part]
        each_row(lambda i: send(rhs.at[:, part], fields.at[0, s, i], row_send.at[s], row_recv.at[s], (d, at_row(i), c)))

    @pl.when(d == 0)
    def _():
        for s in range(STREAMS):
            share_field(s)

    def tables(use, brow, bcol, own_face):
        oy, ox = (brow >> 5) // side, (brow >> 5) % side
        slot_row = ((cy - oy) & (side - 1)) * side + ((cx - ox) & (side - 1))
        slot_col = (r - (bcol >> 5)) & (nrow - 1)

        def table(position, count):
            return (lax.broadcasted_iota(jnp.int32, (count, nz), 0) == position).astype(BF16)

        ohr[use] = table((slot_row << 5) | (brow & 31), ncol * nbf)
        ohc[use] = table((slot_col << 5) | (bcol & 31), nrow * nbf)
        ohf[use] = table(jnp.where((bcol & 31) == own_face, bcol >> 5, -1), LANES)

    tables(0, rows[...], cols[...], jnp.where(d == 0, nbf - 1, 0))

    def turn(i):
        group = [i * TURNED + u for u in range(TURNED)]
        for j in group:
            piece(j).wait()
        for j in group:
            for t in range(nz // LANES):
                mt[0, t, pl.ds(pl.multiple_of(j * LANES, LANES), LANES), :] = raw[j, pl.ds(t * LANES, LANES), :].T

    each(0, pieces // TURNED, turn)

    def fill(ref, x):
        for t, part in enumerate(tiles(x)):
            ref[t] = part

    def gather_field(s):
        await_bytes(fields.at[0, s, pl.ds(0, nrow - 1)], row_recv.at[s])
        fill(xt.at[0, s], picked(fields[0, s].reshape(nrow * nbf, LANES).T, ohc[0]))

    def turn_diag(use, given):
        apart = given.shape[1] // (2 * LANES)

        def some(i):
            for u in range(TURNED):
                j = i * TURNED + u
                low, high = (given[:, pl.ds(pl.multiple_of(k * LANES, LANES), LANES)] for k in (j, j + apart))
                full = jnp.concatenate([low, low, high, high], axis=0)
                dt[use, 0, pl.ds(pl.multiple_of(j * LANES, LANES), LANES), :] = full.T

        each(0, apart // TURNED, some)

    def turn_couple():
        apart = ct.shape[1] // LANES
        for j in range(apart):
            lots = []
            for i in range(8):
                two = cbuf[:, pl.ds(i * apart + j, 1), :].reshape(nrow, LANES)
                lots += [two, two]
            if 16 * nrow < LANES:
                lots.append(jnp.zeros((LANES - 16 * nrow, LANES), F32))
            ct[0, pl.ds(j * LANES, LANES), :] = jnp.concatenate(lots, axis=0).T

    def forward(p, u, s, vecs):
        act(mt.at[p], vecs, done.at[s], 2, parts)
        both = joined(done.at[s])
        for first in (near, 0):
            part = placed(ohr[p, first * nbf : (first + near) * nbf], both)
            term[u, s, first : first + near] = part.reshape(near, nbf, LANES)
            for i in cols_away:
                if first <= i < first + near:
                    send(term.at[u, s, i], rs.at[u, s, i], rs_send.at[u, s], rs_recv.at[u, s], (1, r, back_col(i)))

    def middle(p, u, s, summed):
        small[0] = stood_up_twice(summed)
        act(dt.at[p], small, small_out, 1, parts)
        ag[u, s, 0] = laid_down_halves(small_out[0, : BLOCK // 2], nbf)
        each_col(
            lambda i: send(ag.at[u, s, 0], ag.at[u, s, i], ag_send.at[u, s], ag_recv.at[u, s], (1, r, at_col(i)))
        )

    def own_sum(u, s, field):
        await_bytes(rs.at[u, s, pl.ds(0, ncol - 1)], rs_recv.at[u, s])
        return field + term[u, s, 0] + total([rs[u, s, i] for i in range(1, ncol)])

    def backward(p, u, s):
        await_bytes(ag.at[u, s, pl.ds(0, ncol - 1)], ag_recv.at[u, s])
        fill(work, picked(ag[u, s].reshape(ncol * nbf, LANES).T, ohr[p]))
        act_back(mt.at[p], work, done.at[s], 2)

    def face_out(p, u, s, own, take):
        here = lax.broadcasted_iota(jnp.int32, (nrow, LANES), 0) == r
        face[take, s] = placed(ohf[p, :16], joined(done.at[s]))[:nrow] + jnp.where(here, ag[u, s, 0, own : own + 1], 0.0)
        each_row(
            lambda i: send(
                face.at[take, s], fx.at[take, s, i], fx_send.at[take, s], fx_recv.at[take, s], (1, at_row(i), c)
            )
        )
        fx[take, s, 0] = face[take, s]

    def face_in(p, s, own, action, take):
        await_bytes(fx.at[take, s, pl.ds(0, nrow - 1)], fx_recv.at[take, s])
        moved = action(ct, small, small_out, parts, stood_up(total([fx[take, s, i] for i in range(nrow)])), nrow)
        taken = jnp.concatenate([moved, pltpu.roll(moved, LANES - nrow, 1)], axis=0)
        for t, part in enumerate(tiles(picked(taken, ohf[p]))):
            work[t] = xt[p, s, t] - part
        here = lax.broadcasted_iota(jnp.int32, (nrow, LANES), 0) == r
        mine = jnp.sum(jnp.where(here, laid_down(moved, nrow), 0.0), axis=0, keepdims=True)
        at_own = lax.broadcasted_iota(jnp.int32, (nbf, LANES), 0) == own
        return fields[p, s, 0] - jnp.where(at_own, mine, 0.0)

    def widen(p, s):
        wide[p, s] = placed(ohc[p], joined(done.at[s])).reshape(nrow, nbf, LANES)

    every = range(STREAMS)
    factor = range(nz // LANES)

    @pl.when(d == 0)
    def _():
        for t in factor[0:2]:
            send(mt.at[0, t], mt.at[1, t], late_send.at[2 + t], late_recv.at[2 + t], (1, r, c))
        gather_field(0)
        index0[0, 0:1] = rows[...]
        index0[0, 1:2] = cols[...]
        send(index0.at[0], index0.at[1], early_send.at[0], early_recv.at[0], (1, r, c))
        send(diag, diag0, early_send.at[1], early_recv.at[1], (1, r, c))
        send(fields.at[0, :, 0], fields.at[1, :, 0], late_send.at[1], late_recv.at[1], (1, r, c))
        for s in every:
            if s > 0:
                gather_field(s)
            forward(0, 2, s, xt.at[0, s])
            send(term.at[2, s, 0], rs.at[2, s, 0], rs_send.at[2, s], rs_recv.at[2, s], (1, r, c))
        for t in factor[2:4]:
            send(mt.at[0, t], mt.at[1, t], late_send.at[2 + t], late_recv.at[2 + t], (1, r, c))
        send(xt.at[0], xt.at[1], late_send.at[0], late_recv.at[0], (1, r, c))
        for s in every:
            await_bytes(fin.at[s], fin_recv.at[s])
            out[:, pl.ds(s * LANES, LANES)] = total([fin[s, i] for i in range(nrow)])
        pltpu.make_async_copy(index0.at[0], index0.at[0], early_send.at[0]).wait()
        await_bytes(diag, early_send.at[1])
        await_bytes(xt.at[0], late_send.at[0])
        await_bytes(fields.at[0, :, 0], late_send.at[1])
        for t in factor:
            await_bytes(mt.at[0, t], late_send.at[2 + t])
        for s in every:
            await_bytes(term.at[2, s], rs_send.at[2, s])

    @pl.when(d == 1)
    def _():
        await_bytes(index0.at[1], early_recv.at[0])
        for s in every:
            share_field(s)
        cbuf[pl.ds(r, 1)] = couple[...][None]
        each_row(lambda i: send(couple, cbuf.at[r], c_send, c_recv, (1, at_row(i), c)))
        tables(1, index0[1, 0:1], index0[1, 1:2], nbf - 1)
        await_bytes(diag0, early_recv.at[1])
        turn_diag(1, diag0)
        await_bytes(fields.at[1, :, 0], late_recv.at[1])
        for s in every:
            await_bytes(rs.at[2, s], rs_recv.at[2, s])
            middle(1, 2, s, fields[1, s, 0] + total([rs[2, s, i] for i in range(ncol)]))
        turn_diag(0, diag)
        for s in every:
            gather_field(s)
        await_bytes(cbuf.at[pl.ds(0, nrow - 1)], c_recv)
        turn_couple()
        for t in factor:
            await_bytes(mt.at[1, t], late_recv.at[2 + t])
        for s in every:
            backward(1, 2, s)
            face_out(1, 2, s, nbf - 1, 0)
        held = []
        for s in every:
            held.append(face_in(0, s, 0, couple_on, 0))
            forward(0, 0, s, work)
        for s in every:
            middle(0, 0, s, own_sum(0, s, held[s]))
        for s in every:
            backward(0, 0, s)
            face_out(0, 0, s, 0, 1)
        for s in every:
            widen(0, s)
            each_row(
                lambda i: send(
                    wide.at[0, s, i], fin.at[s, i], fin_send.at[0, s], fin_recv.at[s], (1, at_row(nrow - i), c)
                )
            )
        await_bytes(xt.at[1], late_recv.at[0])
        held = []
        for s in every:
            held.append(face_in(1, s, nbf - 1, couple_back, 1))
            forward(1, 1, s, work)
        for s in every:
            await_bytes(fin.at[s, pl.ds(0, nrow - 1)], fin_recv.at[s])
            out[:, pl.ds(s * LANES, LANES)] = (
                ag[0, s, 0] + wide[0, s, 0] + total([fin[s, i] for i in range(1, nrow)])
            )
        for s in every:
            middle(1, 1, s, own_sum(1, s, held[s]))
        for s in every:
            backward(1, 1, s)
            widen(1, s)
            wide[1, s, 0] += ag[1, s, 0]
            each_row(
                lambda i: send(
                    wide.at[1, s, i], fin.at[s, i], fin_send.at[1, s], fin_recv.at[s], (0, at_row(nrow - i), c)
                )
            )
            send(wide.at[1, s, 0], fin.at[s, 0], fin_send.at[1, s], fin_recv.at[s], (0, r, c))
        await_bytes(cbuf.at[pl.ds(0, nrow - 1)], c_send)
        for s in every:
            await_bytes(wide.at[0, s, pl.ds(0, nrow - 1)], fin_send.at[0, s])
            await_bytes(wide.at[1, s], fin_send.at[1, s])
            for take in range(2):
                await_bytes(fx.at[take, s, pl.ds(0, nrow - 1)], fx_send.at[take, s])
                await_bytes(term.at[take, s, pl.ds(0, ncol - 1)], rs_send.at[take, s])
            for u in range(3):
                await_bytes(ag.at[u, s, pl.ds(0, ncol - 1)], ag_send.at[u, s])

    for s in every:
        await_bytes(fields.at[0, s, pl.ds(0, nrow - 1)], row_send.at[s])


def per_device(nrow, ncol, rhs, factor_blocks, block_rows, block_cols, diag_inverse, coupling):
    nbf = rhs.shape[1]
    nz, size = factor_blocks.shape[-2:]
    vm = pl.BlockSpec(memory_space=pltpu.VMEM)
    dma = pltpu.SemaphoreType.DMA
    got = pl.pallas_call(
        functools.partial(kernel, nrow, ncol),
        out_shape=pltpu.VMEM((nbf, rhs.shape[2]), F32),
        in_specs=[pl.BlockSpec(memory_space=pl.ANY)] * 6,
        out_specs=vm,
        scratch_shapes=[
            pltpu.VMEM((nbf, rhs.shape[2]), F32),
            pltpu.VMEM((1, nz), jnp.int32),
            pltpu.VMEM((1, nz), jnp.int32),
            pltpu.VMEM((nbf, size), F32),
            pltpu.VMEM((size // LANES, LANES), F32),
            pltpu.VMEM((size // LANES, nz, LANES), F32),
            pltpu.VMEM((2, nz // LANES, size, LANES), F32),
            pltpu.VMEM((2, nrow * nbf, nz), BF16),
            pltpu.VMEM((2, ncol * nbf, nz), BF16),
            pltpu.VMEM((2, LANES, nz), BF16),
            pltpu.VMEM((2, 1, size // 2, LANES), F32),
            pltpu.VMEM((1, size // 8, LANES), F32),
            pltpu.VMEM((2, STREAMS, nrow, nbf, LANES), F32),
            pltpu.VMEM((2, STREAMS, nz // LANES, LANES, LANES), F32),
            pltpu.VMEM((nz // LANES, LANES, LANES), F32),
            pltpu.VMEM((STREAMS, nz // LANES, LANES, LANES), F32),
            pltpu.VMEM((1, BLOCK, LANES), F32),
            pltpu.VMEM((1, BLOCK, LANES), F32),
            pltpu.VMEM((2, BLOCK, LANES), F32),
            pltpu.VMEM((3, STREAMS, ncol, nbf, LANES), F32),
            pltpu.VMEM((3, STREAMS, ncol, nbf, LANES), F32),
            pltpu.VMEM((3, STREAMS, ncol, nbf, LANES), F32),
            pltpu.VMEM((2, STREAMS, nrow, LANES), F32),
            pltpu.VMEM((2, STREAMS, nrow, nrow, LANES), F32),
            pltpu.VMEM((2, STREAMS, nrow, nbf, LANES), F32),
            pltpu.VMEM((STREAMS, nrow, nbf, LANES), F32),
            pltpu.VMEM((nrow, size // LANES, LANES), F32),
            pltpu.VMEM((nbf, size), F32),
            pltpu.VMEM((2, 2, nz), jnp.int32),
            dma((size // LANES,)),
            dma((STREAMS,)), dma((STREAMS,)),
            dma((3, STREAMS)), dma((3, STREAMS)),
            dma((3, STREAMS)), dma((3, STREAMS)),
            dma((2, STREAMS)), dma((2, STREAMS)),
            dma((2, STREAMS)), dma((STREAMS,)),
            dma, dma,
            dma((2,)), dma((2,)),
            dma((2 + nz // LANES,)), dma((2 + nz // LANES,)),
            dma((5,)),
        ],
        compiler_params=pltpu.CompilerParams(
            collective_id=0, has_side_effects=True, vmem_limit_bytes=56 * 1024 * 1024
        ),
    )(
        rhs[0],
        factor_blocks.reshape(nz, size),
        block_rows.reshape(1, nz),
        block_cols.reshape(1, nz),
        diag_inverse[0],
        coupling.reshape(size // LANES, LANES),
    )
    return got[None]


def solution(mesh):
    placed_as = (
        P("depth", ("row", "col"), None),
        P("depth", "row", "col", None, None),
        P("depth", "row", "col", None),
        P("depth", "row", "col", None),
        P("depth", ("row", "col"), None),
        P("depth", ("row", "col"), None),
    )
    return jax.shard_map(
        functools.partial(per_device, mesh.shape["row"], mesh.shape["col"]),
        mesh=mesh,
        in_specs=placed_as,
        out_specs=P("depth", ("row", "col"), None),
        check_vma=False,
    )
```
